256 devices in a mesh: pb: 16 (over z, y_lo), ka: 16 (over y_hi, x, core).
Axes of the slice: x: 4, y: 4 (y_hi: 2, y_lo: 2; y = y_hi * 2 + y_lo), z: 8, core: 2. Of those that a mesh axis runs over, the one named last changes fastest.
Arguments:
- queries: bfloat16 [32768, 512], P('pb'), may hold values from -8 to 8
- point_order: int32 [16, 2048], P('pb'), may hold values from 0 to 2047, each once within a row
- keys: bfloat16 [32, 128, 512], P('ka'), may hold values from -4 to 4
- values: bfloat16 [32, 128, 512], P('ka'), may hold values from -6 to 6
- pair_counts: int32 [16, 16], P('pb'), may hold values from 1 to 31, as said below
- pair_keys: int32 [16, 256], P('pb'), may hold values from 0 to 31, as said below
- out_grad: bfloat16 [256, 128, 512], P('pb'), may hold values from -6 to 6
Outputs:
- attended: bfloat16 [256, 128, 512], P(('pb', 'ka'))
- query_grad: float32 [256, 128, 512], P(('pb', 'ka'))
- key_grad: float32 [32, 128, 512], P('ka', 'pb')
- value_grad: float32 [32, 128, 512], P('ka', 'pb')
The draws below stay inside these ranges and needn't reach their ends.
Inputs may be any that keep to these rules, and one draw needn't show every extreme that they name: `pair_counts`: every query block has between 1 and 31 pairs, some query block of every slab exactly 31; the counts of a slab add up to 256. `pair_keys`: the key blocks of one query block are distinct and ascending.
All inputs are finite; a program needn't handle non-finite values.
Results may differ from the reference program's by a relative error of at most 0.02.
Values may be sent and summed in bfloat16 or wider, within the bound.
A program may use at most 192 MiB of HBM per device.

```python
import jax
import jax.numpy as jnp
from jax import lax

H = 8
HD = 64
D = 512
BS = 128
QB_DEV = 16
NSLAB = 16
QB = 256
KB = 32
PAIRS_Q = 16
MOST = 31


def pair_tables(key):
    key = jax.random.fold_in(key, 101)
    split_keys = jax.random.split(key, 4)
    half_count = QB_DEV // 2
    shifts = jax.random.randint(split_keys[0], (NSLAB, half_count), -(PAIRS_Q - 1), PAIRS_Q)
    chosen_pair = jax.random.randint(split_keys[1], (NSLAB, 1), 0, half_count)
    shifts = jnp.where(jnp.arange(half_count)[None, :] == chosen_pair, PAIRS_Q - 1, shifts)
    paired = jnp.stack([PAIRS_Q + shifts, PAIRS_Q - shifts], axis=2).reshape(NSLAB, QB_DEV)

    def shuffled(row_key):
        return jax.random.permutation(row_key, QB_DEV)
    orders = jax.vmap(shuffled)(jax.random.split(split_keys[2], NSLAB))
    counts = jnp.take_along_axis(paired, orders, axis=1)
    block_index = jnp.arange(NSLAB * QB_DEV, dtype=jnp.int32).reshape(NSLAB, QB_DEV)
    centers = block_index * KB // (NSLAB * QB_DEV)
    candidates = jnp.arange(KB, dtype=jnp.int32)
    apart = jnp.abs(candidates[None, None, :] - centers[..., None])
    apart = jnp.minimum(apart, KB - apart)
    jitter = jax.random.randint(split_keys[3], (NSLAB, QB_DEV, KB), 0, 4)
    ranking = (apart * 4 + jitter) * KB + candidates[None, None, :]
    _, nearest = lax.top_k(-ranking, MOST)
    picked = jnp.where(jnp.arange(MOST)[None, None, :] < counts[..., None], nearest, KB)
    picked = jnp.sort(picked, axis=2)
    ends = jnp.cumsum(counts, axis=1)
    starts = ends - counts
    slots = jnp.arange(QB_DEV * PAIRS_Q, dtype=jnp.int32)
    owners = jnp.sum((slots[None, :, None] >= ends[:, None, :]).astype(jnp.int32), axis=2)
    within = slots[None, :] - jnp.take_along_axis(starts, owners, axis=1)
    flat_index = owners * MOST + within
    listing = jnp.take_along_axis(picked.reshape(NSLAB, QB_DEV * MOST), flat_index, axis=1)
    return (counts.astype(jnp.int32), listing.astype(jnp.int32))


def draw_pair_counts(key, part):
    return pair_tables(key)[0]


def draw_pair_keys(key, part):
    return pair_tables(key)[1]


def draw_queries(key, part):
    key = jax.random.fold_in(key, 11)
    point_total = QB * BS
    base = jnp.clip(jax.random.normal(key, (point_total, D), jnp.float32), -8.0, 8.0)
    return base.astype(jnp.bfloat16)


def draw_keys(key, part):
    key = jax.random.fold_in(key, 23)
    base = jnp.clip(jax.random.normal(key, (KB, BS, D), jnp.float32), -4.0, 4.0)
    return base.astype(jnp.bfloat16)


def shard_levels(rng, shape, cuts, smallest, high):
    level, own = 1.0, jax.random.fold_in(rng, 6)
    for position, shards_of in cuts:
        steps = jnp.exp(jax.random.uniform(jax.random.fold_in(own, position), (shards_of,), jnp.float32, smallest / len(cuts), high / len(cuts)))
        level = level * jnp.repeat(steps, shape[position] // shards_of).reshape([-1 if axis == position else 1 for axis in range(len(shape))])
    return level


def noise(rng, shape, width, limit, cuts=(), kind=jnp.bfloat16):
    entries = jax.random.normal(rng, shape, jnp.float32) * width
    if len(cuts) > 0:
        entries = shard_levels(rng, shape, cuts, -0.22, 0.18) * entries
    return jnp.clip(entries, min=-limit, max=limit).astype(kind)


def setup_inputs(seed: int = 0) -> dict:
    seeds = jax.random.split(jax.random.key(seed), 8)
    return {
        "queries": draw_queries(jax.random.fold_in(seeds[7], 71), 0),
        "point_order": jax.vmap(lambda own: jax.random.permutation(own, QB_DEV * BS))(jax.random.split(seeds[1], NSLAB)).reshape((NSLAB, QB_DEV * BS)).astype(jnp.int32),
        "keys": draw_keys(jax.random.fold_in(seeds[7], 71), 0),
        "values": noise(seeds[3], (KB, BS, D), 1.0, 6.0, ((0, 16),)),
        "pair_counts": draw_pair_counts(jax.random.fold_in(seeds[7], 71), 0),
        "pair_keys": draw_pair_keys(jax.random.fold_in(seeds[7], 71), 0),
        "out_grad": noise(seeds[6], (QB, BS, D), 1.0, 6.0, ((0, 16),)),
    }


GROUP = 16
FLOOR = -1.0e30


def head_view(tiles):
    return tiles.astype(jnp.float32).reshape(tiles.shape[0], tiles.shape[1], H, HD)


def reference(queries, point_order, keys, values, pair_counts, pair_keys, out_grad):
    slab_points = QB_DEV * BS
    offsets = (jnp.arange(NSLAB, dtype=jnp.int32) * slab_points)[:, None]
    serial = jnp.take(queries, (point_order + offsets).reshape(-1), axis=0).reshape(QB, BS, D)
    ends = jnp.cumsum(pair_counts, axis=1)
    slots = jnp.arange(QB_DEV * PAIRS_Q, dtype=jnp.int32)
    local_ids = jnp.sum((slots[None, :, None] >= ends[:, None, :]).astype(jnp.int32), axis=2)
    query_ids = (local_ids + jnp.arange(NSLAB, dtype=jnp.int32)[:, None] * QB_DEV).reshape(-1, GROUP)
    key_ids = pair_keys.reshape(-1, GROUP)
    scale = HD ** -0.5

    def scores_of(qids, kids):
        return jnp.einsum("gqhd,gkhd->ghqk", head_view(serial[qids]), head_view(keys[kids])) * scale

    def max_step(running, ids):
        qids, kids = ids
        return running.at[qids].max(jnp.max(scores_of(qids, kids), axis=3)), None

    maxima, _ = lax.scan(max_step, jnp.full((QB, H, BS), FLOOR, jnp.float32), (query_ids, key_ids))

    def sum_step(running, ids):
        totals, weighted = running
        qids, kids = ids
        probs = jnp.exp(scores_of(qids, kids) - maxima[qids][..., None])
        rounded = probs.astype(jnp.bfloat16).astype(jnp.float32)
        mixed = jnp.einsum("ghqk,gkhd->gqhd", rounded, head_view(values[kids]))
        totals = totals.at[qids].add(jnp.sum(probs, axis=3))
        weighted = weighted.at[qids].add(mixed.reshape(GROUP, BS, D))
        return (totals, weighted), None

    start = (jnp.zeros((QB, H, BS), jnp.float32), jnp.zeros((QB, BS, D), jnp.float32))
    (totals, weighted), _ = lax.scan(sum_step, start, (query_ids, key_ids))
    attended = (weighted.reshape(QB, BS, H, HD) / jnp.transpose(totals, (0, 2, 1))[..., None]).reshape(QB, BS, D).astype(jnp.bfloat16)
    log_sum = maxima + jnp.log(totals)
    product = (out_grad.astype(jnp.float32) * attended.astype(jnp.float32)).reshape(QB, BS, H, HD)
    delta = jnp.transpose(jnp.sum(product, axis=3), (0, 2, 1))

    def grad_step(running, ids):
        query_grad, key_grad, value_grad = running
        qids, kids = ids
        query_heads = head_view(serial[qids])
        key_heads = head_view(keys[kids])
        grad_heads = head_view(out_grad[qids])
        value_heads = head_view(values[kids])
        scores = jnp.einsum("gqhd,gkhd->ghqk", query_heads, key_heads) * scale
        probs = jnp.exp(scores - log_sum[qids][..., None])
        rounded = probs.astype(jnp.bfloat16).astype(jnp.float32)
        value_part = jnp.einsum("ghqk,gqhd->gkhd", rounded, grad_heads)
        prob_grad = jnp.einsum("gqhd,gkhd->ghqk", grad_heads, value_heads)
        score_grad = probs * (prob_grad - delta[qids][..., None]) * scale
        query_part = jnp.einsum("ghqk,gkhd->gqhd", score_grad, key_heads, precision=lax.Precision.HIGHEST)
        key_part = jnp.einsum("ghqk,gqhd->gkhd", score_grad, query_heads, precision=lax.Precision.HIGHEST)
        query_grad = query_grad.at[qids].add(query_part.reshape(GROUP, BS, D))
        key_grad = key_grad.at[kids].add(key_part.reshape(GROUP, BS, D))
        value_grad = value_grad.at[kids].add(value_part.reshape(GROUP, BS, D))
        return (query_grad, key_grad, value_grad), None

    start = (jnp.zeros((QB, BS, D), jnp.float32), jnp.zeros((KB, BS, D), jnp.float32), jnp.zeros((KB, BS, D), jnp.float32))
    (query_grad, key_grad, value_grad), _ = lax.scan(grad_step, start, (query_ids, key_ids))
    return attended, query_grad, key_grad, value_grad
```

```python
import functools
import math

import jax
import jax.numpy as jnp
from jax import lax
from jax.experimental import pallas as pl
from jax.experimental.pallas import tpu as pltpu
from jax.sharding import PartitionSpec as P

H = 8
HD = 64
D = 512
BS = 128
NP = 16
NX = 4
NY = 2
NM = NX * NY
NC = 4
QS = NM * BS
KS = 4 * BS
PQ = 2 * BS
SCALE = HD ** -0.5
C2 = SCALE * math.log2(math.e)
FAR = 1e30
MESH = pl.DeviceIdType.MESH
BF = jnp.bfloat16
F32 = jnp.float32

NN = (((1,), (0,)), ((), ()))
NT = (((1,), (1,)), ((), ()))


def dot(a, b, dims=NN):
    return lax.dot_general(a, b, dims, preferred_element_type=F32)


def kernel(
    queries,
    order,
    keys,
    values,
    counts,
    listing,
    out_grad,
    att_out,
    qg_out,
    kg_out,
    vg_out,
    qbuf,
    serial,
    og,
    kv,
    use,
    q_t,
    og_t,
    wq_t,
    wog_t,
    probs,
    dps,
    a_keep,
    m_keep,
    d_keep,
    stat_own,
    stat_got,
    aq,
    x1_got,
    x2_got,
    y_keep,
    y_send,
    y_got,
    c_keep,
    c_send,
    c_got,
    z_send,
    z_got,
    load_sem,
    kv_sem,
    stat_sem,
    x1_sem,
    x2_sem,
    y_sem,
    c_sem,
    z_sem,
):
    pb = lax.axis_index("pb")
    ka = lax.axis_index("ka")
    core = lax.rem(ka, 2)
    chip = ka // 2
    xi = lax.rem(chip, NX)
    yi = chip // NX
    xr = lax.rem(xi + 1, NX)
    xl = lax.rem(xi + NX - 1, NX)
    xo = lax.rem(xi + 2, NX)
    yo = 1 - yi

    def at_ka(y, x, c):
        return {"ka": (y * NX + x) * 2 + c}

    right, left = at_ka(yi, xr, core), at_ka(yi, xl, core)
    across = at_ka(yo, xi, core)
    mate = {"ka": chip * 2 + (1 - core)}

    def peer(d):
        return {"ka": lax.rem(chip + d, NM) * 2 + core}

    def slab(d):
        return {"pb": lax.rem(pb + d, NP)}

    def send(src, dst, send_sem, recv_sem, device):
        return pltpu.make_async_remote_copy(
            src_ref=src, dst_ref=dst, send_sem=send_sem, recv_sem=recv_sem,
            device_id=device, device_id_type=MESH,
        )

    barrier = pltpu.get_barrier_semaphore()
    pl.semaphore_signal(barrier, inc=1, device_id=mate, device_id_type=MESH)

    def hello_ka(d, _):
        pl.semaphore_signal(barrier, inc=1, device_id=peer(d), device_id_type=MESH)
        return 0

    def hello_pb(d, _):
        pl.semaphore_signal(barrier, inc=1, device_id=slab(d), device_id_type=MESH)
        return 0

    lax.fori_loop(1, NM, hello_ka, 0)
    lax.fori_loop(1, NP, hello_pb, 0)

    load_q = pltpu.make_async_copy(queries, qbuf, load_sem.at[0])
    load_q.start()
    own2 = pl.ds(2 * core, 2)
    load_k = pltpu.make_async_copy(keys, kv.at[0, own2], load_sem.at[1])
    load_v = pltpu.make_async_copy(values, kv.at[1, own2], load_sem.at[2])
    load_k.start()
    load_v.start()
    load_og = []
    for b in range(NM):
        cp = pltpu.make_async_copy(out_grad.at[2 * b + core], og.at[b], load_sem.at[3 + b])
        cp.start()
        load_og.append(cp)

    cb = jnp.broadcast_to(counts[...].astype(F32), (16, 16))
    i0 = lax.broadcasted_iota(jnp.int32, (16, 16), 0)
    i1 = lax.broadcasted_iota(jnp.int32, (16, 16), 1)
    starts = jnp.sum(jnp.where(i1 < i0, cb, 0.0), axis=1, keepdims=True)
    sizes = jnp.sum(jnp.where(i1 == i0, cb, 0.0), axis=1, keepdims=True)
    slot = lax.broadcasted_iota(jnp.int32, (16, 256), 1).astype(F32)
    inside = jnp.where((slot >= starts) & (slot < starts + sizes), 1.0, 0.0)
    row = lax.broadcasted_iota(jnp.int32, (8, 256), 0) + 4 * chip
    named = jnp.where(jnp.broadcast_to(listing[...], (8, 256)) == row, 1.0, 0.0)
    joined = dot(named.astype(BF), inside.astype(BF), NT)
    e0 = lax.broadcasted_iota(jnp.int32, (16, QS), 0)
    e1 = lax.broadcasted_iota(jnp.int32, (16, QS), 1)
    spread = jnp.where(e0 == 2 * (e1 // BS) + core, 1.0, 0.0)
    use[...] = dot(joined.astype(BF), spread.astype(BF))

    zero_half = jnp.zeros((HD, QS), BF)
    for arr in (wq_t, wog_t):
        arr[HD:, :QS] = zero_half
        arr[:HD, QS:] = zero_half

    load_q.wait()

    def gather(b, _):
        at = pl.multiple_of((2 * b + core) * BS, BS)
        line = order[:, pl.ds(at, BS)]
        column = jnp.broadcast_to(line, (BS, BS)).T
        lanes = lax.broadcasted_iota(jnp.int32, (BS, BS), 1)
        picks = [
            jnp.where(column == lanes + n * BS, 1.0, 0.0).astype(BF) for n in range(16)
        ]
        pick = jnp.concatenate(picks, axis=1)
        serial[pl.ds(pl.multiple_of(b * BS, BS), BS), :] = dot(pick, qbuf[...]).astype(BF)
        return 0

    lax.fori_loop(0, 2, gather, 0)
    pl.semaphore_wait(barrier, 1 + (NM - 1) + (NP - 1))
    send_k = send(keys, kv.at[0, own2], kv_sem.at[0, 0], kv_sem.at[1, 0], mate)
    send_v = send(values, kv.at[1, own2], kv_sem.at[0, 1], kv_sem.at[1, 1], mate)
    send_k.start()
    send_v.start()
    lax.fori_loop(2, NM, gather, 0)
    load_k.wait()
    load_v.wait()
    for cp in load_og:
        cp.wait()
    send_k.wait()
    send_v.wait()

    def lanes_of(hp):
        return pl.ds(pl.multiple_of(hp * 2 * HD, 2 * HD), 2 * HD)

    def first(hp):
        par = lax.rem(hp, 2)
        cols = lanes_of(hp)
        k2 = kv[0, :, :, cols].reshape(KS, 2 * HD)
        v2 = kv[1, :, :, cols].reshape(KS, 2 * HD)
        v2t = v2.T
        q_t[par] = serial[:, cols].T
        og_t[par] = og[:, :, cols].reshape(QS, 2 * HD).T
        zero = jnp.zeros((HD, PQ), BF)

        def step(p, _):
            at = pl.multiple_of(p * PQ, PQ)
            qc = pl.ds(at, PQ)
            usable = use[0:4, qc] > 0.5
            for h in range(2):
                rows = slice(h * HD, (h + 1) * HD)
                cc = pl.ds(pl.multiple_of(h * QS + at, PQ), PQ)
                qh = q_t[par, rows, qc]
                oh = og_t[par, rows, qc]
                qm = jnp.concatenate([qh, zero] if h == 0 else [zero, qh], axis=0)
                om = jnp.concatenate([oh, zero] if h == 0 else [zero, oh], axis=0)
                st = dot(k2, qm)
                m_raw = jnp.full((1, PQ), -FAR, F32)
                for kb in range(4):
                    top = jnp.max(st[kb * BS:(kb + 1) * BS], axis=0, keepdims=True)
                    m_raw = jnp.maximum(m_raw, jnp.where(usable[kb:kb + 1], top, -FAR))
                m = m_raw * C2
                dp = dot(v2, om).astype(BF)
                total = jnp.zeros((1, PQ), F32)
                weighted = jnp.zeros((1, PQ), F32)
                parts = []
                for kb in range(4):
                    off = jnp.where(usable[kb:kb + 1], m, FAR)
                    pr = jnp.exp2(st[kb * BS:(kb + 1) * BS] * C2 - off)
                    total = total + jnp.sum(pr, axis=0, keepdims=True)
                    prb = pr.astype(BF)
                    weighted = weighted + jnp.sum(
                        prb.astype(F32) * dp[kb * BS:(kb + 1) * BS].astype(F32), axis=0, keepdims=True
                    )
                    parts.append(prb)
                prb = jnp.concatenate(parts, axis=0)
                probs[par, :, cc] = prb
                dps[par, :, cc] = dp
                a_keep[par, rows, qc] = dot(v2t[rows, :], prb)
                total = jnp.maximum(total, 0.5)
                r = pl.ds(2 * p + h, 1)
                m_keep[par, r, :] = m
                stat_own[hp, 0, r, :] = m + jnp.log2(total)
                stat_own[hp, 1, r, :] = weighted / total
            return 0

        lax.fori_loop(0, NM // 2, step, 0)

        def share(d, _):
            send(stat_own.at[hp], stat_got.at[hp, d - 1], stat_sem.at[0, hp], stat_sem.at[1, hp], peer(d)).start()
            return 0

        lax.fori_loop(1, NM, share, 0)

    def stat_all(hp):
        return send(stat_got.at[hp], stat_got.at[hp], stat_sem.at[0, hp], stat_sem.at[1, hp], right)

    def second(hp):
        par = lax.rem(hp, 2)
        cols = lanes_of(hp)
        stat_all(hp).wait_recv()
        lse = [stat_own[hp, 0]] + [stat_got[hp, d, 0] for d in range(NM - 1)]
        dlt = [stat_own[hp, 1]] + [stat_got[hp, d, 1] for d in range(NM - 1)]
        top = functools.reduce(jnp.maximum, lse)
        ws = [jnp.exp2(v - top) for v in lse]
        total = functools.reduce(jnp.add, ws)
        delta_all = functools.reduce(jnp.add, [w * v for w, v in zip(ws, dlt)]) / total
        m_keep[par] = jnp.exp2(m_keep[par] - (top + jnp.log2(total)))
        d_keep[...] = delta_all
        k2t = kv[0, :, :, cols].reshape(KS, 2 * HD).T

        def step(p, _):
            at = pl.multiple_of(p * PQ, PQ)
            qc = pl.ds(at, PQ)
            for h in range(2):
                rows = slice(h * HD, (h + 1) * HD)
                cc = pl.ds(pl.multiple_of(h * QS + at, PQ), PQ)
                r = pl.ds(2 * p + h, 1)
                w = m_keep[par, r, :]
                dl = d_keep[r, :]
                ds = (probs[par, :, cc].astype(F32) * (dps[par, :, cc].astype(F32) - dl)).astype(BF)
                dps[par, :, cc] = ds
                dq = (dot(k2t[rows, :], ds) * (w * SCALE)).astype(BF)
                at_ = (a_keep[par, rows, qc] * w).astype(BF)
                for e in range(2):
                    b = 2 * p + e
                    x, y = lax.rem(b, NX), b // NX
                    aq[hp, x, y, 0, rows, :] = at_[:, e * BS:(e + 1) * BS]
                    aq[hp, x, y, 1, rows, :] = dq[:, e * BS:(e + 1) * BS]
                wog_t[rows, cc] = (og_t[par, rows, qc].astype(F32) * w).astype(BF)
                wq_t[rows, cc] = (q_t[par, rows, qc].astype(F32) * (w * SCALE)).astype(BF)
            return 0

        lax.fori_loop(0, NM // 2, step, 0)
        for cp in x1_copies(hp):
            cp.start()
        dk = dot(dps[par], wq_t[...], NT).reshape(2, 2 * BS, 2 * HD)
        dv = dot(probs[par], wog_t[...], NT).reshape(2, 2 * BS, 2 * HD)
        mine = core == 0
        c_keep[hp, 0] = jnp.where(mine, dk[0], dk[1])
        c_keep[hp, 1] = jnp.where(mine, dv[0], dv[1])
        c_send[hp, 0] = jnp.where(mine, dk[1], dk[0]).astype(BF)
        c_send[hp, 1] = jnp.where(mine, dv[1], dv[0]).astype(BF)
        c_copy(hp).start()

    def x1_copies(hp):
        return (
            send(aq.at[hp, xo, 0], x1_got.at[hp, 0], x1_sem.at[0, hp, 0], x1_sem.at[1, hp, 0], right),
            send(aq.at[hp, xo, 1], x1_got.at[hp, 1], x1_sem.at[0, hp, 1], x1_sem.at[1, hp, 1], left),
        )

    def x2_copies(hp):
        return (
            send(aq.at[hp, xr], x2_got.at[hp, 0], x2_sem.at[0, hp, 0], x2_sem.at[1, hp, 0], right),
            send(aq.at[hp, xl], x2_got.at[hp, 1], x2_sem.at[0, hp, 1], x2_sem.at[1, hp, 1], left),
        )

    def y_copy(hp):
        return send(y_send.at[hp], y_got.at[hp], y_sem.at[0, hp], y_sem.at[1, hp], across)

    def c_copy(hp):
        return send(c_send.at[hp], c_got.at[hp], c_sem.at[0, hp], c_sem.at[1, hp], mate)

    def z_all(hp):
        return send(z_got.at[hp], z_got.at[hp], z_sem.at[0, hp], z_sem.at[1, hp], slab(1))

    def relay_x(hp):
        for cp in x1_copies(hp):
            cp.wait_recv()
        aq[hp, xr, 0] = (aq[hp, xr, 0].astype(F32) + x1_got[hp, 0].astype(F32)).astype(BF)
        aq[hp, xl, 1] = (aq[hp, xl, 1].astype(F32) + x1_got[hp, 1].astype(F32)).astype(BF)
        for cp in x2_copies(hp):
            cp.start()

    def relay_c(hp):
        c_copy(hp).wait_recv()
        for a in range(2):
            total = c_keep[hp, a] + c_got[hp, a].astype(F32)
            total = total.reshape(2, NP, 8, 2 * HD).transpose(1, 0, 2, 3)
            z_send[hp, :, a] = total.reshape(NP, 16, 2 * HD).astype(BF)

        def share(d, _):
            send(
                z_send.at[hp, lax.rem(pb + d, NP)], z_got.at[hp, d - 1],
                z_sem.at[0, hp], z_sem.at[1, hp], slab(d),
            ).start()
            return 0

        lax.fori_loop(1, NP, share, 0)

    def relay_y(hp):
        for cp in x2_copies(hp):
            cp.wait_recv()

        def total(y):
            return (
                aq[hp, xi, y].astype(F32)
                + x2_got[hp, 0, y].astype(F32)
                + x2_got[hp, 1, y].astype(F32)
            )

        y_send[hp] = total(yo).astype(BF)
        y_copy(hp).start()
        y_keep[hp] = total(yi)

    def finish(hp):
        cols = lanes_of(hp)
        z_all(hp).wait_recv()
        for a, out in ((0, kg_out), (1, vg_out)):
            total = z_send[hp, pb, a].astype(F32)
            for d in range(NP - 1):
                total = total + z_got[hp, d, a].astype(F32)
            out[:, :, cols] = total.reshape(2, 8, 2 * HD)
        y_copy(hp).wait_recv()
        both = y_keep[hp] + y_got[hp].astype(F32)
        att_out[0, :, cols] = both[0].T.astype(BF)
        qg_out[0, :, cols] = both[1].T
        stat_all(hp).wait_send()
        for cp in x1_copies(hp) + x2_copies(hp):
            cp.wait_send()
        y_copy(hp).wait_send()
        c_copy(hp).wait_send()
        z_all(hp).wait_send()

    def turn(s, _):
        @pl.when(s < NC)
        def _():
            first(s)

        @pl.when((s >= 2) & (s < NC + 2))
        def _():
            relay_x(s - 2)
            relay_c(s - 2)

        @pl.when((s >= 1) & (s < NC + 1))
        def _():
            second(s - 1)

        @pl.when((s >= 2) & (s < NC + 2))
        def _():
            relay_y(s - 2)

        @pl.when(s >= 3)
        def _():
            finish(s - 3)

        return 0

    lax.fori_loop(0, NC + 3, turn, 0)


def local(queries, point_order, keys, values, pair_counts, pair_keys, out_grad):
    anyspace = pl.BlockSpec(memory_space=pl.ANY)
    vmem = pl.BlockSpec(memory_space=pltpu.VMEM)
    dma = pltpu.SemaphoreType.DMA
    w2 = 2 * HD
    return pl.pallas_call(
        kernel,
        out_shape=(
            jax.ShapeDtypeStruct((1, BS, D), BF),
            jax.ShapeDtypeStruct((1, BS, D), F32),
            jax.ShapeDtypeStruct((2, 8, D), F32),
            jax.ShapeDtypeStruct((2, 8, D), F32),
        ),
        in_specs=[anyspace, vmem, anyspace, anyspace, vmem, vmem, anyspace],
        out_specs=(vmem, vmem, vmem, vmem),
        scratch_shapes=[
            pltpu.VMEM((NP * BS, D), BF),
            pltpu.VMEM((QS, D), BF),
            pltpu.VMEM((NM, BS, D), BF),
            pltpu.VMEM((2, 4, BS, D), BF),
            pltpu.VMEM((8, QS), F32),
            pltpu.VMEM((2, w2, QS), BF),
            pltpu.VMEM((2, w2, QS), BF),
            pltpu.VMEM((w2, 2 * QS), BF),
            pltpu.VMEM((w2, 2 * QS), BF),
            pltpu.VMEM((2, KS, 2 * QS), BF),
            pltpu.VMEM((2, KS, 2 * QS), BF),
            pltpu.VMEM((2, w2, QS), F32),
            pltpu.VMEM((2, 8, PQ), F32),
            pltpu.VMEM((8, PQ), F32),
            pltpu.VMEM((NC, 2, 8, PQ), F32),
            pltpu.VMEM((NC, NM - 1, 2, 8, PQ), F32),
            pltpu.VMEM((NC, NX, NY, 2, w2, BS), BF),
            pltpu.VMEM((NC, 2, 2, w2, BS), BF),
            pltpu.VMEM((NC, 2, NY, 2, w2, BS), BF),
            pltpu.VMEM((NC, 2, w2, BS), F32),
            pltpu.VMEM((NC, 2, w2, BS), BF),
            pltpu.VMEM((NC, 2, w2, BS), BF),
            pltpu.VMEM((NC, 2, 2 * BS, w2), F32),
            pltpu.VMEM((NC, 2, 2 * BS, w2), BF),
            pltpu.VMEM((NC, 2, 2 * BS, w2), BF),
            pltpu.VMEM((NC, NP, 2, 16, w2), BF),
            pltpu.VMEM((NC, NP - 1, 2, 16, w2), BF),
            dma((3 + NM,)),
            dma((2, 2)),
            dma((2, NC)),
            dma((2, NC, 2)),
            dma((2, NC, 2)),
            dma((2, NC)),
            dma((2, NC)),
            dma((2, NC)),
        ],
        compiler_params=pltpu.CompilerParams(
            collective_id=0, has_side_effects=True, vmem_limit_bytes=48 * 1024 * 1024
        ),
        name="sparse_attention",
    )(queries, point_order, keys, values, pair_counts, pair_keys, out_grad)


def solution(mesh):
    return jax.shard_map(
        local,
        mesh=mesh,
        in_specs=(
            P("pb", None),
            P("pb", None),
            P("ka", None, None),
            P("ka", None, None),
            P("pb", None),
            P("pb", None),
            P("pb", None, None),
        ),
        out_specs=(
            P(("pb", "ka"), None, None),
            P(("pb", "ka"), None, None),
            P("ka", "pb", None),
            P("ka", "pb", None),
        ),
        check_vma=False,
    )
```

```python
import functools
import math

import jax
import jax.numpy as jnp
from jax import lax
from jax.experimental import pallas as pl
from jax.experimental.pallas import tpu as pltpu
from jax.sharding import PartitionSpec as P

H = 8
HD = 64
D = 512
BS = 128
NP = 16
NX = 4
NY = 2
NM = NX * NY
NC = 4
QS = NM * BS
KS = 4 * BS
PQ = 2 * BS
SCALE = HD ** -0.5
C2 = SCALE * math.log2(math.e)
FAR = 1e30
MESH = pl.DeviceIdType.MESH
BF = jnp.bfloat16
F32 = jnp.float32

NN = (((1,), (0,)), ((), ()))
NT = (((1,), (1,)), ((), ()))


def dot(a, b, dims=NN):
    return lax.dot_general(a, b, dims, preferred_element_type=F32)


def kernel(
    queries,
    order,
    keys,
    values,
    counts,
    listing,
    out_grad,
    att_out,
    qg_out,
    kg_out,
    vg_out,
    qbuf,
    order_v,
    counts_v,
    listing_v,
    serial,
    og,
    kv,
    use,
    q_m,
    og_m,
    og_t,
    probs,
    dss,
    a_keep,
    m_keep,
    d_keep,
    stat_own,
    stat_got,
    aq,
    x1_got,
    x2_got,
    y_keep,
    y_send,
    y_got,
    c_keep,
    c_send,
    c_got,
    z_send,
    z_got,
    load_sem,
    kv_sem,
    stat_sem,
    x1_sem,
    x2_sem,
    y_sem,
    c_sem,
    z_sem,
):
    pb = lax.axis_index("pb")
    ka = lax.axis_index("ka")
    core = lax.rem(ka, 2)
    chip = ka // 2
    xi = lax.rem(chip, NX)
    yi = chip // NX
    xr = lax.rem(xi + 1, NX)
    xl = lax.rem(xi + NX - 1, NX)
    xo = lax.rem(xi + 2, NX)
    yo = 1 - yi

    def at_ka(y, x, c):
        return {"ka": (y * NX + x) * 2 + c}

    right, left = at_ka(yi, xr, core), at_ka(yi, xl, core)
    across = at_ka(yo, xi, core)
    mate = {"ka": chip * 2 + (1 - core)}

    def peer(d):
        return {"ka": lax.rem(chip + d, NM) * 2 + core}

    def slab(d):
        return {"pb": lax.rem(pb + d, NP)}

    def send(src, dst, send_sem, recv_sem, device):
        return pltpu.make_async_remote_copy(
            src_ref=src, dst_ref=dst, send_sem=send_sem, recv_sem=recv_sem,
            device_id=device, device_id_type=MESH,
        )

    barrier = pltpu.get_barrier_semaphore()
    pl.semaphore_signal(barrier, inc=1, device_id=mate, device_id_type=MESH)

    def hello_ka(d, _):
        pl.semaphore_signal(barrier, inc=1, device_id=peer(d), device_id_type=MESH)
        return 0

    def hello_pb(d, _):
        pl.semaphore_signal(barrier, inc=1, device_id=slab(d), device_id_type=MESH)
        return 0

    lax.fori_loop(1, NM, hello_ka, 0)
    lax.fori_loop(1, NP, hello_pb, 0)

    own2 = pl.ds(2 * core, 2)
    load_q = pltpu.make_async_copy(queries, qbuf, load_sem.at[0])
    load_small = [
        pltpu.make_async_copy(order, order_v, load_sem.at[3]),
        pltpu.make_async_copy(counts, counts_v, load_sem.at[4]),
        pltpu.make_async_copy(listing, listing_v, load_sem.at[5]),
    ]
    load_kv = [
        pltpu.make_async_copy(keys, kv.at[0, own2], load_sem.at[1]),
        pltpu.make_async_copy(values, kv.at[1, own2], load_sem.at[2]),
    ]
    load_og = [
        pltpu.make_async_copy(out_grad.at[2 * b + core], og.at[b], load_sem.at[6 + b])
        for b in range(NM)
    ]
    for cp in load_small + [load_q] + load_kv + load_og:
        cp.start()
    for cp in load_small:
        cp.wait()

    cb = jnp.broadcast_to(counts_v[...].astype(F32), (16, 16))
    i0 = lax.broadcasted_iota(jnp.int32, (16, 16), 0)
    i1 = lax.broadcasted_iota(jnp.int32, (16, 16), 1)
    starts = jnp.sum(jnp.where(i1 < i0, cb, 0.0), axis=1, keepdims=True)
    sizes = jnp.sum(jnp.where(i1 == i0, cb, 0.0), axis=1, keepdims=True)
    slot = lax.broadcasted_iota(jnp.int32, (16, 256), 1).astype(F32)
    inside = jnp.where((slot >= starts) & (slot < starts + sizes), 1.0, 0.0)
    row = lax.broadcasted_iota(jnp.int32, (8, 256), 0) + 4 * chip
    named = jnp.where(jnp.broadcast_to(listing_v[...], (8, 256)) == row, 1.0, 0.0)
    joined = dot(named.astype(BF), inside.astype(BF), NT)
    e0 = lax.broadcasted_iota(jnp.int32, (16, QS), 0)
    e1 = lax.broadcasted_iota(jnp.int32, (16, QS), 1)
    spread = jnp.where(e0 == 2 * (e1 // BS) + core, 1.0, 0.0)
    use[...] = dot(joined.astype(BF), spread.astype(BF))

    load_q.wait()

    def gather(t, _):
        picks = []
        for e in range(4):
            at = pl.multiple_of((8 * t + 2 * e + core) * BS, BS)
            column = jnp.broadcast_to(order_v[:, pl.ds(at, BS)], (BS, BS)).T
            lanes = lax.broadcasted_iota(jnp.int32, (BS, BS), 1)
            picks.append(jnp.concatenate(
                [jnp.where(column == lanes + n * BS, 1.0, 0.0).astype(BF) for n in range(16)], axis=1
            ))
        pick = jnp.concatenate(picks, axis=0)
        serial[pl.ds(pl.multiple_of(t * 4 * BS, 4 * BS), 4 * BS), :] = dot(pick, qbuf[...]).astype(BF)
        return 0

    lax.fori_loop(0, 1, gather, 0)
    pl.semaphore_wait(barrier, 1 + (NM - 1) + (NP - 1))
    send_k = send(keys, kv.at[0, own2], kv_sem.at[0, 0], kv_sem.at[1, 0], mate)
    send_v = send(values, kv.at[1, own2], kv_sem.at[0, 1], kv_sem.at[1, 1], mate)
    send_k.start()
    send_v.start()
    lax.fori_loop(1, 2, gather, 0)
    for cp in load_kv + load_og:
        cp.wait()
    send_k.wait()
    send_v.wait()

    def lanes_of(hp):
        return pl.ds(pl.multiple_of(hp * 2 * HD, 2 * HD), 2 * HD)

    def flip(a):
        unit = jnp.where(
            lax.broadcasted_iota(jnp.int32, (2 * HD, 2 * HD), 0)
            == lax.broadcasted_iota(jnp.int32, (2 * HD, 2 * HD), 1), 1.0, 0.0
        ).astype(BF)
        return dot(unit, a, NT)

    def first(hp):
        par = lax.rem(hp, 2)
        cols = lanes_of(hp)
        k2 = kv[0, :, :, cols].reshape(KS, 2 * HD)
        v2t = flip(kv[1, :, :, cols].reshape(KS, 2 * HD)).astype(BF)
        og_t[...] = flip(og[:, :, cols].reshape(QS, 2 * HD))
        low = lax.broadcasted_iota(jnp.int32, (QS, 2 * HD), 1) < HD
        none = jnp.zeros((QS, 2 * HD), BF)
        for src, dst in ((serial[:, cols], q_m), (og[:, :, cols].reshape(QS, 2 * HD), og_m)):
            dst[par, :QS] = jnp.where(low, src, none)
            dst[par, QS:] = jnp.where(low, none, src)

        for p in range(NM // 2):
            qc = slice(p * PQ, (p + 1) * PQ)
            usable = use[0:4, qc] > 0.5
            for h in range(2):
                rows = slice(h * HD, (h + 1) * HD)
                cc = slice(h * QS + p * PQ, h * QS + (p + 1) * PQ)
                st = dot(k2, q_m[par, cc, :], NT)
                m_raw = jnp.full((1, PQ), -FAR, F32)
                for kb in range(4):
                    top = jnp.max(st[kb * BS:(kb + 1) * BS], axis=0, keepdims=True)
                    m_raw = jnp.maximum(m_raw, jnp.where(usable[kb:kb + 1], top, -FAR))
                m = m_raw * C2
                parts = []
                for kb in range(4):
                    off = jnp.where(usable[kb:kb + 1], m, FAR)
                    parts.append(jnp.exp2(st[kb * BS:(kb + 1) * BS] * C2 - off))
                total = jnp.sum(parts[0] + parts[1] + parts[2] + parts[3], axis=0, keepdims=True)
                prb = jnp.concatenate([v.astype(BF) for v in parts], axis=0)
                probs[par, :, cc] = prb
                a_h = dot(v2t[rows, :], prb)
                a_keep[par, rows, qc] = a_h
                weighted = jnp.sum(a_h * og_t[rows, qc], axis=0, keepdims=True)
                total = jnp.maximum(total, 0.5)
                r = slice(2 * p + h, 2 * p + h + 1)
                m_keep[par, r, :] = m
                stat_own[hp, 0, r, :] = m + jnp.log2(total)
                stat_own[hp, 1, r, :] = weighted / total

        def share(d, _):
            send(stat_own.at[hp], stat_got.at[hp, d - 1], stat_sem.at[0, hp], stat_sem.at[1, hp], peer(d)).start()
            return 0

        lax.fori_loop(1, NM, share, 0)

    def stat_all(hp):
        return send(stat_got.at[hp], stat_got.at[hp], stat_sem.at[0, hp], stat_sem.at[1, hp], right)

    def second(hp):
        par = lax.rem(hp, 2)
        cols = lanes_of(hp)
        stat_all(hp).wait_recv()
        lse = [stat_own[hp, 0]] + [stat_got[hp, d, 0] for d in range(NM - 1)]
        dlt = [stat_own[hp, 1]] + [stat_got[hp, d, 1] for d in range(NM - 1)]
        top = functools.reduce(jnp.maximum, lse)
        ws = [jnp.exp2(v - top) for v in lse]
        total = functools.reduce(jnp.add, ws)
        delta_all = functools.reduce(jnp.add, [w * v for w, v in zip(ws, dlt)]) / total
        m_keep[par] = jnp.exp2(m_keep[par] - (top + jnp.log2(total)))
        d_keep[...] = delta_all
        k2t = flip(kv[0, :, :, cols].reshape(KS, 2 * HD)).astype(BF)
        v2 = kv[1, :, :, cols].reshape(KS, 2 * HD)

        for p in range(NM // 2):
            qc = slice(p * PQ, (p + 1) * PQ)
            for h in range(2):
                rows = slice(h * HD, (h + 1) * HD)
                cc = slice(h * QS + p * PQ, h * QS + (p + 1) * PQ)
                r = slice(2 * p + h, 2 * p + h + 1)
                w = m_keep[par, r, :]
                dp = dot(v2, og_m[par, cc, :], NT)
                qf = probs[par, :, cc].astype(F32) * w
                ds = (qf * (dp - d_keep[r, :])).astype(BF)
                probs[par, :, cc] = qf.astype(BF)
                dss[:, cc] = ds
                dq = (dot(k2t[rows, :], ds) * SCALE).astype(BF)
                at_ = (a_keep[par, rows, qc] * w).astype(BF)
                for e in range(2):
                    b = 2 * p + e
                    x, y = b % NX, b // NX
                    aq[hp, x, y, 0, rows, :] = at_[:, e * BS:(e + 1) * BS]
                    aq[hp, x, y, 1, rows, :] = dq[:, e * BS:(e + 1) * BS]
        for cp in x1_copies(hp):
            cp.start()
        dk = (dot(dss[...], q_m[par]) * SCALE).reshape(2, 2 * BS, 2 * HD)
        dv = dot(probs[par], og_m[par]).reshape(2, 2 * BS, 2 * HD)
        mine = core == 0
        c_keep[hp, 0] = jnp.where(mine, dk[0], dk[1])
        c_keep[hp, 1] = jnp.where(mine, dv[0], dv[1])
        c_send[hp, 0] = jnp.where(mine, dk[1], dk[0]).astype(BF)
        c_send[hp, 1] = jnp.where(mine, dv[1], dv[0]).astype(BF)
        c_copy(hp).start()

    def x1_copies(hp):
        return (
            send(aq.at[hp, xo, 0], x1_got.at[hp, 0], x1_sem.at[0, hp, 0], x1_sem.at[1, hp, 0], right),
            send(aq.at[hp, xo, 1], x1_got.at[hp, 1], x1_sem.at[0, hp, 1], x1_sem.at[1, hp, 1], left),
        )

    def x2_copies(hp):
        return (
            send(aq.at[hp, xr], x2_got.at[hp, 0], x2_sem.at[0, hp, 0], x2_sem.at[1, hp, 0], right),
            send(aq.at[hp, xl], x2_got.at[hp, 1], x2_sem.at[0, hp, 1], x2_sem.at[1, hp, 1], left),
        )

    def y_copy(hp):
        return send(y_send.at[hp], y_got.at[hp], y_sem.at[0, hp], y_sem.at[1, hp], across)

    def c_copy(hp):
        return send(c_send.at[hp], c_got.at[hp], c_sem.at[0, hp], c_sem.at[1, hp], mate)

    def z_all(hp):
        return send(z_got.at[hp], z_got.at[hp], z_sem.at[0, hp], z_sem.at[1, hp], slab(1))

    def relay_x(hp):
        for cp in x1_copies(hp):
            cp.wait_recv()
        aq[hp, xr, 0] = (aq[hp, xr, 0].astype(F32) + x1_got[hp, 0].astype(F32)).astype(BF)
        aq[hp, xl, 1] = (aq[hp, xl, 1].astype(F32) + x1_got[hp, 1].astype(F32)).astype(BF)
        for cp in x2_copies(hp):
            cp.start()

    def relay_c(hp):
        c_copy(hp).wait_recv()
        for a in range(2):
            total = c_keep[hp, a] + c_got[hp, a].astype(F32)
            total = total.reshape(2, NP, 8, 2 * HD).transpose(1, 0, 2, 3)
            z_send[hp, :, a] = total.reshape(NP, 16, 2 * HD).astype(BF)

        def share(d, _):
            send(
                z_send.at[hp, lax.rem(pb + d, NP)], z_got.at[hp, d - 1],
                z_sem.at[0, hp], z_sem.at[1, hp], slab(d),
            ).start()
            return 0

        lax.fori_loop(1, NP, share, 0)

    def relay_y(hp):
        for cp in x2_copies(hp):
            cp.wait_recv()

        def total(y):
            return (
                aq[hp, xi, y].astype(F32)
                + x2_got[hp, 0, y].astype(F32)
                + x2_got[hp, 1, y].astype(F32)
            )

        y_send[hp] = total(yo).astype(BF)
        y_copy(hp).start()
        y_keep[hp] = total(yi)

    def finish(hp):
        cols = lanes_of(hp)
        z_all(hp).wait_recv()
        for a, out in ((0, kg_out), (1, vg_out)):
            total = z_send[hp, pb, a].astype(F32)
            for d in range(NP - 1):
                total = total + z_got[hp, d, a].astype(F32)
            out[:, :, cols] = total.reshape(2, 8, 2 * HD)
        y_copy(hp).wait_recv()
        both = y_keep[hp] + y_got[hp].astype(F32)
        att_out[0, :, cols] = both[0].T.astype(BF)
        qg_out[0, :, cols] = both[1].T
        stat_all(hp).wait_send()
        for cp in x1_copies(hp) + x2_copies(hp):
            cp.wait_send()
        y_copy(hp).wait_send()
        c_copy(hp).wait_send()
        z_all(hp).wait_send()

    def turn(s, _):
        @pl.when(s < NC)
        def _():
            first(s)

        @pl.when((s >= 2) & (s < NC + 2))
        def _():
            relay_x(s - 2)
            relay_c(s - 2)

        @pl.when((s >= 1) & (s < NC + 1))
        def _():
            second(s - 1)

        @pl.when((s >= 2) & (s < NC + 2))
        def _():
            relay_y(s - 2)

        @pl.when(s >= 3)
        def _():
            finish(s - 3)

        return 0

    lax.fori_loop(0, NC + 3, turn, 0)


def local(queries, point_order, keys, values, pair_counts, pair_keys, out_grad):
    anyspace = pl.BlockSpec(memory_space=pl.ANY)
    vmem = pl.BlockSpec(memory_space=pltpu.VMEM)
    dma = pltpu.SemaphoreType.DMA
    w2 = 2 * HD
    return pl.pallas_call(
        kernel,
        out_shape=(
            jax.ShapeDtypeStruct((1, BS, D), BF),
            jax.ShapeDtypeStruct((1, BS, D), F32),
            jax.ShapeDtypeStruct((2, 8, D), F32),
            jax.ShapeDtypeStruct((2, 8, D), F32),
        ),
        in_specs=[anyspace] * 7,
        out_specs=(vmem, vmem, vmem, vmem),
        scratch_shapes=[
            pltpu.VMEM((NP * BS, D), BF),
            pltpu.VMEM((1, NP * BS), jnp.int32),
            pltpu.VMEM((1, NP), jnp.int32),
            pltpu.VMEM((1, 256), jnp.int32),
            pltpu.VMEM((QS, D), BF),
            pltpu.VMEM((NM, BS, D), BF),
            pltpu.VMEM((2, 4, BS, D), BF),
            pltpu.VMEM((8, QS), F32),
            pltpu.VMEM((2, 2 * QS, w2), BF),
            pltpu.VMEM((2, 2 * QS, w2), BF),
            pltpu.VMEM((w2, QS), F32),
            pltpu.VMEM((2, KS, 2 * QS), BF),
            pltpu.VMEM((KS, 2 * QS), BF),
            pltpu.VMEM((2, w2, QS), F32),
            pltpu.VMEM((2, 8, PQ), F32),
            pltpu.VMEM((8, PQ), F32),
            pltpu.VMEM((NC, 2, 8, PQ), F32),
            pltpu.VMEM((NC, NM - 1, 2, 8, PQ), F32),
            pltpu.VMEM((NC, NX, NY, 2, w2, BS), BF),
            pltpu.VMEM((NC, 2, 2, w2, BS), BF),
            pltpu.VMEM((NC, 2, NY, 2, w2, BS), BF),
            pltpu.VMEM((NC, 2, w2, BS), F32),
            pltpu.VMEM((NC, 2, w2, BS), BF),
            pltpu.VMEM((NC, 2, w2, BS), BF),
            pltpu.VMEM((NC, 2, 2 * BS, w2), F32),
            pltpu.VMEM((NC, 2, 2 * BS, w2), BF),
            pltpu.VMEM((NC, 2, 2 * BS, w2), BF),
            pltpu.VMEM((NC, NP, 2, 16, w2), BF),
            pltpu.VMEM((NC, NP - 1, 2, 16, w2), BF),
            dma((6 + NM,)),
            dma((2, 2)),
            dma((2, NC)),
            dma((2, NC, 2)),
            dma((2, NC, 2)),
            dma((2, NC)),
            dma((2, NC)),
            dma((2, NC)),
        ],
        compiler_params=pltpu.CompilerParams(
            collective_id=0, has_side_effects=True, vmem_limit_bytes=60 * 1024 * 1024
        ),
        name="sparse_attention",
    )(queries, point_order, keys, values, pair_counts, pair_keys, out_grad)


def solution(mesh):
    return jax.shard_map(
        local,
        mesh=mesh,
        in_specs=(
            P("pb", None),
            P("pb", None),
            P("ka", None, None),
            P("ka", None, None),
            P("pb", None),
            P("pb", None),
            P("pb", None, None),
        ),
        out_specs=(
            P(("pb", "ka"), None, None),
            P(("pb", "ka"), None, None),
            P("ka", "pb", None),
            P("ka", "pb", None),
        ),
        check_vma=False,
    )
```

```python
import functools
import math

import jax
import jax.numpy as jnp
from jax import lax
from jax.experimental import pallas as pl
from jax.experimental.pallas import tpu as pltpu
from jax.sharding import PartitionSpec as P

H = 8
HD = 64
D = 512
BS = 128
NP = 16
NX = 4
NY = 2
NM = NX * NY
NC = 4
QS = NM * BS
KS = 4 * BS
PQ = 2 * BS
SCALE = HD ** -0.5
C2 = SCALE * math.log2(math.e)
FAR = 1e30
MESH = pl.DeviceIdType.MESH
BF = jnp.bfloat16
F32 = jnp.float32

NN = (((1,), (0,)), ((), ()))
NT = (((1,), (1,)), ((), ()))


def dot(a, b, dims=NN):
    return lax.dot_general(a, b, dims, preferred_element_type=F32)


def kernel(
    queries,
    order,
    keys,
    values,
    counts,
    listing,
    out_grad,
    att_out,
    qg_out,
    kg_out,
    vg_out,
    qbuf,
    order_v,
    counts_v,
    listing_v,
    serial,
    og,
    kv,
    use,
    q_m,
    og_m,
    og_t,
    probs,
    dss,
    a_keep,
    m_keep,
    d_keep,
    stat_own,
    stat_got,
    aq,
    x1_got,
    x2_got,
    y_keep,
    y_send,
    y_got,
    c_keep,
    c_send,
    c_got,
    z_send,
    z_got,
    load_sem,
    kv_sem,
    stat_sem,
    x1_sem,
    x2_sem,
    y_sem,
    c_sem,
    z_sem,
):
    pb = lax.axis_index("pb")
    ka = lax.axis_index("ka")
    core = lax.rem(ka, 2)
    chip = ka // 2
    xi = lax.rem(chip, NX)
    yi = chip // NX
    xr = lax.rem(xi + 1, NX)
    xl = lax.rem(xi + NX - 1, NX)
    xo = lax.rem(xi + 2, NX)
    yo = 1 - yi

    def at_ka(y, x, c):
        return {"ka": (y * NX + x) * 2 + c}

    right, left = at_ka(yi, xr, core), at_ka(yi, xl, core)
    across = at_ka(yo, xi, core)
    mate = {"ka": chip * 2 + (1 - core)}

    def peer(d):
        return {"ka": lax.rem(chip + d, NM) * 2 + core}

    def slab(d):
        return {"pb": lax.rem(pb + d, NP)}

    def send(src, dst, send_sem, recv_sem, device):
        return pltpu.make_async_remote_copy(
            src_ref=src, dst_ref=dst, send_sem=send_sem, recv_sem=recv_sem,
            device_id=device, device_id_type=MESH,
        )

    barrier = pltpu.get_barrier_semaphore()
    pl.semaphore_signal(barrier, inc=1, device_id=mate, device_id_type=MESH)

    def hello_ka(d, _):
        pl.semaphore_signal(barrier, inc=1, device_id=peer(d), device_id_type=MESH)
        return 0

    def hello_pb(d, _):
        pl.semaphore_signal(barrier, inc=1, device_id=slab(d), device_id_type=MESH)
        return 0

    lax.fori_loop(1, NM, hello_ka, 0)
    lax.fori_loop(1, NP, hello_pb, 0)

    own2 = pl.ds(2 * core, 2)
    load_q = pltpu.make_async_copy(queries, qbuf, load_sem.at[0])
    load_small = [
        pltpu.make_async_copy(order, order_v, load_sem.at[3]),
        pltpu.make_async_copy(counts, counts_v, load_sem.at[4]),
        pltpu.make_async_copy(listing, listing_v, load_sem.at[5]),
    ]
    load_kv = [
        pltpu.make_async_copy(keys, kv.at[0, own2], load_sem.at[1]),
        pltpu.make_async_copy(values, kv.at[1, own2], load_sem.at[2]),
    ]
    load_og = [
        pltpu.make_async_copy(out_grad.at[2 * b + core], og.at[b], load_sem.at[6 + b])
        for b in range(NM)
    ]
    for cp in load_small + [load_q] + load_kv + load_og:
        cp.start()
    for cp in load_small:
        cp.wait()

    cb = jnp.broadcast_to(counts_v[...].astype(F32), (16, 16))
    i0 = lax.broadcasted_iota(jnp.int32, (16, 16), 0)
    i1 = lax.broadcasted_iota(jnp.int32, (16, 16), 1)
    starts = jnp.sum(jnp.where(i1 < i0, cb, 0.0), axis=1, keepdims=True)
    sizes = jnp.sum(jnp.where(i1 == i0, cb, 0.0), axis=1, keepdims=True)
    slot = lax.broadcasted_iota(jnp.int32, (16, 256), 1).astype(F32)
    inside = jnp.where((slot >= starts) & (slot < starts + sizes), 1.0, 0.0)
    row = lax.broadcasted_iota(jnp.int32, (8, 256), 0) + 4 * chip
    named = jnp.where(jnp.broadcast_to(listing_v[...], (8, 256)) == row, 1.0, 0.0)
    joined = dot(named.astype(BF), inside.astype(BF), NT)
    e0 = lax.broadcasted_iota(jnp.int32, (16, QS), 0)
    e1 = lax.broadcasted_iota(jnp.int32, (16, QS), 1)
    spread = jnp.where(e0 == 2 * (e1 // BS) + core, 1.0, 0.0)
    use[...] = dot(joined.astype(BF), spread.astype(BF))

    load_q.wait()

    send_k = send(keys, kv.at[0, own2], kv_sem.at[0, 0], kv_sem.at[1, 0], mate)
    send_v = send(values, kv.at[1, own2], kv_sem.at[0, 1], kv_sem.at[1, 1], mate)

    def gather(t, _):
        @pl.when(t == 1)
        def _():
            pl.semaphore_wait(barrier, 1 + (NM - 1) + (NP - 1))
            send_k.start()
            send_v.start()

        picks = []
        for e in range(4):
            at = pl.multiple_of((8 * t + 2 * e + core) * BS, BS)
            column = jnp.broadcast_to(order_v[:, pl.ds(at, BS)], (BS, BS)).T
            lanes = lax.broadcasted_iota(jnp.int32, (BS, BS), 1)
            picks.append(jnp.concatenate(
                [jnp.where(column == lanes + n * BS, 1.0, 0.0).astype(BF) for n in range(16)], axis=1
            ))
        pick = jnp.concatenate(picks, axis=0)
        serial[pl.ds(pl.multiple_of(t * 4 * BS, 4 * BS), 4 * BS), :] = dot(pick, qbuf[...]).astype(BF)
        return 0

    lax.fori_loop(0, 2, gather, 0)
    for cp in load_kv + load_og:
        cp.wait()
    send_k.wait()
    send_v.wait()

    def lanes_of(hp):
        return pl.ds(pl.multiple_of(hp * 2 * HD, 2 * HD), 2 * HD)

    def flip(a):
        unit = jnp.where(
            lax.broadcasted_iota(jnp.int32, (2 * HD, 2 * HD), 0)
            == lax.broadcasted_iota(jnp.int32, (2 * HD, 2 * HD), 1), 1.0, 0.0
        ).astype(BF)
        return dot(unit, a, NT)

    def first(hp):
        par = lax.rem(hp, 2)
        cols = lanes_of(hp)
        k2 = kv[0, :, :, cols].reshape(KS, 2 * HD)
        v2t = flip(kv[1, :, :, cols].reshape(KS, 2 * HD)).astype(BF)
        og_t[...] = flip(og[:, :, cols].reshape(QS, 2 * HD))
        low = lax.broadcasted_iota(jnp.int32, (QS, 2 * HD), 1) < HD
        none = jnp.zeros((QS, 2 * HD), BF)
        for src, dst in ((serial[:, cols], q_m), (og[:, :, cols].reshape(QS, 2 * HD), og_m)):
            dst[par, :QS] = jnp.where(low, src, none)
            dst[par, QS:] = jnp.where(low, none, src)

        def step(p, _):
            at = pl.multiple_of(p * PQ, PQ)
            qc = pl.ds(at, PQ)
            usable = use[0:4, qc] > 0.5
            for h in range(2):
                rows = slice(h * HD, (h + 1) * HD)
                cc = pl.ds(pl.multiple_of(h * QS + at, PQ), PQ)
                st = dot(k2, q_m[par, cc, :], NT)
                m_raw = jnp.full((1, PQ), -FAR, F32)
                for kb in range(4):
                    top = jnp.max(st[kb * BS:(kb + 1) * BS], axis=0, keepdims=True)
                    m_raw = jnp.maximum(m_raw, jnp.where(usable[kb:kb + 1], top, -FAR))
                m = m_raw * C2
                parts = []
                for kb in range(4):
                    off = jnp.where(usable[kb:kb + 1], m, FAR)
                    parts.append(jnp.exp2(st[kb * BS:(kb + 1) * BS] * C2 - off))
                total = jnp.sum(parts[0] + parts[1] + parts[2] + parts[3], axis=0, keepdims=True)
                prb = jnp.concatenate([v.astype(BF) for v in parts], axis=0)
                probs[par, :, cc] = prb
                a_h = dot(v2t[rows, :], prb)
                a_keep[par, rows, qc] = a_h
                weighted = jnp.sum(a_h * og_t[rows, qc], axis=0, keepdims=True)
                total = jnp.maximum(total, 0.5)
                r = pl.ds(2 * p + h, 1)
                m_keep[par, r, :] = m
                stat_own[hp, 0, r, :] = m + jnp.log2(total)
                stat_own[hp, 1, r, :] = weighted / total
            return 0

        lax.fori_loop(0, NM // 2, step, 0)

        def share(d, _):
            send(stat_own.at[hp], stat_got.at[hp, d - 1], stat_sem.at[0, hp], stat_sem.at[1, hp], peer(d)).start()
            return 0

        lax.fori_loop(1, NM, share, 0)

    def stat_all(hp):
        return send(stat_got.at[hp], stat_got.at[hp], stat_sem.at[0, hp], stat_sem.at[1, hp], right)

    def second(hp):
        par = lax.rem(hp, 2)
        cols = lanes_of(hp)
        stat_all(hp).wait_recv()
        lse = [stat_own[hp, 0]] + [stat_got[hp, d, 0] for d in range(NM - 1)]
        dlt = [stat_own[hp, 1]] + [stat_got[hp, d, 1] for d in range(NM - 1)]
        top = functools.reduce(jnp.maximum, lse)
        ws = [jnp.exp2(v - top) for v in lse]
        total = functools.reduce(jnp.add, ws)
        delta_all = functools.reduce(jnp.add, [w * v for w, v in zip(ws, dlt)]) / total
        m_keep[par] = jnp.exp2(m_keep[par] - (top + jnp.log2(total)))
        d_keep[...] = delta_all
        k2t = flip(kv[0, :, :, cols].reshape(KS, 2 * HD)).astype(BF)
        v2 = kv[1, :, :, cols].reshape(KS, 2 * HD)

        def step(p, _):
            at = pl.multiple_of(p * PQ, PQ)
            qc = pl.ds(at, PQ)
            for h in range(2):
                rows = slice(h * HD, (h + 1) * HD)
                cc = pl.ds(pl.multiple_of(h * QS + at, PQ), PQ)
                r = pl.ds(2 * p + h, 1)
                w = m_keep[par, r, :]
                dp = dot(v2, og_m[par, cc, :], NT)
                qf = probs[par, :, cc].astype(F32) * w
                ds = (qf * (dp - d_keep[r, :])).astype(BF)
                probs[par, :, cc] = qf.astype(BF)
                dss[:, cc] = ds
                dq = (dot(k2t[rows, :], ds) * SCALE).astype(BF)
                at_ = (a_keep[par, rows, qc] * w).astype(BF)
                for e in range(2):
                    b = 2 * p + e
                    x, y = lax.rem(b, NX), b // NX
                    aq[hp, x, y, 0, rows, :] = at_[:, e * BS:(e + 1) * BS]
                    aq[hp, x, y, 1, rows, :] = dq[:, e * BS:(e + 1) * BS]
            return 0

        lax.fori_loop(0, NM // 2, step, 0)
        for cp in x1_copies(hp):
            cp.start()
        dk = (dot(dss[...], q_m[par]) * SCALE).reshape(2, 2 * BS, 2 * HD)
        dv = dot(probs[par], og_m[par]).reshape(2, 2 * BS, 2 * HD)
        mine = core == 0
        c_keep[hp, 0] = jnp.where(mine, dk[0], dk[1])
        c_keep[hp, 1] = jnp.where(mine, dv[0], dv[1])
        c_send[hp, 0] = jnp.where(mine, dk[1], dk[0]).astype(BF)
        c_send[hp, 1] = jnp.where(mine, dv[1], dv[0]).astype(BF)
        c_copy(hp).start()

    def x1_copies(hp):
        return (
            send(aq.at[hp, xo, 0], x1_got.at[hp, 0], x1_sem.at[0, hp, 0], x1_sem.at[1, hp, 0], right),
            send(aq.at[hp, xo, 1], x1_got.at[hp, 1], x1_sem.at[0, hp, 1], x1_sem.at[1, hp, 1], left),
        )

    def x2_copies(hp):
        return (
            send(aq.at[hp, xr], x2_got.at[hp, 0], x2_sem.at[0, hp, 0], x2_sem.at[1, hp, 0], right),
            send(aq.at[hp, xl], x2_got.at[hp, 1], x2_sem.at[0, hp, 1], x2_sem.at[1, hp, 1], left),
        )

    def y_copy(hp):
        return send(y_send.at[hp], y_got.at[hp], y_sem.at[0, hp], y_sem.at[1, hp], across)

    def c_copy(hp):
        return send(c_send.at[hp], c_got.at[hp], c_sem.at[0, hp], c_sem.at[1, hp], mate)

    def z_all(hp):
        return send(z_got.at[hp], z_got.at[hp], z_sem.at[0, hp], z_sem.at[1, hp], slab(1))

    def relay_x(hp):
        for cp in x1_copies(hp):
            cp.wait_recv()
        aq[hp, xr, 0] = (aq[hp, xr, 0].astype(F32) + x1_got[hp, 0].astype(F32)).astype(BF)
        aq[hp, xl, 1] = (aq[hp, xl, 1].astype(F32) + x1_got[hp, 1].astype(F32)).astype(BF)
        for cp in x2_copies(hp):
            cp.start()

    def relay_c(hp):
        c_copy(hp).wait_recv()
        for a in range(2):
            total = c_keep[hp, a] + c_got[hp, a].astype(F32)
            total = total.reshape(2, NP, 8, 2 * HD).transpose(1, 0, 2, 3)
            z_send[hp, :, a] = total.reshape(NP, 16, 2 * HD).astype(BF)

        def share(d, _):
            send(
                z_send.at[hp, lax.rem(pb + d, NP)], z_got.at[hp, d - 1],
                z_sem.at[0, hp], z_sem.at[1, hp], slab(d),
            ).start()
            return 0

        lax.fori_loop(1, NP, share, 0)

    def relay_y(hp):
        for cp in x2_copies(hp):
            cp.wait_recv()

        def total(y):
            return (
                aq[hp, xi, y].astype(F32)
                + x2_got[hp, 0, y].astype(F32)
                + x2_got[hp, 1, y].astype(F32)
            )

        y_send[hp] = total(yo).astype(BF)
        y_copy(hp).start()
        y_keep[hp] = total(yi)

    def finish(hp):
        cols = lanes_of(hp)
        z_all(hp).wait_recv()
        for a, out in ((0, kg_out), (1, vg_out)):
            total = z_send[hp, pb, a].astype(F32)
            for d in range(NP - 1):
                total = total + z_got[hp, d, a].astype(F32)
            out[:, :, cols] = total.reshape(2, 8, 2 * HD)
        y_copy(hp).wait_recv()
        both = y_keep[hp] + y_got[hp].astype(F32)
        att_out[0, :, cols] = both[0].T.astype(BF)
        qg_out[0, :, cols] = both[1].T
        stat_all(hp).wait_send()
        for cp in x1_copies(hp) + x2_copies(hp):
            cp.wait_send()
        y_copy(hp).wait_send()
        c_copy(hp).wait_send()
        z_all(hp).wait_send()

    def turn(s, _):
        @pl.when(s < NC)
        def _():
            first(s)

        @pl.when((s >= 2) & (s < NC + 2))
        def _():
            relay_x(s - 2)
            relay_c(s - 2)

        @pl.when((s >= 1) & (s < NC + 1))
        def _():
            second(s - 1)

        @pl.when((s >= 2) & (s < NC + 2))
        def _():
            relay_y(s - 2)

        @pl.when(s >= 3)
        def _():
            finish(s - 3)

        return 0

    lax.fori_loop(0, NC + 3, turn, 0)


def write_out(*refs):
    sems = refs[8]
    copies = [pltpu.make_async_copy(refs[i], refs[4 + i], sems.at[i]) for i in range(4)]
    for cp in copies:
        cp.start()
    for cp in copies:
        cp.wait()


def local(queries, point_order, keys, values, pair_counts, pair_keys, out_grad):
    hbm = pl.BlockSpec(memory_space=pl.ANY)
    vmem = pl.BlockSpec(memory_space=pltpu.VMEM)
    dma = pltpu.SemaphoreType.DMA
    w2 = 2 * HD
    out_shape = (
        jax.ShapeDtypeStruct((1, BS, D), BF),
        jax.ShapeDtypeStruct((1, BS, D), F32),
        jax.ShapeDtypeStruct((2, 8, D), F32),
        jax.ShapeDtypeStruct((2, 8, D), F32),
    )
    results = pl.pallas_call(
        kernel,
        out_shape=out_shape,
        in_specs=[hbm] * 7,
        out_specs=(vmem, vmem, vmem, vmem),
        scratch_shapes=[
            pltpu.VMEM((NP * BS, D), BF),
            pltpu.VMEM((1, NP * BS), jnp.int32),
            pltpu.VMEM((1, NP), jnp.int32),
            pltpu.VMEM((1, 256), jnp.int32),
            pltpu.VMEM((QS, D), BF),
            pltpu.VMEM((NM, BS, D), BF),
            pltpu.VMEM((2, 4, BS, D), BF),
            pltpu.VMEM((8, QS), F32),
            pltpu.VMEM((2, 2 * QS, w2), BF),
            pltpu.VMEM((2, 2 * QS, w2), BF),
            pltpu.VMEM((w2, QS), F32),
            pltpu.VMEM((2, KS, 2 * QS), BF),
            pltpu.VMEM((KS, 2 * QS), BF),
            pltpu.VMEM((2, w2, QS), F32),
            pltpu.VMEM((2, 8, PQ), F32),
            pltpu.VMEM((8, PQ), F32),
            pltpu.VMEM((NC, 2, 8, PQ), F32),
            pltpu.VMEM((NC, NM - 1, 2, 8, PQ), F32),
            pltpu.VMEM((NC, NX, NY, 2, w2, BS), BF),
            pltpu.VMEM((NC, 2, 2, w2, BS), BF),
            pltpu.VMEM((NC, 2, NY, 2, w2, BS), BF),
            pltpu.VMEM((NC, 2, w2, BS), F32),
            pltpu.VMEM((NC, 2, w2, BS), BF),
            pltpu.VMEM((NC, 2, w2, BS), BF),
            pltpu.VMEM((NC, 2, 2 * BS, w2), F32),
            pltpu.VMEM((NC, 2, 2 * BS, w2), BF),
            pltpu.VMEM((NC, 2, 2 * BS, w2), BF),
            pltpu.VMEM((NC, NP, 2, 16, w2), BF),
            pltpu.VMEM((NC, NP - 1, 2, 16, w2), BF),
            dma((6 + NM,)),
            dma((2, 2)),
            dma((2, NC)),
            dma((2, NC, 2)),
            dma((2, NC, 2)),
            dma((2, NC)),
            dma((2, NC)),
            dma((2, NC)),
        ],
        compiler_params=pltpu.CompilerParams(
            collective_id=0, has_side_effects=True, vmem_limit_bytes=60 * 1024 * 1024
        ),
        name="sparse_attention",
    )(queries, point_order, keys, values, pair_counts, pair_keys, out_grad)
    return pl.pallas_call(
        write_out,
        out_shape=out_shape,
        in_specs=[vmem] * 4,
        out_specs=(hbm,) * 4,
        scratch_shapes=[dma((4,))],
        name="write_out",
    )(*results)


def solution(mesh):
    return jax.shard_map(
        local,
        mesh=mesh,
        in_specs=(
            P("pb", None),
            P("pb", None),
            P("ka", None, None),
            P("ka", None, None),
            P("pb", None),
            P("pb", None),
            P("pb", None, None),
        ),
        out_specs=(
            P(("pb", "ka"), None, None),
            P(("pb", "ka"), None, None),
            P("ka", "pb", None),
            P("ka", "pb", None),
        ),
        check_vma=False,
    )
```

```python
import functools
import math

import jax
import jax.numpy as jnp
from jax import lax
from jax.experimental import pallas as pl
from jax.experimental.pallas import tpu as pltpu
from jax.sharding import PartitionSpec as P

H = 8
HD = 64
D = 512
BS = 128
NP = 16
NX = 4
NY = 2
NM = NX * NY
NC = 4
QS = NM * BS
KS = 4 * BS
PQ = 2 * BS
SCALE = HD ** -0.5
C2 = SCALE * math.log2(math.e)
FAR = 1e30
MESH = pl.DeviceIdType.MESH
BF = jnp.bfloat16
F32 = jnp.float32

NN = (((1,), (0,)), ((), ()))
NT = (((1,), (1,)), ((), ()))
TN = (((0,), (0,)), ((), ()))


def dot(a, b, dims=NN):
    return lax.dot_general(a, b, dims, preferred_element_type=F32)


def kernel(
    queries,
    order,
    keys,
    values,
    counts,
    listing,
    out_grad,
    att_out,
    qg_out,
    kg_out,
    vg_out,
    qbuf,
    order_v,
    counts_v,
    listing_v,
    serial,
    og,
    kv,
    use,
    q_m,
    og_m,
    k_m,
    v_m,
    probs,
    dps,
    m_keep,
    d_keep,
    stat_own,
    stat_got,
    aq,
    x1_got,
    x2_got,
    y_keep,
    y_send,
    y_got,
    c_keep,
    c_send,
    c_got,
    z_send,
    z_got,
    load_sem,
    kv_sem,
    stat_sem,
    x1_sem,
    x2_sem,
    y_sem,
    c_sem,
    z_sem,
):
    pb = lax.axis_index("pb")
    ka = lax.axis_index("ka")
    core = lax.rem(ka, 2)
    chip = ka // 2
    xi = lax.rem(chip, NX)
    yi = chip // NX
    xr = lax.rem(xi + 1, NX)
    xl = lax.rem(xi + NX - 1, NX)
    xo = lax.rem(xi + 2, NX)
    yo = 1 - yi

    def at_ka(y, x, c):
        return {"ka": (y * NX + x) * 2 + c}

    right, left = at_ka(yi, xr, core), at_ka(yi, xl, core)
    across = at_ka(yo, xi, core)
    mate = {"ka": chip * 2 + (1 - core)}

    def peer(d):
        return {"ka": lax.rem(chip + d, NM) * 2 + core}

    def slab(d):
        return {"pb": lax.rem(pb + d, NP)}

    def send(src, dst, send_sem, recv_sem, device):
        return pltpu.make_async_remote_copy(
            src_ref=src, dst_ref=dst, send_sem=send_sem, recv_sem=recv_sem,
            device_id=device, device_id_type=MESH,
        )

    barrier = pltpu.get_barrier_semaphore()
    pl.semaphore_signal(barrier, inc=1, device_id=mate, device_id_type=MESH)

    def hello_ka(d, _):
        pl.semaphore_signal(barrier, inc=1, device_id=peer(d), device_id_type=MESH)
        return 0

    def hello_pb(d, _):
        pl.semaphore_signal(barrier, inc=1, device_id=slab(d), device_id_type=MESH)
        return 0

    lax.fori_loop(1, NM, hello_ka, 0)
    lax.fori_loop(1, NP, hello_pb, 0)

    own2 = pl.ds(2 * core, 2)
    load_q = pltpu.make_async_copy(queries, qbuf, load_sem.at[0])
    load_small = [
        pltpu.make_async_copy(order, order_v, load_sem.at[3]),
        pltpu.make_async_copy(counts, counts_v, load_sem.at[4]),
        pltpu.make_async_copy(listing, listing_v, load_sem.at[5]),
    ]
    load_kv = [
        pltpu.make_async_copy(keys, kv.at[0, own2], load_sem.at[1]),
        pltpu.make_async_copy(values, kv.at[1, own2], load_sem.at[2]),
    ]
    load_og = [
        pltpu.make_async_copy(out_grad.at[2 * b + core], og.at[b], load_sem.at[6 + b])
        for b in range(NM)
    ]
    for cp in load_small + [load_q] + load_kv + load_og:
        cp.start()
    for cp in load_small:
        cp.wait()

    cb = jnp.broadcast_to(counts_v[...].astype(F32), (16, 16))
    i0 = lax.broadcasted_iota(jnp.int32, (16, 16), 0)
    i1 = lax.broadcasted_iota(jnp.int32, (16, 16), 1)
    starts = jnp.sum(jnp.where(i1 < i0, cb, 0.0), axis=1, keepdims=True)
    sizes = jnp.sum(jnp.where(i1 == i0, cb, 0.0), axis=1, keepdims=True)
    slot = lax.broadcasted_iota(jnp.int32, (16, 256), 1).astype(F32)
    inside = jnp.where((slot >= starts) & (slot < starts + sizes), 1.0, 0.0)
    row = lax.broadcasted_iota(jnp.int32, (8, 256), 0) + 4 * chip
    named = jnp.where(jnp.broadcast_to(listing_v[...], (8, 256)) == row, 1.0, 0.0)
    joined = dot(named.astype(BF), inside.astype(BF), NT)
    e0 = lax.broadcasted_iota(jnp.int32, (16, QS), 0)
    e1 = lax.broadcasted_iota(jnp.int32, (16, QS), 1)
    spread = jnp.where(e0 == 2 * (e1 // BS) + core, 1.0, 0.0)
    use[...] = dot(joined.astype(BF), spread.astype(BF))

    load_q.wait()

    send_k = send(keys, kv.at[0, own2], kv_sem.at[0, 0], kv_sem.at[1, 0], mate)
    send_v = send(values, kv.at[1, own2], kv_sem.at[0, 1], kv_sem.at[1, 1], mate)

    def gather(t, _):
        @pl.when(t == 1)
        def _():
            pl.semaphore_wait(barrier, 1 + (NM - 1) + (NP - 1))
            send_k.start()
            send_v.start()

        picks = []
        for e in range(4):
            at = pl.multiple_of((8 * t + 2 * e + core) * BS, BS)
            column = jnp.broadcast_to(order_v[:, pl.ds(at, BS)], (BS, BS)).T
            lanes = lax.broadcasted_iota(jnp.int32, (BS, BS), 1)
            picks.append(jnp.concatenate(
                [jnp.where(column == lanes + n * BS, 1.0, 0.0).astype(BF) for n in range(16)], axis=1
            ))
        pick = jnp.concatenate(picks, axis=0)
        serial[pl.ds(pl.multiple_of(t * 4 * BS, 4 * BS), 4 * BS), :] = dot(pick, qbuf[...]).astype(BF)
        return 0

    lax.fori_loop(0, 2, gather, 0)
    for cp in load_kv + load_og:
        cp.wait()
    send_k.wait()
    send_v.wait()

    def lanes_of(hp):
        return pl.ds(pl.multiple_of(hp * 2 * HD, 2 * HD), 2 * HD)

    def split_heads(src, dst, n):
        low = lax.broadcasted_iota(jnp.int32, (n, 2 * HD), 1) < HD
        none = jnp.zeros((n, 2 * HD), BF)
        dst[:n] = jnp.where(low, src, none)
        dst[n:] = jnp.where(low, none, src)

    def first(hp):
        par = lax.rem(hp, 2)
        cols = lanes_of(hp)
        k2 = kv[0, :, :, cols].reshape(KS, 2 * HD)
        v2 = kv[1, :, :, cols].reshape(KS, 2 * HD)
        split_heads(serial[:, cols], q_m.at[par], QS)
        split_heads(og[:, :, cols].reshape(QS, 2 * HD), og_m.at[par], QS)

        for p in range(NM // 2):
            qc = slice(p * PQ, (p + 1) * PQ)
            usable = use[0:4, qc] > 0.5
            for h in range(2):
                cc = slice(h * QS + p * PQ, h * QS + (p + 1) * PQ)
                st = dot(k2, q_m[par, cc, :], NT)
                m_raw = jnp.full((1, PQ), -FAR, F32)
                for kb in range(4):
                    top = jnp.max(st[kb * BS:(kb + 1) * BS], axis=0, keepdims=True)
                    m_raw = jnp.maximum(m_raw, jnp.where(usable[kb:kb + 1], top, -FAR))
                m = m_raw * C2
                dp = dot(v2, og_m[par, cc, :], NT)
                total = jnp.zeros((BS, PQ), F32)
                weighted = jnp.zeros((BS, PQ), F32)
                for kb in range(4):
                    ks = slice(kb * BS, (kb + 1) * BS)
                    off = jnp.where(usable[kb:kb + 1], m, FAR)
                    pr = jnp.exp2(st[ks] * C2 - off)
                    total = total + pr
                    weighted = weighted + pr * dp[ks]
                    probs[par, ks, cc] = pr.astype(BF)
                dps[par, :, cc] = dp.astype(BF)
                total = jnp.maximum(jnp.sum(total, axis=0, keepdims=True), 0.5)
                weighted = jnp.sum(weighted, axis=0, keepdims=True)
                r = slice(2 * p + h, 2 * p + h + 1)
                m_keep[par, r, :] = m
                stat_own[hp, 0, r, :] = m + jnp.log2(total)
                stat_own[hp, 1, r, :] = weighted / total

        def share(d, _):
            send(stat_own.at[hp], stat_got.at[hp, d - 1], stat_sem.at[0, hp], stat_sem.at[1, hp], peer(d)).start()
            return 0

        lax.fori_loop(1, NM, share, 0)

    def stat_all(hp):
        return send(stat_got.at[hp], stat_got.at[hp], stat_sem.at[0, hp], stat_sem.at[1, hp], right)

    def second(hp):
        par = lax.rem(hp, 2)
        cols = lanes_of(hp)
        stat_all(hp).wait_recv()
        lse = [stat_own[hp, 0]] + [stat_got[hp, d, 0] for d in range(NM - 1)]
        dlt = [stat_own[hp, 1]] + [stat_got[hp, d, 1] for d in range(NM - 1)]
        top = functools.reduce(jnp.maximum, lse)
        ws = [jnp.exp2(v - top) for v in lse]
        total = functools.reduce(jnp.add, ws)
        delta_all = functools.reduce(jnp.add, [w * v for w, v in zip(ws, dlt)]) / total
        m_keep[par] = jnp.exp2(m_keep[par] - (top + jnp.log2(total)))
        d_keep[...] = delta_all
        split_heads(kv[0, :, :, cols].reshape(KS, 2 * HD), k_m, KS)
        split_heads(kv[1, :, :, cols].reshape(KS, 2 * HD), v_m, KS)

        for p in range(NM // 2):
            att = jnp.zeros((PQ, 2 * HD), F32)
            dq = jnp.zeros((PQ, 2 * HD), F32)
            for h in range(2):
                cc = slice(h * QS + p * PQ, h * QS + (p + 1) * PQ)
                r = slice(2 * p + h, 2 * p + h + 1)
                qf = probs[par, :, cc].astype(F32) * m_keep[par, r, :]
                qb = qf.astype(BF)
                ds = (qf * (dps[par, :, cc].astype(F32) - d_keep[r, :])).astype(BF)
                probs[par, :, cc] = qb
                dps[par, :, cc] = ds
                hk = slice(h * KS, (h + 1) * KS)
                att = att + dot(qb, v_m[hk, :], TN)
                dq = dq + dot(ds, k_m[hk, :], TN)
            att = att.astype(BF)
            dq = (dq * SCALE).astype(BF)
            for e in range(2):
                b = 2 * p + e
                x, y = b % NX, b // NX
                aq[hp, x, y, 0] = att[e * BS:(e + 1) * BS]
                aq[hp, x, y, 1] = dq[e * BS:(e + 1) * BS]
        for cp in x1_copies(hp):
            cp.start()
        dk = (dot(dps[par], q_m[par]) * SCALE).reshape(2, 2 * BS, 2 * HD)
        dv = dot(probs[par], og_m[par]).reshape(2, 2 * BS, 2 * HD)
        mine = core == 0
        c_keep[hp, 0] = jnp.where(mine, dk[0], dk[1])
        c_keep[hp, 1] = jnp.where(mine, dv[0], dv[1])
        c_send[hp, 0] = jnp.where(mine, dk[1], dk[0]).astype(BF)
        c_send[hp, 1] = jnp.where(mine, dv[1], dv[0]).astype(BF)
        c_copy(hp).start()

    def x1_copies(hp):
        return (
            send(aq.at[hp, xo, 0], x1_got.at[hp, 0], x1_sem.at[0, hp, 0], x1_sem.at[1, hp, 0], right),
            send(aq.at[hp, xo, 1], x1_got.at[hp, 1], x1_sem.at[0, hp, 1], x1_sem.at[1, hp, 1], left),
        )

    def x2_copies(hp):
        return (
            send(aq.at[hp, xr], x2_got.at[hp, 0], x2_sem.at[0, hp, 0], x2_sem.at[1, hp, 0], right),
            send(aq.at[hp, xl], x2_got.at[hp, 1], x2_sem.at[0, hp, 1], x2_sem.at[1, hp, 1], left),
        )

    def y_copy(hp):
        return send(y_send.at[hp], y_got.at[hp], y_sem.at[0, hp], y_sem.at[1, hp], across)

    def c_copy(hp):
        return send(c_send.at[hp], c_got.at[hp], c_sem.at[0, hp], c_sem.at[1, hp], mate)

    def z_all(hp):
        return send(z_got.at[hp], z_got.at[hp], z_sem.at[0, hp], z_sem.at[1, hp], slab(1))

    def relay_x(hp):
        for cp in x1_copies(hp):
            cp.wait_recv()
        aq[hp, xr, 0] = (aq[hp, xr, 0].astype(F32) + x1_got[hp, 0].astype(F32)).astype(BF)
        aq[hp, xl, 1] = (aq[hp, xl, 1].astype(F32) + x1_got[hp, 1].astype(F32)).astype(BF)
        for cp in x2_copies(hp):
            cp.start()

    def relay_c(hp):
        c_copy(hp).wait_recv()
        for a in range(2):
            total = c_keep[hp, a] + c_got[hp, a].astype(F32)
            total = total.reshape(2, NP, 8, 2 * HD).transpose(1, 0, 2, 3)
            z_send[hp, :, a] = total.reshape(NP, 16, 2 * HD).astype(BF)

        def share(d, _):
            send(
                z_send.at[hp, lax.rem(pb + d, NP)], z_got.at[hp, d - 1],
                z_sem.at[0, hp], z_sem.at[1, hp], slab(d),
            ).start()
            return 0

        lax.fori_loop(1, NP, share, 0)

    def relay_y(hp):
        for cp in x2_copies(hp):
            cp.wait_recv()

        def total(y):
            return (
                aq[hp, xi, y].astype(F32)
                + x2_got[hp, 0, y].astype(F32)
                + x2_got[hp, 1, y].astype(F32)
            )

        y_send[hp] = total(yo).astype(BF)
        y_copy(hp).start()
        y_keep[hp] = total(yi)

    def finish(hp):
        cols = lanes_of(hp)
        z_all(hp).wait_recv()
        for a, out in ((0, kg_out), (1, vg_out)):
            total = z_send[hp, pb, a].astype(F32)
            for d in range(NP - 1):
                total = total + z_got[hp, d, a].astype(F32)
            out[:, :, cols] = total.reshape(2, 8, 2 * HD)
        y_copy(hp).wait_recv()
        both = y_keep[hp] + y_got[hp].astype(F32)
        att_out[0, :, cols] = both[0].astype(BF)
        qg_out[0, :, cols] = both[1]
        stat_all(hp).wait_send()
        for cp in x1_copies(hp) + x2_copies(hp):
            cp.wait_send()
        y_copy(hp).wait_send()
        c_copy(hp).wait_send()
        z_all(hp).wait_send()

    def turn(s, _):
        @pl.when(s < NC)
        def _():
            first(s)

        @pl.when((s >= 2) & (s < NC + 2))
        def _():
            relay_x(s - 2)
            relay_c(s - 2)

        @pl.when((s >= 1) & (s < NC + 1))
        def _():
            second(s - 1)

        @pl.when((s >= 2) & (s < NC + 2))
        def _():
            relay_y(s - 2)

        @pl.when(s >= 3)
        def _():
            finish(s - 3)

        return 0

    lax.fori_loop(0, NC + 3, turn, 0)


def write_out(*refs):
    sems = refs[8]
    copies = [pltpu.make_async_copy(refs[i], refs[4 + i], sems.at[i]) for i in range(4)]
    for cp in copies:
        cp.start()
    for cp in copies:
        cp.wait()


def local(queries, point_order, keys, values, pair_counts, pair_keys, out_grad):
    hbm = pl.BlockSpec(memory_space=pl.ANY)
    vmem = pl.BlockSpec(memory_space=pltpu.VMEM)
    dma = pltpu.SemaphoreType.DMA
    w2 = 2 * HD
    out_shape = (
        jax.ShapeDtypeStruct((1, BS, D), BF),
        jax.ShapeDtypeStruct((1, BS, D), F32),
        jax.ShapeDtypeStruct((2, 8, D), F32),
        jax.ShapeDtypeStruct((2, 8, D), F32),
    )
    results = pl.pallas_call(
        kernel,
        out_shape=out_shape,
        in_specs=[hbm] * 7,
        out_specs=(vmem, vmem, vmem, vmem),
        scratch_shapes=[
            pltpu.VMEM((NP * BS, D), BF),
            pltpu.VMEM((1, NP * BS), jnp.int32),
            pltpu.VMEM((1, NP), jnp.int32),
            pltpu.VMEM((1, 256), jnp.int32),
            pltpu.VMEM((QS, D), BF),
            pltpu.VMEM((NM, BS, D), BF),
            pltpu.VMEM((2, 4, BS, D), BF),
            pltpu.VMEM((8, QS), F32),
            pltpu.VMEM((2, 2 * QS, w2), BF),
            pltpu.VMEM((2, 2 * QS, w2), BF),
            pltpu.VMEM((2 * KS, w2), BF),
            pltpu.VMEM((2 * KS, w2), BF),
            pltpu.VMEM((2, KS, 2 * QS), BF),
            pltpu.VMEM((2, KS, 2 * QS), BF),
            pltpu.VMEM((2, 8, PQ), F32),
            pltpu.VMEM((8, PQ), F32),
            pltpu.VMEM((NC, 2, 8, PQ), F32),
            pltpu.VMEM((NC, NM - 1, 2, 8, PQ), F32),
            pltpu.VMEM((NC, NX, NY, 2, BS, w2), BF),
            pltpu.VMEM((NC, 2, 2, BS, w2), BF),
            pltpu.VMEM((NC, 2, NY, 2, BS, w2), BF),
            pltpu.VMEM((NC, 2, BS, w2), F32),
            pltpu.VMEM((NC, 2, BS, w2), BF),
            pltpu.VMEM((NC, 2, BS, w2), BF),
            pltpu.VMEM((NC, 2, 2 * BS, w2), F32),
            pltpu.VMEM((NC, 2, 2 * BS, w2), BF),
            pltpu.VMEM((NC, 2, 2 * BS, w2), BF),
            pltpu.VMEM((NC, NP, 2, 16, w2), BF),
            pltpu.VMEM((NC, NP - 1, 2, 16, w2), BF),
            dma((6 + NM,)),
            dma((2, 2)),
            dma((2, NC)),
            dma((2, NC, 2)),
            dma((2, NC, 2)),
            dma((2, NC)),
            dma((2, NC)),
            dma((2, NC)),
        ],
        compiler_params=pltpu.CompilerParams(
            collective_id=0, has_side_effects=True, vmem_limit_bytes=60 * 1024 * 1024
        ),
        name="sparse_attention",
    )(queries, point_order, keys, values, pair_counts, pair_keys, out_grad)
    return pl.pallas_call(
        write_out,
        out_shape=out_shape,
        in_specs=[vmem] * 4,
        out_specs=(hbm,) * 4,
        scratch_shapes=[dma((4,))],
        name="write_out",
    )(*results)


def solution(mesh):
    return jax.shard_map(
        local,
        mesh=mesh,
        in_specs=(
            P("pb", None),
            P("pb", None),
            P("ka", None, None),
            P("ka", None, None),
            P("pb", None),
            P("pb", None),
            P("pb", None, None),
        ),
        out_specs=(
            P(("pb", "ka"), None, None),
            P(("pb", "ka"), None, None),
            P("ka", "pb", None),
            P("ka", "pb", None),
        ),
        check_vma=False,
    )
```

```python
import functools
import math

import jax
import jax.numpy as jnp
from jax import lax
from jax.experimental import pallas as pl
from jax.experimental.pallas import tpu as pltpu
from jax.sharding import PartitionSpec as P

H = 8
HD = 64
D = 512
BS = 128
NP = 16
NX = 4
NY = 2
NM = NX * NY
NC = 4
QS = NM * BS
KS = 4 * BS
PQ = 2 * BS
SCALE = HD ** -0.5
C2 = SCALE * math.log2(math.e)
FAR = 1e30
MESH = pl.DeviceIdType.MESH
BF = jnp.bfloat16
F32 = jnp.float32

NN = (((1,), (0,)), ((), ()))
NT = (((1,), (1,)), ((), ()))
TN = (((0,), (0,)), ((), ()))


def dot(a, b, dims=NN):
    return lax.dot_general(a, b, dims, preferred_element_type=F32)


def kernel(
    queries,
    order,
    keys,
    values,
    counts,
    listing,
    out_grad,
    att_out,
    qg_out,
    kg_out,
    vg_out,
    qbuf,
    order_v,
    counts_v,
    listing_v,
    pick,
    serial,
    og,
    kv,
    use,
    q_m,
    og_m,
    k_m,
    v_m,
    probs,
    dps,
    m_keep,
    stat_own,
    stat_got,
    fin_got,
    aq,
    x1_got,
    x2_got,
    y_keep,
    y_send,
    y_got,
    c_keep,
    c_send,
    c_got,
    z_send,
    z_got,
    load_sem,
    kv_sem,
    stat_sem,
    fin_sem,
    x1_sem,
    x2_sem,
    y_sem,
    c_sem,
    z_sem,
):
    pb = lax.axis_index("pb")
    ka = lax.axis_index("ka")
    core = lax.rem(ka, 2)
    chip = ka // 2
    xi = lax.rem(chip, NX)
    yi = chip // NX
    xr = lax.rem(xi + 1, NX)
    xl = lax.rem(xi + NX - 1, NX)
    xo = lax.rem(xi + 2, NX)
    yo = 1 - yi

    def at_ka(y, x, c):
        return {"ka": (y * NX + x) * 2 + c}

    right, left = at_ka(yi, xr, core), at_ka(yi, xl, core)
    across = at_ka(yo, xi, core)
    mate = {"ka": chip * 2 + (1 - core)}

    def peer(d):
        return {"ka": lax.rem(chip + d, NM) * 2 + core}

    def slab(d):
        return {"pb": lax.rem(pb + d, NP)}

    def send(src, dst, send_sem, recv_sem, device):
        return pltpu.make_async_remote_copy(
            src_ref=src, dst_ref=dst, send_sem=send_sem, recv_sem=recv_sem,
            device_id=device, device_id_type=MESH,
        )

    own2 = pl.ds(2 * core, 2)
    load_q = pltpu.make_async_copy(queries, qbuf, load_sem.at[0])
    load_small = [
        pltpu.make_async_copy(order, order_v, load_sem.at[3]),
        pltpu.make_async_copy(counts, counts_v, load_sem.at[4]),
        pltpu.make_async_copy(listing, listing_v, load_sem.at[5]),
    ]
    load_kv = [
        pltpu.make_async_copy(keys, kv.at[0, own2], load_sem.at[1]),
        pltpu.make_async_copy(values, kv.at[1, own2], load_sem.at[2]),
    ]
    load_og = [
        pltpu.make_async_copy(out_grad.at[2 * b + core], og.at[b], load_sem.at[6 + b])
        for b in range(NM)
    ]
    for cp in load_small + [load_q] + load_kv + load_og:
        cp.start()

    barrier = pltpu.get_barrier_semaphore()
    pl.semaphore_signal(barrier, inc=1, device_id=mate, device_id_type=MESH)

    def hello_ka(d, _):
        pl.semaphore_signal(barrier, inc=1, device_id=peer(d), device_id_type=MESH)
        return 0

    def hello_pb(d, _):
        pl.semaphore_signal(barrier, inc=1, device_id=slab(d), device_id_type=MESH)
        return 0

    lax.fori_loop(1, NM, hello_ka, 0)
    lax.fori_loop(1, NP, hello_pb, 0)

    for cp in load_small:
        cp.wait()

    cb = jnp.broadcast_to(counts_v[...].astype(F32), (16, 16))
    i0 = lax.broadcasted_iota(jnp.int32, (16, 16), 0)
    i1 = lax.broadcasted_iota(jnp.int32, (16, 16), 1)
    starts = jnp.sum(jnp.where(i1 < i0, cb, 0.0), axis=1, keepdims=True)
    sizes = jnp.sum(jnp.where(i1 == i0, cb, 0.0), axis=1, keepdims=True)
    slot = lax.broadcasted_iota(jnp.int32, (16, 256), 1).astype(F32)
    inside = jnp.where((slot >= starts) & (slot < starts + sizes), 1.0, 0.0)
    row = lax.broadcasted_iota(jnp.int32, (8, 256), 0) + 4 * chip
    named = jnp.where(jnp.broadcast_to(listing_v[...], (8, 256)) == row, 1.0, 0.0)
    joined = dot(named.astype(BF), inside.astype(BF), NT)
    e0 = lax.broadcasted_iota(jnp.int32, (16, QS), 0)
    e1 = lax.broadcasted_iota(jnp.int32, (16, QS), 1)
    spread = jnp.where(e0 == 2 * (e1 // BS) + core, 1.0, 0.0)
    use[...] = dot(joined.astype(BF), spread.astype(BF))

    half = D // 2
    for b in range(NM):
        at = pl.multiple_of((2 * b + core) * BS, BS)
        column = jnp.broadcast_to(order_v[:, pl.ds(at, BS)], (BS, BS)).T
        lanes = lax.broadcasted_iota(jnp.int32, (BS, BS), 1)
        for n in range(16):
            pick[b * BS:(b + 1) * BS, n * BS:(n + 1) * BS] = jnp.where(
                column == lanes + n * BS, 1.0, 0.0
            ).astype(BF)
    load_q.wait()

    def gather(c):
        def part(t, _):
            rows = pl.ds(pl.multiple_of(t * 4 * BS, 4 * BS), 4 * BS)
            serial[rows, c * half:(c + 1) * half] = dot(
                pick[rows, :], qbuf[:, c * half:(c + 1) * half]
            ).astype(BF)
            return 0

        lax.fori_loop(0, 2, part, 0)

    send_k = send(keys, kv.at[0, own2], kv_sem.at[0, 0], kv_sem.at[1, 0], mate)
    send_v = send(values, kv.at[1, own2], kv_sem.at[0, 1], kv_sem.at[1, 1], mate)
    pl.semaphore_wait(barrier, 1 + (NM - 1) + (NP - 1))
    send_k.start()
    send_v.start()
    gather(0)
    for cp in load_kv + load_og:
        cp.wait()
    send_k.wait()
    send_v.wait()

    def lanes_of(hp):
        return pl.ds(pl.multiple_of(hp * 2 * HD, 2 * HD), 2 * HD)

    def split_heads(src, dst, n):
        low = lax.broadcasted_iota(jnp.int32, (n, 2 * HD), 1) < HD
        none = jnp.zeros((n, 2 * HD), BF)
        dst[:n] = jnp.where(low, src, none)
        dst[n:] = jnp.where(low, none, src)

    def first(hp):
        par = lax.rem(hp, 2)
        cols = lanes_of(hp)
        k2 = kv[0, :, :, cols].reshape(KS, 2 * HD)
        v2 = kv[1, :, :, cols].reshape(KS, 2 * HD)
        split_heads(serial[:, cols], q_m.at[par], QS)
        split_heads(og[:, :, cols].reshape(QS, 2 * HD), og_m.at[par], QS)

        for p in range(NM // 2):
            qc = slice(p * PQ, (p + 1) * PQ)
            usable = use[0:4, qc] > 0.5
            for h in range(2):
                cc = slice(h * QS + p * PQ, h * QS + (p + 1) * PQ)
                st = dot(k2, q_m[par, cc, :], NT)
                m_raw = jnp.full((1, PQ), -FAR, F32)
                for kb in range(4):
                    top = jnp.max(st[kb * BS:(kb + 1) * BS], axis=0, keepdims=True)
                    m_raw = jnp.maximum(m_raw, jnp.where(usable[kb:kb + 1], top, -FAR))
                m = m_raw * C2
                dp = dot(v2, og_m[par, cc, :], NT)
                total = jnp.zeros((BS, PQ), F32)
                weighted = jnp.zeros((BS, PQ), F32)
                for kb in range(4):
                    ks = slice(kb * BS, (kb + 1) * BS)
                    off = jnp.where(usable[kb:kb + 1], m, FAR)
                    pr = jnp.exp2(st[ks] * C2 - off)
                    total = total + pr
                    weighted = weighted + pr * dp[ks]
                    probs[par, ks, cc] = pr.astype(BF)
                dps[par, :, cc] = dp.astype(BF)
                total = jnp.maximum(jnp.sum(total, axis=0, keepdims=True), 0.5)
                weighted = jnp.sum(weighted, axis=0, keepdims=True)
                r = slice(2 * p + h, 2 * p + h + 1)
                m_keep[par, r, :] = m
                lse = m + jnp.log2(total)
                delta = weighted / total
                for e in range(2):
                    stat_own[hp, 2 * p + e, h:h + 1, :] = lse[:, e * BS:(e + 1) * BS]
                    stat_own[hp, 2 * p + e, 2 + h:3 + h, :] = delta[:, e * BS:(e + 1) * BS]

        def share(d, _):
            send(
                stat_own.at[hp, lax.rem(chip + d, NM)], stat_got.at[hp, d - 1],
                stat_sem.at[0, hp], stat_sem.at[1, hp], peer(d),
            ).start()
            return 0

        lax.fori_loop(1, NM, share, 0)

    def stat_all(hp):
        return send(stat_got.at[hp], stat_got.at[hp], stat_sem.at[0, hp], stat_sem.at[1, hp], right)

    def fin_all(hp):
        got = fin_got.at[hp, pl.ds(0, NM - 1)]
        return send(got, got, fin_sem.at[0, hp], fin_sem.at[1, hp], right)

    def combine(hp):
        stat_all(hp).wait_recv()
        own = stat_own[hp, chip]
        parts = [own] + [stat_got[hp, d] for d in range(NM - 1)]
        lse = [v[0:2] for v in parts]
        top = functools.reduce(jnp.maximum, lse)
        ws = [jnp.exp2(v - top) for v in lse]
        total = functools.reduce(jnp.add, ws)
        delta = functools.reduce(jnp.add, [w * v[2:4] for w, v in zip(ws, parts)]) / total
        fin_got[hp, NM - 1, 0:2] = top + jnp.log2(total)
        fin_got[hp, NM - 1, 2:4] = delta

        def share(d, _):
            send(
                fin_got.at[hp, NM - 1], fin_got.at[hp, d - 1],
                fin_sem.at[0, hp], fin_sem.at[1, hp], peer(d),
            ).start()
            return 0

        lax.fori_loop(1, NM, share, 0)

    def fin_row(hp, p, row):
        return jnp.concatenate(
            [fin_got[hp, lax.rem(chip - (2 * p + e) + 2 * NM - 1, NM), row:row + 1, :] for e in range(2)], axis=1
        )

    def put(hp, kind, p, block):
        for e in range(2):
            b = 2 * p + e
            aq[hp, kind, b % NX, b // NX] = block[e * BS:(e + 1) * BS]

    def hand_over(hp, kind, grad):
        grad = grad.reshape(2, 2 * BS, 2 * HD)
        mine = core == 0
        c_keep[hp, kind] = jnp.where(mine, grad[0], grad[1])
        c_send[hp, kind] = jnp.where(mine, grad[1], grad[0]).astype(BF)
        c_copy(hp, kind).start()

    def second_v(hp):
        par = lax.rem(hp, 2)
        cols = lanes_of(hp)
        fin_all(hp).wait_recv()
        split_heads(kv[1, :, :, cols].reshape(KS, 2 * HD), v_m, KS)
        for p in range(NM // 2):
            att = jnp.zeros((PQ, 2 * HD), F32)
            for h in range(2):
                cc = slice(h * QS + p * PQ, h * QS + (p + 1) * PQ)
                r = slice(2 * p + h, 2 * p + h + 1)
                w = jnp.exp2(m_keep[par, r, :] - fin_row(hp, p, h))
                qb = (probs[par, :, cc].astype(F32) * w).astype(BF)
                probs[par, :, cc] = qb
                att = att + dot(qb, v_m[h * KS:(h + 1) * KS, :], TN)
            put(hp, 0, p, att.astype(BF))
        for cp in x1_copies(hp, 0):
            cp.start()

    def value_part(hp):
        par = lax.rem(hp, 2)
        hand_over(hp, 1, dot(probs[par], og_m[par]))

    def second_k(hp):
        par = lax.rem(hp, 2)
        cols = lanes_of(hp)
        split_heads(kv[0, :, :, cols].reshape(KS, 2 * HD), k_m, KS)
        for p in range(NM // 2):
            dq = jnp.zeros((PQ, 2 * HD), F32)
            for h in range(2):
                cc = slice(h * QS + p * PQ, h * QS + (p + 1) * PQ)
                ds = (
                    probs[par, :, cc].astype(F32) * (dps[par, :, cc].astype(F32) - fin_row(hp, p, 2 + h))
                ).astype(BF)
                dps[par, :, cc] = ds
                dq = dq + dot(ds, k_m[h * KS:(h + 1) * KS, :], TN)
            put(hp, 1, p, (dq * SCALE).astype(BF))
        for cp in x1_copies(hp, 1):
            cp.start()

    def key_part(hp):
        par = lax.rem(hp, 2)
        hand_over(hp, 0, dot(dps[par], q_m[par]) * SCALE)

    def x1_copies(hp, kind):
        return tuple(
            send(
                aq.at[hp, kind, xo, way], x1_got.at[hp, kind, way],
                x1_sem.at[0, hp, kind, way], x1_sem.at[1, hp, kind, way], (right, left)[way],
            ) for way in range(2)
        )

    def x2_copies(hp, kind):
        return tuple(
            send(
                aq.at[hp, kind, (xr, xl)[way]], x2_got.at[hp, kind, way],
                x2_sem.at[0, hp, kind, way], x2_sem.at[1, hp, kind, way], (right, left)[way],
            ) for way in range(2)
        )

    def y_copy(hp, kind):
        return send(y_send.at[hp, kind], y_got.at[hp, kind], y_sem.at[0, hp, kind], y_sem.at[1, hp, kind], across)

    def c_copy(hp, kind):
        return send(c_send.at[hp, kind], c_got.at[hp, kind], c_sem.at[0, hp, kind], c_sem.at[1, hp, kind], mate)

    def z_all(hp):
        return send(z_got.at[hp], z_got.at[hp], z_sem.at[0, hp], z_sem.at[1, hp], slab(1))

    def relay_x(hp, kind):
        for cp in x1_copies(hp, kind):
            cp.wait_recv()
        for way, x in ((0, xr), (1, xl)):
            aq[hp, kind, x, way] = (aq[hp, kind, x, way].astype(F32) + x1_got[hp, kind, way].astype(F32)).astype(BF)
        for cp in x2_copies(hp, kind):
            cp.start()

    def relay_y(hp, kind):
        for cp in x2_copies(hp, kind):
            cp.wait_recv()

        def total(y):
            return (
                aq[hp, kind, xi, y].astype(F32)
                + x2_got[hp, kind, 0, y].astype(F32)
                + x2_got[hp, kind, 1, y].astype(F32)
            )

        y_send[hp, kind] = total(yo).astype(BF)
        y_copy(hp, kind).start()
        y_keep[hp, kind] = total(yi)

    def relay_c(hp):
        for a in range(2):
            c_copy(hp, a).wait_recv()
            total = c_keep[hp, a] + c_got[hp, a].astype(F32)
            total = total.reshape(2, NP, 8, 2 * HD).transpose(1, 0, 2, 3)
            z_send[hp, :, a] = total.reshape(NP, 16, 2 * HD).astype(BF)

        def share(d, _):
            send(
                z_send.at[hp, lax.rem(pb + d, NP)], z_got.at[hp, d - 1],
                z_sem.at[0, hp], z_sem.at[1, hp], slab(d),
            ).start()
            return 0

        lax.fori_loop(1, NP, share, 0)

    def finish(hp):
        cols = lanes_of(hp)
        for kind, out in ((0, att_out), (1, qg_out)):
            y_copy(hp, kind).wait_recv()
            out[0, :, cols] = (y_keep[hp, kind] + y_got[hp, kind].astype(F32)).astype(out.dtype)
        z_all(hp).wait_recv()
        for a, out in ((0, kg_out), (1, vg_out)):
            total = z_send[hp, pb, a].astype(F32)
            for d in range(NP - 1):
                total = total + z_got[hp, d, a].astype(F32)
            out[:, :, cols] = total.reshape(2, 8, 2 * HD)
        stat_all(hp).wait_send()
        fin_all(hp).wait_send()
        for kind in range(2):
            for cp in x1_copies(hp, kind) + x2_copies(hp, kind):
                cp.wait_send()
            y_copy(hp, kind).wait_send()
            c_copy(hp, kind).wait_send()
        z_all(hp).wait_send()

    def turn(s, _):
        @pl.when(s < NC)
        def _():
            first(s)

        @pl.when(s == 0)
        def _():
            gather(1)

        @pl.when(s >= 2)
        def _():
            relay_x(s - 2, 1)
            relay_y(s - 2, 0)
            relay_c(s - 2)

        @pl.when((s >= 1) & (s <= NC))
        def _():
            second_v(s - 1)

        @pl.when(s >= 2)
        def _():
            relay_y(s - 2, 1)

        @pl.when((s >= 1) & (s <= NC))
        def _():
            value_part(s - 1)

        @pl.when(s < NC)
        def _():
            combine(s)

        @pl.when((s >= 1) & (s <= NC))
        def _():
            second_k(s - 1)
            relay_x(s - 1, 0)
            key_part(s - 1)

        @pl.when(s >= 2)
        def _():
            finish(s - 2)

        return 0

    lax.fori_loop(0, NC + 2, turn, 0)


def write_out(*refs):
    sems = refs[8]
    copies = [pltpu.make_async_copy(refs[i], refs[4 + i], sems.at[i]) for i in range(4)]
    for cp in copies:
        cp.start()
    for cp in copies:
        cp.wait()


def local(queries, point_order, keys, values, pair_counts, pair_keys, out_grad):
    hbm = pl.BlockSpec(memory_space=pl.ANY)
    vmem = pl.BlockSpec(memory_space=pltpu.VMEM)
    dma = pltpu.SemaphoreType.DMA
    w2 = 2 * HD
    out_shape = (
        jax.ShapeDtypeStruct((1, BS, D), BF),
        jax.ShapeDtypeStruct((1, BS, D), F32),
        jax.ShapeDtypeStruct((2, 8, D), F32),
        jax.ShapeDtypeStruct((2, 8, D), F32),
    )
    results = pl.pallas_call(
        kernel,
        out_shape=out_shape,
        in_specs=[hbm] * 7,
        out_specs=(vmem, vmem, vmem, vmem),
        scratch_shapes=[
            pltpu.VMEM((NP * BS, D), BF),
            pltpu.VMEM((1, NP * BS), jnp.int32),
            pltpu.VMEM((1, NP), jnp.int32),
            pltpu.VMEM((1, 256), jnp.int32),
            pltpu.VMEM((QS, NP * BS), BF),
            pltpu.VMEM((QS, D), BF),
            pltpu.VMEM((NM, BS, D), BF),
            pltpu.VMEM((2, 4, BS, D), BF),
            pltpu.VMEM((8, QS), F32),
            pltpu.VMEM((2, 2 * QS, w2), BF),
            pltpu.VMEM((2, 2 * QS, w2), BF),
            pltpu.VMEM((2 * KS, w2), BF),
            pltpu.VMEM((2 * KS, w2), BF),
            pltpu.VMEM((2, KS, 2 * QS), BF),
            pltpu.VMEM((2, KS, 2 * QS), BF),
            pltpu.VMEM((2, 8, PQ), F32),
            pltpu.VMEM((NC, NM, 4, BS), F32),
            pltpu.VMEM((NC, NM - 1, 4, BS), F32),
            pltpu.VMEM((NC, NM, 4, BS), F32),
            pltpu.VMEM((NC, 2, NX, NY, BS, w2), BF),
            pltpu.VMEM((NC, 2, 2, BS, w2), BF),
            pltpu.VMEM((NC, 2, 2, NY, BS, w2), BF),
            pltpu.VMEM((NC, 2, BS, w2), F32),
            pltpu.VMEM((NC, 2, BS, w2), BF),
            pltpu.VMEM((NC, 2, BS, w2), BF),
            pltpu.VMEM((NC, 2, 2 * BS, w2), F32),
            pltpu.VMEM((NC, 2, 2 * BS, w2), BF),
            pltpu.VMEM((NC, 2, 2 * BS, w2), BF),
            pltpu.VMEM((NC, NP, 2, 16, w2), BF),
            pltpu.VMEM((NC, NP - 1, 2, 16, w2), BF),
            dma((6 + NM,)),
            dma((2, 2)),
            dma((2, NC)),
            dma((2, NC)),
            dma((2, NC, 2, 2)),
            dma((2, NC, 2, 2)),
            dma((2, NC, 2)),
            dma((2, NC, 2)),
            dma((2, NC)),
        ],
        compiler_params=pltpu.CompilerParams(
            collective_id=0, has_side_effects=True, vmem_limit_bytes=60 * 1024 * 1024
        ),
        name="sparse_attention",
    )(queries, point_order, keys, values, pair_counts, pair_keys, out_grad)
    return pl.pallas_call(
        write_out,
        out_shape=out_shape,
        in_specs=[vmem] * 4,
        out_specs=(hbm,) * 4,
        scratch_shapes=[dma((4,))],
        name="write_out",
    )(*results)


def solution(mesh):
    return jax.shard_map(
        local,
        mesh=mesh,
        in_specs=(
            P("pb", None),
            P("pb", None),
            P("ka", None, None),
            P("ka", None, None),
            P("pb", None),
            P("pb", None),
            P("pb", None, None),
        ),
        out_specs=(
            P(("pb", "ka"), None, None),
            P(("pb", "ka"), None, None),
            P("ka", "pb", None),
            P("ka", "pb", None),
        ),
        check_vma=False,
    )
```

```python
import functools
import math

import jax
import jax.numpy as jnp
from jax import lax
from jax.experimental import pallas as pl
from jax.experimental.pallas import tpu as pltpu
from jax.sharding import PartitionSpec as P

H = 8
HD = 64
D = 512
BS = 128
NP = 16
NX = 4
NY = 2
NM = NX * NY
NC = 4
QS = NM * BS
KS = 4 * BS
PQ = 2 * BS
SCALE = HD ** -0.5
C2 = SCALE * math.log2(math.e)
FAR = 1e30
MESH = pl.DeviceIdType.MESH
BF = jnp.bfloat16
F32 = jnp.float32

NN = (((1,), (0,)), ((), ()))
NT = (((1,), (1,)), ((), ()))
TN = (((0,), (0,)), ((), ()))


def dot(a, b, dims=NN):
    return lax.dot_general(a, b, dims, preferred_element_type=F32)


def kernel(
    queries,
    order,
    keys,
    values,
    counts,
    listing,
    out_grad,
    att_out,
    qg_out,
    kg_out,
    vg_out,
    qbuf,
    order_v,
    counts_v,
    listing_v,
    serial,
    og,
    kv,
    use,
    q_m,
    og_m,
    k_m,
    v_m,
    probs,
    dps,
    m_keep,
    d_keep,
    stat_own,
    stat_got,
    aq,
    x1_got,
    x2_got,
    y_keep,
    y_send,
    y_got,
    c_keep,
    c_send,
    c_got,
    z_send,
    z_got,
    load_sem,
    kv_sem,
    stat_sem,
    x1_sem,
    x2_sem,
    y_sem,
    c_sem,
    z_sem,
):
    pb = lax.axis_index("pb")
    ka = lax.axis_index("ka")
    core = lax.rem(ka, 2)
    chip = ka // 2
    xi = lax.rem(chip, NX)
    yi = chip // NX
    xr = lax.rem(xi + 1, NX)
    xl = lax.rem(xi + NX - 1, NX)
    xo = lax.rem(xi + 2, NX)
    yo = 1 - yi

    def at_ka(y, x, c):
        return {"ka": (y * NX + x) * 2 + c}

    right, left = at_ka(yi, xr, core), at_ka(yi, xl, core)
    across = at_ka(yo, xi, core)
    mate = {"ka": chip * 2 + (1 - core)}

    def peer(d):
        return {"ka": lax.rem(chip + d, NM) * 2 + core}

    def slab(d):
        return {"pb": lax.rem(pb + d, NP)}

    def send(src, dst, send_sem, recv_sem, device):
        return pltpu.make_async_remote_copy(
            src_ref=src, dst_ref=dst, send_sem=send_sem, recv_sem=recv_sem,
            device_id=device, device_id_type=MESH,
        )

    own2 = pl.ds(2 * core, 2)
    load_q = pltpu.make_async_copy(queries, qbuf, load_sem.at[0])
    load_small = [
        pltpu.make_async_copy(order, order_v, load_sem.at[3]),
        pltpu.make_async_copy(counts, counts_v, load_sem.at[4]),
        pltpu.make_async_copy(listing, listing_v, load_sem.at[5]),
    ]
    load_kv = [
        pltpu.make_async_copy(keys, kv.at[0, own2], load_sem.at[1]),
        pltpu.make_async_copy(values, kv.at[1, own2], load_sem.at[2]),
    ]
    load_og = [
        pltpu.make_async_copy(out_grad.at[2 * b + core], og.at[b], load_sem.at[6 + b])
        for b in range(NM)
    ]
    for cp in load_small + [load_q] + load_kv + load_og:
        cp.start()

    barrier = pltpu.get_barrier_semaphore()
    pl.semaphore_signal(barrier, inc=1, device_id=mate, device_id_type=MESH)

    def hello_ka(d, _):
        pl.semaphore_signal(barrier, inc=1, device_id=peer(d), device_id_type=MESH)
        return 0

    def hello_pb(d, _):
        pl.semaphore_signal(barrier, inc=1, device_id=slab(d), device_id_type=MESH)
        return 0

    lax.fori_loop(1, NM, hello_ka, 0)
    lax.fori_loop(1, NP, hello_pb, 0)

    for cp in load_small:
        cp.wait()

    cb = jnp.broadcast_to(counts_v[...].astype(F32), (16, 16))
    i0 = lax.broadcasted_iota(jnp.int32, (16, 16), 0)
    i1 = lax.broadcasted_iota(jnp.int32, (16, 16), 1)
    starts = jnp.sum(jnp.where(i1 < i0, cb, 0.0), axis=1, keepdims=True)
    sizes = jnp.sum(jnp.where(i1 == i0, cb, 0.0), axis=1, keepdims=True)
    slot = lax.broadcasted_iota(jnp.int32, (16, 256), 1).astype(F32)
    inside = jnp.where((slot >= starts) & (slot < starts + sizes), 1.0, 0.0)
    row = lax.broadcasted_iota(jnp.int32, (8, 256), 0) + 4 * chip
    named = jnp.where(jnp.broadcast_to(listing_v[...], (8, 256)) == row, 1.0, 0.0)
    joined = dot(named.astype(BF), inside.astype(BF), NT)
    e0 = lax.broadcasted_iota(jnp.int32, (16, QS), 0)
    e1 = lax.broadcasted_iota(jnp.int32, (16, QS), 1)
    spread = jnp.where(e0 == 2 * (e1 // BS) + core, 1.0, 0.0)
    use[...] = dot(joined.astype(BF), spread.astype(BF))

    load_q.wait()

    send_k = send(keys, kv.at[0, own2], kv_sem.at[0, 0], kv_sem.at[1, 0], mate)
    send_v = send(values, kv.at[1, own2], kv_sem.at[0, 1], kv_sem.at[1, 1], mate)

    def gather(t, _):
        @pl.when(t == 1)
        def _():
            pl.semaphore_wait(barrier, 1 + (NM - 1) + (NP - 1))
            send_k.start()
            send_v.start()

        picks = []
        for e in range(4):
            at = pl.multiple_of((8 * t + 2 * e + core) * BS, BS)
            column = jnp.broadcast_to(order_v[:, pl.ds(at, BS)], (BS, BS)).T
            lanes = lax.broadcasted_iota(jnp.int32, (BS, BS), 1)
            picks.append(jnp.concatenate(
                [jnp.where(column == lanes + n * BS, 1.0, 0.0).astype(BF) for n in range(16)], axis=1
            ))
        pick = jnp.concatenate(picks, axis=0)
        serial[pl.ds(pl.multiple_of(t * 4 * BS, 4 * BS), 4 * BS), :] = dot(pick, qbuf[...]).astype(BF)
        return 0

    lax.fori_loop(0, 2, gather, 0)
    for cp in load_kv + load_og:
        cp.wait()
    send_k.wait()
    send_v.wait()

    def lanes_of(hp):
        return pl.ds(pl.multiple_of(hp * 2 * HD, 2 * HD), 2 * HD)

    def split_heads(src, dst, n):
        low = lax.broadcasted_iota(jnp.int32, (n, 2 * HD), 1) < HD
        none = jnp.zeros((n, 2 * HD), BF)
        dst[:n] = jnp.where(low, src, none)
        dst[n:] = jnp.where(low, none, src)

    def first(hp):
        par = lax.rem(hp, 2)
        cols = lanes_of(hp)
        k2 = kv[0, :, :, cols].reshape(KS, 2 * HD)
        v2 = kv[1, :, :, cols].reshape(KS, 2 * HD)
        split_heads(serial[:, cols], q_m.at[par], QS)
        split_heads(og[:, :, cols].reshape(QS, 2 * HD), og_m.at[par], QS)

        for p in range(NM // 2):
            qc = slice(p * PQ, (p + 1) * PQ)
            usable = use[0:4, qc] > 0.5
            for h in range(2):
                cc = slice(h * QS + p * PQ, h * QS + (p + 1) * PQ)
                st = dot(k2, q_m[par, cc, :], NT)
                m_raw = jnp.full((1, PQ), -FAR, F32)
                for kb in range(4):
                    top = jnp.max(st[kb * BS:(kb + 1) * BS], axis=0, keepdims=True)
                    m_raw = jnp.maximum(m_raw, jnp.where(usable[kb:kb + 1], top, -FAR))
                m = m_raw * C2
                dp = dot(v2, og_m[par, cc, :], NT)
                total = jnp.zeros((BS, PQ), F32)
                weighted = jnp.zeros((BS, PQ), F32)
                for kb in range(4):
                    ks = slice(kb * BS, (kb + 1) * BS)
                    off = jnp.where(usable[kb:kb + 1], m, FAR)
                    pr = jnp.exp2(st[ks] * C2 - off)
                    total = total + pr
                    weighted = weighted + pr * dp[ks]
                    probs[par, ks, cc] = pr.astype(BF)
                dps[par, :, cc] = dp.astype(BF)
                total = jnp.maximum(jnp.sum(total, axis=0, keepdims=True), 0.5)
                weighted = jnp.sum(weighted, axis=0, keepdims=True)
                r = slice(2 * p + h, 2 * p + h + 1)
                m_keep[par, r, :] = m
                stat_own[hp, 0, r, :] = m + jnp.log2(total)
                stat_own[hp, 1, r, :] = weighted / total

        def share(d, _):
            send(stat_own.at[hp], stat_got.at[hp, d - 1], stat_sem.at[0, hp], stat_sem.at[1, hp], peer(d)).start()
            return 0

        lax.fori_loop(1, NM, share, 0)

    def stat_all(hp):
        return send(stat_got.at[hp], stat_got.at[hp], stat_sem.at[0, hp], stat_sem.at[1, hp], right)

    def second(hp):
        par = lax.rem(hp, 2)
        cols = lanes_of(hp)
        stat_all(hp).wait_recv()
        lse = [stat_own[hp, 0]] + [stat_got[hp, d, 0] for d in range(NM - 1)]
        dlt = [stat_own[hp, 1]] + [stat_got[hp, d, 1] for d in range(NM - 1)]
        top = functools.reduce(jnp.maximum, lse)
        ws = [jnp.exp2(v - top) for v in lse]
        total = functools.reduce(jnp.add, ws)
        delta_all = functools.reduce(jnp.add, [w * v for w, v in zip(ws, dlt)]) / total
        m_keep[par] = jnp.exp2(m_keep[par] - (top + jnp.log2(total)))
        d_keep[...] = delta_all
        split_heads(kv[0, :, :, cols].reshape(KS, 2 * HD), k_m, KS)
        split_heads(kv[1, :, :, cols].reshape(KS, 2 * HD), v_m, KS)

        for p in range(NM // 2):
            att = jnp.zeros((PQ, 2 * HD), F32)
            dq = jnp.zeros((PQ, 2 * HD), F32)
            for h in range(2):
                cc = slice(h * QS + p * PQ, h * QS + (p + 1) * PQ)
                r = slice(2 * p + h, 2 * p + h + 1)
                qf = probs[par, :, cc].astype(F32) * m_keep[par, r, :]
                qb = qf.astype(BF)
                ds = (qf * (dps[par, :, cc].astype(F32) - d_keep[r, :])).astype(BF)
                probs[par, :, cc] = qb
                dps[par, :, cc] = ds
                hk = slice(h * KS, (h + 1) * KS)
                att = att + dot(qb, v_m[hk, :], TN)
                dq = dq + dot(ds, k_m[hk, :], TN)
            att = att.astype(BF)
            dq = (dq * SCALE).astype(BF)
            for e in range(2):
                b = 2 * p + e
                x, y = b % NX, b // NX
                aq[hp, x, y, 0] = att[e * BS:(e + 1) * BS]
                aq[hp, x, y, 1] = dq[e * BS:(e + 1) * BS]
        for cp in x1_copies(hp):
            cp.start()
        dk = (dot(dps[par], q_m[par]) * SCALE).reshape(2, 2 * BS, 2 * HD)
        dv = dot(probs[par], og_m[par]).reshape(2, 2 * BS, 2 * HD)
        mine = core == 0
        c_keep[hp, 0] = jnp.where(mine, dk[0], dk[1])
        c_keep[hp, 1] = jnp.where(mine, dv[0], dv[1])
        c_send[hp, 0] = jnp.where(mine, dk[1], dk[0]).astype(BF)
        c_send[hp, 1] = jnp.where(mine, dv[1], dv[0]).astype(BF)
        c_copy(hp).start()

    def x1_copies(hp):
        return (
            send(aq.at[hp, xo, 0], x1_got.at[hp, 0], x1_sem.at[0, hp, 0], x1_sem.at[1, hp, 0], right),
            send(aq.at[hp, xo, 1], x1_got.at[hp, 1], x1_sem.at[0, hp, 1], x1_sem.at[1, hp, 1], left),
        )

    def x2_copies(hp):
        return (
            send(aq.at[hp, xr], x2_got.at[hp, 0], x2_sem.at[0, hp, 0], x2_sem.at[1, hp, 0], right),
            send(aq.at[hp, xl], x2_got.at[hp, 1], x2_sem.at[0, hp, 1], x2_sem.at[1, hp, 1], left),
        )

    def y_copy(hp):
        return send(y_send.at[hp], y_got.at[hp], y_sem.at[0, hp], y_sem.at[1, hp], across)

    def c_copy(hp):
        return send(c_send.at[hp], c_got.at[hp], c_sem.at[0, hp], c_sem.at[1, hp], mate)

    def z_all(pair):
        return send(z_got.at[pair], z_got.at[pair], z_sem.at[0, pair], z_sem.at[1, pair], slab(1))

    def relay_x(hp):
        for cp in x1_copies(hp):
            cp.wait_recv()
        aq[hp, xr, 0] = (aq[hp, xr, 0].astype(F32) + x1_got[hp, 0].astype(F32)).astype(BF)
        aq[hp, xl, 1] = (aq[hp, xl, 1].astype(F32) + x1_got[hp, 1].astype(F32)).astype(BF)
        for cp in x2_copies(hp):
            cp.start()

    def relay_c(hp):
        c_copy(hp).wait_recv()
        pair = hp // 2
        for a in range(2):
            total = c_keep[hp, a] + c_got[hp, a].astype(F32)
            total = total.reshape(2, NP, 8, 2 * HD).transpose(1, 0, 2, 3)
            z_send[pair, :, 2 * lax.rem(hp, 2) + a] = total.reshape(NP, 16, 2 * HD).astype(BF)

        def share(d, _):
            send(
                z_send.at[pair, lax.rem(pb + d, NP)], z_got.at[pair, d - 1],
                z_sem.at[0, pair], z_sem.at[1, pair], slab(d),
            ).start()
            return 0

        @pl.when(lax.rem(hp, 2) == 1)
        def _():
            lax.fori_loop(1, NP, share, 0)

    def relay_y(hp):
        for cp in x2_copies(hp):
            cp.wait_recv()

        def total(y):
            return (
                aq[hp, xi, y].astype(F32)
                + x2_got[hp, 0, y].astype(F32)
                + x2_got[hp, 1, y].astype(F32)
            )

        y_send[hp] = total(yo).astype(BF)
        y_copy(hp).start()
        y_keep[hp] = total(yi)

    def finish(hp):
        cols = lanes_of(hp)
        y_copy(hp).wait_recv()
        both = y_keep[hp] + y_got[hp].astype(F32)
        att_out[0, :, cols] = both[0].astype(BF)
        qg_out[0, :, cols] = both[1]
        stat_all(hp).wait_send()
        for cp in x1_copies(hp) + x2_copies(hp):
            cp.wait_send()
        y_copy(hp).wait_send()
        c_copy(hp).wait_send()

        @pl.when(lax.rem(hp, 2) == 1)
        def _():
            pair = hp // 2
            z_all(pair).wait_recv()
            for q in range(2):
                cols = lanes_of(2 * pair + q)
                for a, out in ((0, kg_out), (1, vg_out)):
                    total = z_send[pair, pb, 2 * q + a].astype(F32)
                    for d in range(NP - 1):
                        total = total + z_got[pair, d, 2 * q + a].astype(F32)
                    out[:, :, cols] = total.reshape(2, 8, 2 * HD)
            z_all(pair).wait_send()

    def turn(s, _):
        @pl.when(s < NC)
        def _():
            first(s)

        @pl.when((s >= 2) & (s < NC + 2))
        def _():
            relay_x(s - 2)
            relay_c(s - 2)

        @pl.when((s >= 1) & (s < NC + 1))
        def _():
            second(s - 1)

        @pl.when((s >= 2) & (s < NC + 2))
        def _():
            relay_y(s - 2)

        @pl.when(s >= 3)
        def _():
            finish(s - 3)

        return 0

    lax.fori_loop(0, NC + 3, turn, 0)


def write_out(*refs):
    sems = refs[8]
    copies = [pltpu.make_async_copy(refs[i], refs[4 + i], sems.at[i]) for i in range(4)]
    for cp in copies:
        cp.start()
    for cp in copies:
        cp.wait()


def local(queries, point_order, keys, values, pair_counts, pair_keys, out_grad):
    hbm = pl.BlockSpec(memory_space=pl.ANY)
    vmem = pl.BlockSpec(memory_space=pltpu.VMEM)
    dma = pltpu.SemaphoreType.DMA
    w2 = 2 * HD
    out_shape = (
        jax.ShapeDtypeStruct((1, BS, D), BF),
        jax.ShapeDtypeStruct((1, BS, D), F32),
        jax.ShapeDtypeStruct((2, 8, D), F32),
        jax.ShapeDtypeStruct((2, 8, D), F32),
    )
    results = pl.pallas_call(
        kernel,
        out_shape=out_shape,
        in_specs=[hbm] * 7,
        out_specs=(vmem, vmem, vmem, vmem),
        scratch_shapes=[
            pltpu.VMEM((NP * BS, D), BF),
            pltpu.VMEM((1, NP * BS), jnp.int32),
            pltpu.VMEM((1, NP), jnp.int32),
            pltpu.VMEM((1, 256), jnp.int32),
            pltpu.VMEM((QS, D), BF),
            pltpu.VMEM((NM, BS, D), BF),
            pltpu.VMEM((2, 4, BS, D), BF),
            pltpu.VMEM((8, QS), F32),
            pltpu.VMEM((2, 2 * QS, w2), BF),
            pltpu.VMEM((2, 2 * QS, w2), BF),
            pltpu.VMEM((2 * KS, w2), BF),
            pltpu.VMEM((2 * KS, w2), BF),
            pltpu.VMEM((2, KS, 2 * QS), BF),
            pltpu.VMEM((2, KS, 2 * QS), BF),
            pltpu.VMEM((2, 8, PQ), F32),
            pltpu.VMEM((8, PQ), F32),
            pltpu.VMEM((NC, 2, 8, PQ), F32),
            pltpu.VMEM((NC, NM - 1, 2, 8, PQ), F32),
            pltpu.VMEM((NC, NX, NY, 2, BS, w2), BF),
            pltpu.VMEM((NC, 2, 2, BS, w2), BF),
            pltpu.VMEM((NC, 2, NY, 2, BS, w2), BF),
            pltpu.VMEM((NC, 2, BS, w2), F32),
            pltpu.VMEM((NC, 2, BS, w2), BF),
            pltpu.VMEM((NC, 2, BS, w2), BF),
            pltpu.VMEM((NC, 2, 2 * BS, w2), F32),
            pltpu.VMEM((NC, 2, 2 * BS, w2), BF),
            pltpu.VMEM((NC, 2, 2 * BS, w2), BF),
            pltpu.VMEM((NC // 2, NP, 4, 16, w2), BF),
            pltpu.VMEM((NC // 2, NP - 1, 4, 16, w2), BF),
            dma((6 + NM,)),
            dma((2, 2)),
            dma((2, NC)),
            dma((2, NC, 2)),
            dma((2, NC, 2)),
            dma((2, NC)),
            dma((2, NC)),
            dma((2, NC // 2)),
        ],
        compiler_params=pltpu.CompilerParams(
            collective_id=0, has_side_effects=True, vmem_limit_bytes=60 * 1024 * 1024
        ),
        name="sparse_attention",
    )(queries, point_order, keys, values, pair_counts, pair_keys, out_grad)
    return pl.pallas_call(
        write_out,
        out_shape=out_shape,
        in_specs=[vmem] * 4,
        out_specs=(hbm,) * 4,
        scratch_shapes=[dma((4,))],
        name="write_out",
    )(*results)


def solution(mesh):
    return jax.shard_map(
        local,
        mesh=mesh,
        in_specs=(
            P("pb", None),
            P("pb", None),
            P("ka", None, None),
            P("ka", None, None),
            P("pb", None),
            P("pb", None),
            P("pb", None, None),
        ),
        out_specs=(
            P(("pb", "ka"), None, None),
            P(("pb", "ka"), None, None),
            P("ka", "pb", None),
            P("ka", "pb", None),
        ),
        check_vma=False,
    )
```

```python
import functools
import math

import jax
import jax.numpy as jnp
from jax import lax
from jax.experimental import pallas as pl
from jax.experimental.pallas import tpu as pltpu
from jax.sharding import PartitionSpec as P

H = 8
HD = 64
D = 512
BS = 128
NP = 16
NX = 4
NY = 2
NM = NX * NY
NC = 4
QS = NM * BS
KS = 4 * BS
PQ = 2 * BS
SCALE = HD ** -0.5
C2 = SCALE * math.log2(math.e)
FAR = 1e30
MESH = pl.DeviceIdType.MESH
BF = jnp.bfloat16
F32 = jnp.float32

NN = (((1,), (0,)), ((), ()))
NT = (((1,), (1,)), ((), ()))
TN = (((0,), (0,)), ((), ()))


def dot(a, b, dims=NN):
    return lax.dot_general(a, b, dims, preferred_element_type=F32)


def kernel(
    queries,
    order,
    keys,
    values,
    counts,
    listing,
    out_grad,
    att_out,
    qg_out,
    kg_out,
    vg_out,
    qbuf,
    order_v,
    counts_v,
    listing_v,
    serial,
    og,
    kv,
    use,
    q_m,
    og_m,
    k_m,
    v_m,
    probs,
    dps,
    m_keep,
    d_keep,
    stat_own,
    stat_got,
    aq,
    x1_got,
    x2_got,
    y_keep,
    y_send,
    y_got,
    c_keep,
    c_send,
    c_got,
    z_send,
    z_got,
    load_sem,
    kv_sem,
    stat_sem,
    x1_sem,
    x2_sem,
    y_sem,
    c_sem,
    z_sem,
):
    pb = lax.axis_index("pb")
    ka = lax.axis_index("ka")
    core = lax.rem(ka, 2)
    chip = ka // 2
    xi = lax.rem(chip, NX)
    yi = chip // NX
    xr = lax.rem(xi + 1, NX)
    xl = lax.rem(xi + NX - 1, NX)
    xo = lax.rem(xi + 2, NX)
    yo = 1 - yi

    def at_ka(y, x, c):
        return {"ka": (y * NX + x) * 2 + c}

    right, left = at_ka(yi, xr, core), at_ka(yi, xl, core)
    across = at_ka(yo, xi, core)
    mate = {"ka": chip * 2 + (1 - core)}

    def peer(d):
        return {"ka": lax.rem(chip + d, NM) * 2 + core}

    def slab(d):
        return {"pb": lax.rem(pb + d, NP)}

    def send(src, dst, send_sem, recv_sem, device):
        return pltpu.make_async_remote_copy(
            src_ref=src, dst_ref=dst, send_sem=send_sem, recv_sem=recv_sem,
            device_id=device, device_id_type=MESH,
        )

    own2 = pl.ds(2 * core, 2)
    load_q = pltpu.make_async_copy(queries, qbuf, load_sem.at[0])
    load_small = [
        pltpu.make_async_copy(order, order_v, load_sem.at[3]),
        pltpu.make_async_copy(counts, counts_v, load_sem.at[4]),
        pltpu.make_async_copy(listing, listing_v, load_sem.at[5]),
    ]
    load_kv = [
        pltpu.make_async_copy(keys, kv.at[0, own2], load_sem.at[1]),
        pltpu.make_async_copy(values, kv.at[1, own2], load_sem.at[2]),
    ]
    load_og = [
        pltpu.make_async_copy(out_grad.at[2 * b + core], og.at[b], load_sem.at[6 + b])
        for b in range(NM)
    ]
    for cp in load_small + [load_q] + load_kv + load_og:
        cp.start()

    barrier = pltpu.get_barrier_semaphore()
    pl.semaphore_signal(barrier, inc=1, device_id=mate, device_id_type=MESH)

    def hello_ka(d, _):
        pl.semaphore_signal(barrier, inc=1, device_id=peer(d), device_id_type=MESH)
        return 0

    def hello_pb(d, _):
        pl.semaphore_signal(barrier, inc=1, device_id=slab(d), device_id_type=MESH)
        return 0

    lax.fori_loop(1, NM, hello_ka, 0)
    lax.fori_loop(1, NP, hello_pb, 0)

    for cp in load_small:
        cp.wait()

    cb = jnp.broadcast_to(counts_v[...].astype(F32), (16, 16))
    i0 = lax.broadcasted_iota(jnp.int32, (16, 16), 0)
    i1 = lax.broadcasted_iota(jnp.int32, (16, 16), 1)
    starts = jnp.sum(jnp.where(i1 < i0, cb, 0.0), axis=1, keepdims=True)
    sizes = jnp.sum(jnp.where(i1 == i0, cb, 0.0), axis=1, keepdims=True)
    slot = lax.broadcasted_iota(jnp.int32, (16, 256), 1).astype(F32)
    inside = jnp.where((slot >= starts) & (slot < starts + sizes), 1.0, 0.0)
    row = lax.broadcasted_iota(jnp.int32, (8, 256), 0) + 4 * chip
    named = jnp.where(jnp.broadcast_to(listing_v[...], (8, 256)) == row, 1.0, 0.0)
    joined = dot(named.astype(BF), inside.astype(BF), NT)
    e0 = lax.broadcasted_iota(jnp.int32, (16, QS), 0)
    e1 = lax.broadcasted_iota(jnp.int32, (16, QS), 1)
    spread = jnp.where(e0 == 2 * (e1 // BS) + core, 1.0, 0.0)
    use[...] = dot(joined.astype(BF), spread.astype(BF))

    load_q.wait()

    send_k = send(keys, kv.at[0, own2], kv_sem.at[0, 0], kv_sem.at[1, 0], mate)
    send_v = send(values, kv.at[1, own2], kv_sem.at[0, 1], kv_sem.at[1, 1], mate)

    def gather(t, _):
        @pl.when(t == 1)
        def _():
            pl.semaphore_wait(barrier, 1 + (NM - 1) + (NP - 1))
            send_k.start()
            send_v.start()

        picks = []
        for e in range(4):
            at = pl.multiple_of((8 * t + 2 * e + core) * BS, BS)
            column = jnp.broadcast_to(order_v[:, pl.ds(at, BS)], (BS, BS)).T
            lanes = lax.broadcasted_iota(jnp.int32, (BS, BS), 1)
            picks.append(jnp.concatenate(
                [jnp.where(column == lanes + n * BS, 1.0, 0.0).astype(BF) for n in range(16)], axis=1
            ))
        pick = jnp.concatenate(picks, axis=0)
        serial[pl.ds(pl.multiple_of(t * 4 * BS, 4 * BS), 4 * BS), :] = dot(pick, qbuf[...]).astype(BF)
        return 0

    lax.fori_loop(0, 2, gather, 0)
    for cp in load_kv + load_og:
        cp.wait()
    send_k.wait()
    send_v.wait()

    def lanes_of(hp):
        return pl.ds(pl.multiple_of(hp * 2 * HD, 2 * HD), 2 * HD)

    def split_heads(src, dst, n):
        low = lax.broadcasted_iota(jnp.int32, (n, 2 * HD), 1) < HD
        none = jnp.zeros((n, 2 * HD), BF)
        dst[:n] = jnp.where(low, src, none)
        dst[n:] = jnp.where(low, none, src)

    def columns(u):
        p, h = u // 2, u % 2
        return slice(h * QS + p * PQ, h * QS + (p + 1) * PQ)

    def first(hp):
        par = lax.rem(hp, 2)
        cols = lanes_of(hp)
        k2 = kv[0, :, :, cols].reshape(KS, 2 * HD)
        v2 = kv[1, :, :, cols].reshape(KS, 2 * HD)
        split_heads(serial[:, cols], q_m.at[par], QS)
        split_heads(og[:, :, cols].reshape(QS, 2 * HD), og_m.at[par], QS)

        def products(u):
            cc = columns(u)
            return dot(k2, q_m[par, cc, :], NT), dot(v2, og_m[par, cc, :], NT)

        def softmax(u, st, dp):
            p, h = u // 2, u % 2
            cc = columns(u)
            usable = use[0:4, p * PQ:(p + 1) * PQ] > 0.5
            m_raw = jnp.full((1, PQ), -FAR, F32)
            for kb in range(4):
                top = jnp.max(st[kb * BS:(kb + 1) * BS], axis=0, keepdims=True)
                m_raw = jnp.maximum(m_raw, jnp.where(usable[kb:kb + 1], top, -FAR))
            m = m_raw * C2
            total = jnp.zeros((BS, PQ), F32)
            weighted = jnp.zeros((BS, PQ), F32)
            for kb in range(4):
                ks = slice(kb * BS, (kb + 1) * BS)
                off = jnp.where(usable[kb:kb + 1], m, FAR)
                pr = jnp.exp2(st[ks] * C2 - off)
                total = total + pr
                weighted = weighted + pr * dp[ks]
                probs[par, ks, cc] = pr.astype(BF)
            dps[par, :, cc] = dp.astype(BF)
            total = jnp.maximum(jnp.sum(total, axis=0, keepdims=True), 0.5)
            weighted = jnp.sum(weighted, axis=0, keepdims=True)
            r = slice(u, u + 1)
            m_keep[par, r, :] = m
            stat_own[hp, 0, r, :] = m + jnp.log2(total)
            stat_own[hp, 1, r, :] = weighted / total

        ahead = products(0)
        for u in range(NM):
            now = ahead
            if u + 1 < NM:
                ahead = products(u + 1)
            softmax(u, *now)

        def share(d, _):
            send(stat_own.at[hp], stat_got.at[hp, d - 1], stat_sem.at[0, hp], stat_sem.at[1, hp], peer(d)).start()
            return 0

        lax.fori_loop(1, NM, share, 0)

    def stat_all(hp):
        return send(stat_got.at[hp], stat_got.at[hp], stat_sem.at[0, hp], stat_sem.at[1, hp], right)

    def second(hp):
        par = lax.rem(hp, 2)
        cols = lanes_of(hp)
        stat_all(hp).wait_recv()
        lse = [stat_own[hp, 0]] + [stat_got[hp, d, 0] for d in range(NM - 1)]
        dlt = [stat_own[hp, 1]] + [stat_got[hp, d, 1] for d in range(NM - 1)]
        top = functools.reduce(jnp.maximum, lse)
        ws = [jnp.exp2(v - top) for v in lse]
        total = functools.reduce(jnp.add, ws)
        delta_all = functools.reduce(jnp.add, [w * v for w, v in zip(ws, dlt)]) / total
        m_keep[par] = jnp.exp2(m_keep[par] - (top + jnp.log2(total)))
        d_keep[...] = delta_all
        split_heads(kv[0, :, :, cols].reshape(KS, 2 * HD), k_m, KS)
        split_heads(kv[1, :, :, cols].reshape(KS, 2 * HD), v_m, KS)

        for u in range(NM):
            probs[par, :, columns(u)] = (
                probs[par, :, columns(u)].astype(F32) * m_keep[par, u:u + 1, :]
            ).astype(BF)
        dv = dot(probs[par], og_m[par]).reshape(2, 2 * BS, 2 * HD)

        def scores_grad(u):
            cc = columns(u)
            dps[par, :, cc] = (
                probs[par, :, cc].astype(F32) * (dps[par, :, cc].astype(F32) - d_keep[u:u + 1, :])
            ).astype(BF)

        def outputs(p):
            att = jnp.zeros((PQ, 2 * HD), F32)
            dq = jnp.zeros((PQ, 2 * HD), F32)
            for h in range(2):
                cc = columns(2 * p + h)
                hk = slice(h * KS, (h + 1) * KS)
                att = att + dot(probs[par, :, cc], v_m[hk, :], TN)
                dq = dq + dot(dps[par, :, cc], k_m[hk, :], TN)
            att = att.astype(BF)
            dq = (dq * SCALE).astype(BF)
            for e in range(2):
                b = 2 * p + e
                x, y = b % NX, b // NX
                aq[hp, x, y, 0] = att[e * BS:(e + 1) * BS]
                aq[hp, x, y, 1] = dq[e * BS:(e + 1) * BS]

        for p in range(NM // 2):
            scores_grad(2 * p)
            scores_grad(2 * p + 1)
            if p > 0:
                outputs(p - 1)
        outputs(NM // 2 - 1)
        for cp in x1_copies(hp):
            cp.start()
        dk = (dot(dps[par], q_m[par]) * SCALE).reshape(2, 2 * BS, 2 * HD)
        mine = core == 0
        c_keep[hp, 0] = jnp.where(mine, dk[0], dk[1])
        c_keep[hp, 1] = jnp.where(mine, dv[0], dv[1])
        c_send[hp, 0] = jnp.where(mine, dk[1], dk[0]).astype(BF)
        c_send[hp, 1] = jnp.where(mine, dv[1], dv[0]).astype(BF)
        c_copy(hp).start()

    def x1_copies(hp):
        return (
            send(aq.at[hp, xo, 0], x1_got.at[hp, 0], x1_sem.at[0, hp, 0], x1_sem.at[1, hp, 0], right),
            send(aq.at[hp, xo, 1], x1_got.at[hp, 1], x1_sem.at[0, hp, 1], x1_sem.at[1, hp, 1], left),
        )

    def x2_copies(hp):
        return (
            send(aq.at[hp, xr], x2_got.at[hp, 0], x2_sem.at[0, hp, 0], x2_sem.at[1, hp, 0], right),
            send(aq.at[hp, xl], x2_got.at[hp, 1], x2_sem.at[0, hp, 1], x2_sem.at[1, hp, 1], left),
        )

    def y_copy(hp):
        return send(y_send.at[hp], y_got.at[hp], y_sem.at[0, hp], y_sem.at[1, hp], across)

    def c_copy(hp):
        return send(c_send.at[hp], c_got.at[hp], c_sem.at[0, hp], c_sem.at[1, hp], mate)

    def z_all(pair):
        return send(z_got.at[pair], z_got.at[pair], z_sem.at[0, pair], z_sem.at[1, pair], slab(1))

    def relay_x(hp):
        for cp in x1_copies(hp):
            cp.wait_recv()
        aq[hp, xr, 0] = (aq[hp, xr, 0].astype(F32) + x1_got[hp, 0].astype(F32)).astype(BF)
        aq[hp, xl, 1] = (aq[hp, xl, 1].astype(F32) + x1_got[hp, 1].astype(F32)).astype(BF)
        for cp in x2_copies(hp):
            cp.start()

    def relay_c(hp):
        c_copy(hp).wait_recv()
        pair = hp // 2
        for a in range(2):
            total = c_keep[hp, a] + c_got[hp, a].astype(F32)
            total = total.reshape(2, NP, 8, 2 * HD).transpose(1, 0, 2, 3)
            z_send[pair, :, 2 * lax.rem(hp, 2) + a] = total.reshape(NP, 16, 2 * HD).astype(BF)

        def share(d, _):
            send(
                z_send.at[pair, lax.rem(pb + d, NP)], z_got.at[pair, d - 1],
                z_sem.at[0, pair], z_sem.at[1, pair], slab(d),
            ).start()
            return 0

        @pl.when(lax.rem(hp, 2) == 1)
        def _():
            lax.fori_loop(1, NP, share, 0)

    def relay_y(hp):
        for cp in x2_copies(hp):
            cp.wait_recv()

        def total(y):
            return (
                aq[hp, xi, y].astype(F32)
                + x2_got[hp, 0, y].astype(F32)
                + x2_got[hp, 1, y].astype(F32)
            )

        y_send[hp] = total(yo).astype(BF)
        y_copy(hp).start()
        y_keep[hp] = total(yi)

    def finish(hp):
        cols = lanes_of(hp)
        y_copy(hp).wait_recv()
        both = y_keep[hp] + y_got[hp].astype(F32)
        att_out[0, :, cols] = both[0].astype(BF)
        qg_out[0, :, cols] = both[1]
        stat_all(hp).wait_send()
        for cp in x1_copies(hp) + x2_copies(hp):
            cp.wait_send()
        y_copy(hp).wait_send()
        c_copy(hp).wait_send()

        @pl.when(lax.rem(hp, 2) == 1)
        def _():
            pair = hp // 2
            z_all(pair).wait_recv()
            for q in range(2):
                cols = lanes_of(2 * pair + q)
                for a, out in ((0, kg_out), (1, vg_out)):
                    total = z_send[pair, pb, 2 * q + a].astype(F32)
                    for d in range(NP - 1):
                        total = total + z_got[pair, d, 2 * q + a].astype(F32)
                    out[:, :, cols] = total.reshape(2, 8, 2 * HD)
            z_all(pair).wait_send()

    def turn(s, _):
        @pl.when(s < NC)
        def _():
            first(s)

        @pl.when((s >= 2) & (s < NC + 2))
        def _():
            relay_x(s - 2)
            relay_c(s - 2)

        @pl.when((s >= 1) & (s < NC + 1))
        def _():
            second(s - 1)

        @pl.when((s >= 2) & (s < NC + 2))
        def _():
            relay_y(s - 2)

        @pl.when(s >= 3)
        def _():
            finish(s - 3)

        return 0

    lax.fori_loop(0, NC + 3, turn, 0)


def write_out(*refs):
    sems = refs[8]
    copies = [pltpu.make_async_copy(refs[i], refs[4 + i], sems.at[i]) for i in range(4)]
    for cp in copies:
        cp.start()
    for cp in copies:
        cp.wait()


def local(queries, point_order, keys, values, pair_counts, pair_keys, out_grad):
    hbm = pl.BlockSpec(memory_space=pl.ANY)
    vmem = pl.BlockSpec(memory_space=pltpu.VMEM)
    dma = pltpu.SemaphoreType.DMA
    w2 = 2 * HD
    out_shape = (
        jax.ShapeDtypeStruct((1, BS, D), BF),
        jax.ShapeDtypeStruct((1, BS, D), F32),
        jax.ShapeDtypeStruct((2, 8, D), F32),
        jax.ShapeDtypeStruct((2, 8, D), F32),
    )
    results = pl.pallas_call(
        kernel,
        out_shape=out_shape,
        in_specs=[hbm] * 7,
        out_specs=(vmem, vmem, vmem, vmem),
        scratch_shapes=[
            pltpu.VMEM((NP * BS, D), BF),
            pltpu.VMEM((1, NP * BS), jnp.int32),
            pltpu.VMEM((1, NP), jnp.int32),
            pltpu.VMEM((1, 256), jnp.int32),
            pltpu.VMEM((QS, D), BF),
            pltpu.VMEM((NM, BS, D), BF),
            pltpu.VMEM((2, 4, BS, D), BF),
            pltpu.VMEM((8, QS), F32),
            pltpu.VMEM((2, 2 * QS, w2), BF),
            pltpu.VMEM((2, 2 * QS, w2), BF),
            pltpu.VMEM((2 * KS, w2), BF),
            pltpu.VMEM((2 * KS, w2), BF),
            pltpu.VMEM((2, KS, 2 * QS), BF),
            pltpu.VMEM((2, KS, 2 * QS), BF),
            pltpu.VMEM((2, 8, PQ), F32),
            pltpu.VMEM((8, PQ), F32),
            pltpu.VMEM((NC, 2, 8, PQ), F32),
            pltpu.VMEM((NC, NM - 1, 2, 8, PQ), F32),
            pltpu.VMEM((NC, NX, NY, 2, BS, w2), BF),
            pltpu.VMEM((NC, 2, 2, BS, w2), BF),
            pltpu.VMEM((NC, 2, NY, 2, BS, w2), BF),
            pltpu.VMEM((NC, 2, BS, w2), F32),
            pltpu.VMEM((NC, 2, BS, w2), BF),
            pltpu.VMEM((NC, 2, BS, w2), BF),
            pltpu.VMEM((NC, 2, 2 * BS, w2), F32),
            pltpu.VMEM((NC, 2, 2 * BS, w2), BF),
            pltpu.VMEM((NC, 2, 2 * BS, w2), BF),
            pltpu.VMEM((NC // 2, NP, 4, 16, w2), BF),
            pltpu.VMEM((NC // 2, NP - 1, 4, 16, w2), BF),
            dma((6 + NM,)),
            dma((2, 2)),
            dma((2, NC)),
            dma((2, NC, 2)),
            dma((2, NC, 2)),
            dma((2, NC)),
            dma((2, NC)),
            dma((2, NC // 2)),
        ],
        compiler_params=pltpu.CompilerParams(
            collective_id=0, has_side_effects=True, vmem_limit_bytes=60 * 1024 * 1024
        ),
        name="sparse_attention",
    )(queries, point_order, keys, values, pair_counts, pair_keys, out_grad)
    return pl.pallas_call(
        write_out,
        out_shape=out_shape,
        in_specs=[vmem] * 4,
        out_specs=(hbm,) * 4,
        scratch_shapes=[dma((4,))],
        name="write_out",
    )(*results)


def solution(mesh):
    return jax.shard_map(
        local,
        mesh=mesh,
        in_specs=(
            P("pb", None),
            P("pb", None),
            P("ka", None, None),
            P("ka", None, None),
            P("pb", None),
            P("pb", None),
            P("pb", None, None),
        ),
        out_specs=(
            P(("pb", "ka"), None, None),
            P(("pb", "ka"), None, None),
            P("ka", "pb", None),
            P("ka", "pb", None),
        ),
        check_vma=False,
    )
```

```python
import functools
import math

import jax
import jax.numpy as jnp
from jax import lax
from jax.experimental import pallas as pl
from jax.experimental.pallas import tpu as pltpu
from jax.sharding import PartitionSpec as P

H = 8
HD = 64
D = 512
BS = 128
NP = 16
NX = 4
NY = 2
NM = NX * NY
NC = 4
QS = NM * BS
KS = 4 * BS
PQ = 2 * BS
SCALE = HD ** -0.5
C2 = SCALE * math.log2(math.e)
FAR = 1e30
MESH = pl.DeviceIdType.MESH
BF = jnp.bfloat16
F32 = jnp.float32

NN = (((1,), (0,)), ((), ()))
NT = (((1,), (1,)), ((), ()))
TN = (((0,), (0,)), ((), ()))


def dot(a, b, dims=NN):
    return lax.dot_general(a, b, dims, preferred_element_type=F32)


def kernel(
    queries,
    order,
    keys,
    values,
    counts,
    listing,
    out_grad,
    att_out,
    qg_out,
    kg_out,
    vg_out,
    qbuf,
    order_v,
    counts_v,
    listing_v,
    serial,
    og,
    kv,
    use,
    q_m,
    og_m,
    k_m,
    v_m,
    probs,
    dps,
    m_keep,
    d_keep,
    stat_own,
    stat_got,
    aq,
    x1_got,
    x2_got,
    y_keep,
    y_send,
    y_got,
    c_keep,
    c_send,
    c_got,
    z_send,
    z_got,
    load_sem,
    kv_sem,
    stat_sem,
    x1_sem,
    x2_sem,
    y_sem,
    c_sem,
    z_sem,
):
    pb = lax.axis_index("pb")
    ka = lax.axis_index("ka")
    core = lax.rem(ka, 2)
    chip = ka // 2
    xi = lax.rem(chip, NX)
    yi = chip // NX
    xr = lax.rem(xi + 1, NX)
    xl = lax.rem(xi + NX - 1, NX)
    xo = lax.rem(xi + 2, NX)
    yo = 1 - yi

    def at_ka(y, x, c):
        return {"ka": (y * NX + x) * 2 + c}

    right, left = at_ka(yi, xr, core), at_ka(yi, xl, core)
    across = at_ka(yo, xi, core)
    mate = {"ka": chip * 2 + (1 - core)}

    def peer(d):
        return {"ka": lax.rem(chip + d, NM) * 2 + core}

    def slab(d):
        return {"pb": lax.rem(pb + d, NP)}

    def send(src, dst, send_sem, recv_sem, device):
        return pltpu.make_async_remote_copy(
            src_ref=src, dst_ref=dst, send_sem=send_sem, recv_sem=recv_sem,
            device_id=device, device_id_type=MESH,
        )

    own2 = pl.ds(2 * core, 2)
    load_q = pltpu.make_async_copy(queries, qbuf, load_sem.at[0])
    load_small = [
        pltpu.make_async_copy(order, order_v, load_sem.at[3]),
        pltpu.make_async_copy(counts, counts_v, load_sem.at[4]),
        pltpu.make_async_copy(listing, listing_v, load_sem.at[5]),
    ]
    load_kv = [
        pltpu.make_async_copy(keys, kv.at[0, own2], load_sem.at[1]),
        pltpu.make_async_copy(values, kv.at[1, own2], load_sem.at[2]),
    ]
    load_og = [
        pltpu.make_async_copy(out_grad.at[2 * b + core], og.at[b], load_sem.at[6 + b])
        for b in range(NM)
    ]
    for cp in load_small + [load_q] + load_kv + load_og:
        cp.start()

    barrier = pltpu.get_barrier_semaphore()
    pl.semaphore_signal(barrier, inc=1, device_id=mate, device_id_type=MESH)

    def hello_ka(d, _):
        pl.semaphore_signal(barrier, inc=1, device_id=peer(d), device_id_type=MESH)
        return 0

    def hello_pb(d, _):
        pl.semaphore_signal(barrier, inc=1, device_id=slab(d), device_id_type=MESH)
        return 0

    lax.fori_loop(1, NM, hello_ka, 0)
    lax.fori_loop(1, NP, hello_pb, 0)

    for cp in load_small:
        cp.wait()

    cb = jnp.broadcast_to(counts_v[...].astype(F32), (16, 16))
    i0 = lax.broadcasted_iota(jnp.int32, (16, 16), 0)
    i1 = lax.broadcasted_iota(jnp.int32, (16, 16), 1)
    starts = jnp.sum(jnp.where(i1 < i0, cb, 0.0), axis=1, keepdims=True)
    sizes = jnp.sum(jnp.where(i1 == i0, cb, 0.0), axis=1, keepdims=True)
    slot = lax.broadcasted_iota(jnp.int32, (16, 256), 1).astype(F32)
    inside = jnp.where((slot >= starts) & (slot < starts + sizes), 1.0, 0.0)
    row = lax.broadcasted_iota(jnp.int32, (8, 256), 0) + 4 * chip
    named = jnp.where(jnp.broadcast_to(listing_v[...], (8, 256)) == row, 1.0, 0.0)
    joined = dot(named.astype(BF), inside.astype(BF), NT)
    e0 = lax.broadcasted_iota(jnp.int32, (16, QS), 0)
    e1 = lax.broadcasted_iota(jnp.int32, (16, QS), 1)
    spread = jnp.where(e0 == 2 * (e1 // BS) + core, 1.0, 0.0)
    use[...] = dot(joined.astype(BF), spread.astype(BF))

    load_q.wait()

    send_k = send(keys, kv.at[0, own2], kv_sem.at[0, 0], kv_sem.at[1, 0], mate)
    send_v = send(values, kv.at[1, own2], kv_sem.at[0, 1], kv_sem.at[1, 1], mate)

    def gather(t, _):
        @pl.when(t == 1)
        def _():
            pl.semaphore_wait(barrier, 1 + (NM - 1) + (NP - 1))
            send_k.start()
            send_v.start()

        picks = []
        for e in range(4):
            at = pl.multiple_of((8 * t + 2 * e + core) * BS, BS)
            column = jnp.broadcast_to(order_v[:, pl.ds(at, BS)], (BS, BS)).T
            lanes = lax.broadcasted_iota(jnp.int32, (BS, BS), 1)
            picks.append(jnp.concatenate(
                [jnp.where(column == lanes + n * BS, 1.0, 0.0).astype(BF) for n in range(16)], axis=1
            ))
        pick = jnp.concatenate(picks, axis=0)
        serial[pl.ds(pl.multiple_of(t * 4 * BS, 4 * BS), 4 * BS), :] = dot(pick, qbuf[...]).astype(BF)
        return 0

    lax.fori_loop(0, 2, gather, 0)
    for cp in load_kv + load_og:
        cp.wait()
    send_k.wait()
    send_v.wait()

    def lanes_of(hp):
        return pl.ds(pl.multiple_of(hp * 2 * HD, 2 * HD), 2 * HD)

    def split_heads(src, dst, n):
        low = lax.broadcasted_iota(jnp.int32, (n, 2 * HD), 1) < HD
        none = jnp.zeros((n, 2 * HD), BF)
        dst[:n] = jnp.where(low, src, none)
        dst[n:] = jnp.where(low, none, src)

    def columns(u):
        p, h = u // 2, u % 2
        return slice(h * QS + p * PQ, h * QS + (p + 1) * PQ)

    def first(hp):
        par = lax.rem(hp, 2)
        cols = lanes_of(hp)
        k2 = kv[0, :, :, cols].reshape(KS, 2 * HD)
        v2 = kv[1, :, :, cols].reshape(KS, 2 * HD)
        split_heads(serial[:, cols], q_m.at[par], QS)
        split_heads(og[:, :, cols].reshape(QS, 2 * HD), og_m.at[par], QS)

        def products(u):
            cc = columns(u)
            return dot(k2, q_m[par, cc, :], NT), dot(v2, og_m[par, cc, :], NT)

        def softmax(u, st, dp):
            p, h = u // 2, u % 2
            cc = columns(u)
            usable = use[0:4, p * PQ:(p + 1) * PQ] > 0.5
            m_raw = jnp.full((1, PQ), -FAR, F32)
            for kb in range(4):
                top = jnp.max(st[kb * BS:(kb + 1) * BS], axis=0, keepdims=True)
                m_raw = jnp.maximum(m_raw, jnp.where(usable[kb:kb + 1], top, -FAR))
            m = m_raw * C2
            total = jnp.zeros((BS, PQ), F32)
            weighted = jnp.zeros((BS, PQ), F32)
            for kb in range(4):
                ks = slice(kb * BS, (kb + 1) * BS)
                off = jnp.where(usable[kb:kb + 1], m, FAR)
                pr = jnp.exp2(st[ks] * C2 - off)
                total = total + pr
                weighted = weighted + pr * dp[ks]
                probs[par, ks, cc] = pr.astype(BF)
            dps[par, :, cc] = dp.astype(BF)
            total = jnp.maximum(jnp.sum(total, axis=0, keepdims=True), 0.5)
            weighted = jnp.sum(weighted, axis=0, keepdims=True)
            r = slice(u, u + 1)
            m_keep[par, r, :] = m
            stat_own[hp, 0, r, :] = m + jnp.log2(total)
            stat_own[hp, 1, r, :] = weighted / total

        ahead = products(0)
        for u in range(NM):
            now = ahead
            if u + 1 < NM:
                ahead = products(u + 1)
            softmax(u, *now)

        def share(d, _):
            send(stat_own.at[hp], stat_got.at[hp, d - 1], stat_sem.at[0, hp], stat_sem.at[1, hp], peer(d)).start()
            return 0

        lax.fori_loop(1, NM, share, 0)

    def stat_all(hp):
        return send(stat_got.at[hp], stat_got.at[hp], stat_sem.at[0, hp], stat_sem.at[1, hp], right)

    def second(hp):
        par = lax.rem(hp, 2)
        cols = lanes_of(hp)
        stat_all(hp).wait_recv()
        lse = [stat_own[hp, 0]] + [stat_got[hp, d, 0] for d in range(NM - 1)]
        dlt = [stat_own[hp, 1]] + [stat_got[hp, d, 1] for d in range(NM - 1)]
        top = functools.reduce(jnp.maximum, lse)
        ws = [jnp.exp2(v - top) for v in lse]
        total = functools.reduce(jnp.add, ws)
        delta_all = functools.reduce(jnp.add, [w * v for w, v in zip(ws, dlt)]) / total
        m_keep[par] = jnp.exp2(m_keep[par] - (top + jnp.log2(total)))
        d_keep[...] = delta_all
        split_heads(kv[0, :, :, cols].reshape(KS, 2 * HD), k_m, KS)
        split_heads(kv[1, :, :, cols].reshape(KS, 2 * HD), v_m, KS)

        for u in range(NM):
            probs[par, :, columns(u)] = (
                probs[par, :, columns(u)].astype(F32) * m_keep[par, u:u + 1, :]
            ).astype(BF)
        dv = dot(probs[par], og_m[par]).reshape(2, 2 * BS, 2 * HD)

        def scores_grad(u):
            cc = columns(u)
            dps[par, :, cc] = (
                probs[par, :, cc].astype(F32) * (dps[par, :, cc].astype(F32) - d_keep[u:u + 1, :])
            ).astype(BF)

        def outputs(p):
            att = jnp.zeros((PQ, 2 * HD), F32)
            dq = jnp.zeros((PQ, 2 * HD), F32)
            for h in range(2):
                cc = columns(2 * p + h)
                hk = slice(h * KS, (h + 1) * KS)
                att = att + dot(probs[par, :, cc], v_m[hk, :], TN)
                dq = dq + dot(dps[par, :, cc], k_m[hk, :], TN)
            att = att.astype(BF)
            dq = (dq * SCALE).astype(BF)
            for e in range(2):
                b = 2 * p + e
                x, y = b % NX, b // NX
                aq[hp, x, y, 0] = att[e * BS:(e + 1) * BS]
                aq[hp, x, y, 1] = dq[e * BS:(e + 1) * BS]

        for p in range(NM // 2):
            scores_grad(2 * p)
            scores_grad(2 * p + 1)
            if p > 0:
                outputs(p - 1)
        outputs(NM // 2 - 1)
        for cp in x1_copies(hp):
            cp.start()
        dk = (dot(dps[par], q_m[par]) * SCALE).reshape(2, 2 * BS, 2 * HD)
        mine = core == 0
        c_keep[hp, 0] = jnp.where(mine, dk[0], dk[1])
        c_keep[hp, 1] = jnp.where(mine, dv[0], dv[1])
        c_send[hp, 0] = jnp.where(mine, dk[1], dk[0]).astype(BF)
        c_send[hp, 1] = jnp.where(mine, dv[1], dv[0]).astype(BF)
        c_copy(hp).start()

    def x1_copies(hp):
        return (
            send(aq.at[hp, xo, 0], x1_got.at[hp, 0], x1_sem.at[0, hp, 0], x1_sem.at[1, hp, 0], right),
            send(aq.at[hp, xo, 1], x1_got.at[hp, 1], x1_sem.at[0, hp, 1], x1_sem.at[1, hp, 1], left),
        )

    def x2_copies(hp):
        return (
            send(aq.at[hp, xr], x2_got.at[hp, 0], x2_sem.at[0, hp, 0], x2_sem.at[1, hp, 0], right),
            send(aq.at[hp, xl], x2_got.at[hp, 1], x2_sem.at[0, hp, 1], x2_sem.at[1, hp, 1], left),
        )

    def y_copy(hp):
        return send(y_send.at[hp], y_got.at[hp], y_sem.at[0, hp], y_sem.at[1, hp], across)

    def c_copy(hp):
        return send(c_send.at[hp], c_got.at[hp], c_sem.at[0, hp], c_sem.at[1, hp], mate)

    def z_all(pair):
        return send(z_got.at[pair], z_got.at[pair], z_sem.at[0, pair], z_sem.at[1, pair], slab(1))

    def relay_x(hp):
        for cp in x1_copies(hp):
            cp.wait_recv()
        aq[hp, xr, 0] = (aq[hp, xr, 0].astype(F32) + x1_got[hp, 0].astype(F32)).astype(BF)
        aq[hp, xl, 1] = (aq[hp, xl, 1].astype(F32) + x1_got[hp, 1].astype(F32)).astype(BF)
        for cp in x2_copies(hp):
            cp.start()

    def relay_c(hp):
        c_copy(hp).wait_recv()
        pair = hp // 2
        for a in range(2):
            total = c_keep[hp, a] + c_got[hp, a].astype(F32)
            total = total.reshape(2, NP, 8, 2 * HD).transpose(1, 0, 2, 3)
            z_send[pair, :, 2 * lax.rem(hp, 2) + a] = total.reshape(NP, 16, 2 * HD).astype(BF)

        def share(d, _):
            send(
                z_send.at[pair, lax.rem(pb + d, NP)], z_got.at[pair, d - 1],
                z_sem.at[0, pair], z_sem.at[1, pair], slab(d),
            ).start()
            return 0

        @pl.when(lax.rem(hp, 2) == 1)
        def _():
            lax.fori_loop(1, NP, share, 0)

    def relay_y(hp):
        for cp in x2_copies(hp):
            cp.wait_recv()

        def total(y):
            return (
                aq[hp, xi, y].astype(F32)
                + x2_got[hp, 0, y].astype(F32)
                + x2_got[hp, 1, y].astype(F32)
            )

        y_send[hp] = total(yo).astype(BF)
        y_copy(hp).start()
        y_keep[hp] = total(yi)

    def finish(hp):
        cols = lanes_of(hp)
        y_copy(hp).wait_recv()
        both = y_keep[hp] + y_got[hp].astype(F32)
        att_out[0, :, cols] = both[0].astype(BF)
        qg_out[0, :, cols] = both[1]
        stat_all(hp).wait_send()
        for cp in x1_copies(hp) + x2_copies(hp):
            cp.wait_send()
        y_copy(hp).wait_send()
        c_copy(hp).wait_send()

        @pl.when(lax.rem(hp, 2) == 1)
        def _():
            pair = hp // 2
            z_all(pair).wait_recv()
            for q in range(2):
                cols = lanes_of(2 * pair + q)
                for a, out in ((0, kg_out), (1, vg_out)):
                    total = z_send[pair, pb, 2 * q + a].astype(F32)
                    for d in range(NP - 1):
                        total = total + z_got[pair, d, 2 * q + a].astype(F32)
                    out[:, :, cols] = total.reshape(2, 8, 2 * HD)
            z_all(pair).wait_send()

    def turn(s, _):
        @pl.when(s < NC)
        def _():
            first(s)

        @pl.when((s >= 1) & (s < NC + 1))
        def _():
            second(s - 1)

        @pl.when((s >= 2) & (s < NC + 2))
        def _():
            relay_x(s - 2)
            relay_c(s - 2)

        @pl.when((s >= 3) & (s < NC + 3))
        def _():
            relay_y(s - 3)

        @pl.when(s >= 4)
        def _():
            finish(s - 4)

        return 0

    lax.fori_loop(0, NC + 4, turn, 0)


def write_out(*refs):
    sems = refs[8]
    copies = [pltpu.make_async_copy(refs[i], refs[4 + i], sems.at[i]) for i in range(4)]
    for cp in copies:
        cp.start()
    for cp in copies:
        cp.wait()


def local(queries, point_order, keys, values, pair_counts, pair_keys, out_grad):
    hbm = pl.BlockSpec(memory_space=pl.ANY)
    vmem = pl.BlockSpec(memory_space=pltpu.VMEM)
    dma = pltpu.SemaphoreType.DMA
    w2 = 2 * HD
    out_shape = (
        jax.ShapeDtypeStruct((1, BS, D), BF),
        jax.ShapeDtypeStruct((1, BS, D), F32),
        jax.ShapeDtypeStruct((2, 8, D), F32),
        jax.ShapeDtypeStruct((2, 8, D), F32),
    )
    results = pl.pallas_call(
        kernel,
        out_shape=out_shape,
        in_specs=[hbm] * 7,
        out_specs=(vmem, vmem, vmem, vmem),
        scratch_shapes=[
            pltpu.VMEM((NP * BS, D), BF),
            pltpu.VMEM((1, NP * BS), jnp.int32),
            pltpu.VMEM((1, NP), jnp.int32),
            pltpu.VMEM((1, 256), jnp.int32),
            pltpu.VMEM((QS, D), BF),
            pltpu.VMEM((NM, BS, D), BF),
            pltpu.VMEM((2, 4, BS, D), BF),
            pltpu.VMEM((8, QS), F32),
            pltpu.VMEM((2, 2 * QS, w2), BF),
            pltpu.VMEM((2, 2 * QS, w2), BF),
            pltpu.VMEM((2 * KS, w2), BF),
            pltpu.VMEM((2 * KS, w2), BF),
            pltpu.VMEM((2, KS, 2 * QS), BF),
            pltpu.VMEM((2, KS, 2 * QS), BF),
            pltpu.VMEM((2, 8, PQ), F32),
            pltpu.VMEM((8, PQ), F32),
            pltpu.VMEM((NC, 2, 8, PQ), F32),
            pltpu.VMEM((NC, NM - 1, 2, 8, PQ), F32),
            pltpu.VMEM((NC, NX, NY, 2, BS, w2), BF),
            pltpu.VMEM((NC, 2, 2, BS, w2), BF),
            pltpu.VMEM((NC, 2, NY, 2, BS, w2), BF),
            pltpu.VMEM((NC, 2, BS, w2), F32),
            pltpu.VMEM((NC, 2, BS, w2), BF),
            pltpu.VMEM((NC, 2, BS, w2), BF),
            pltpu.VMEM((NC, 2, 2 * BS, w2), F32),
            pltpu.VMEM((NC, 2, 2 * BS, w2), BF),
            pltpu.VMEM((NC, 2, 2 * BS, w2), BF),
            pltpu.VMEM((NC // 2, NP, 4, 16, w2), BF),
            pltpu.VMEM((NC // 2, NP - 1, 4, 16, w2), BF),
            dma((6 + NM,)),
            dma((2, 2)),
            dma((2, NC)),
            dma((2, NC, 2)),
            dma((2, NC, 2)),
            dma((2, NC)),
            dma((2, NC)),
            dma((2, NC // 2)),
        ],
        compiler_params=pltpu.CompilerParams(
            collective_id=0, has_side_effects=True, vmem_limit_bytes=60 * 1024 * 1024
        ),
        name="sparse_attention",
    )(queries, point_order, keys, values, pair_counts, pair_keys, out_grad)
    return pl.pallas_call(
        write_out,
        out_shape=out_shape,
        in_specs=[vmem] * 4,
        out_specs=(hbm,) * 4,
        scratch_shapes=[dma((4,))],
        name="write_out",
    )(*results)


def solution(mesh):
    return jax.shard_map(
        local,
        mesh=mesh,
        in_specs=(
            P("pb", None),
            P("pb", None),
            P("ka", None, None),
            P("ka", None, None),
            P("pb", None),
            P("pb", None),
            P("pb", None, None),
        ),
        out_specs=(
            P(("pb", "ka"), None, None),
            P(("pb", "ka"), None, None),
            P("ka", "pb", None),
            P("ka", "pb", None),
        ),
        check_vma=False,
    )
```

```python
import functools
import math

import jax
import jax.numpy as jnp
from jax import lax
from jax.experimental import pallas as pl
from jax.experimental.pallas import tpu as pltpu
from jax.sharding import PartitionSpec as P

H = 8
HD = 64
D = 512
BS = 128
NP = 16
NX = 4
NY = 2
NM = NX * NY
NC = 4
QS = NM * BS
KS = 4 * BS
PQ = 2 * BS
SCALE = HD ** -0.5
C2 = SCALE * math.log2(math.e)
FAR = 1e30
MESH = pl.DeviceIdType.MESH
BF = jnp.bfloat16
F32 = jnp.float32

NN = (((1,), (0,)), ((), ()))
NT = (((1,), (1,)), ((), ()))
TN = (((0,), (0,)), ((), ()))


def dot(a, b, dims=NN):
    return lax.dot_general(a, b, dims, preferred_element_type=F32)


def kernel(
    queries,
    order,
    keys,
    values,
    counts,
    listing,
    out_grad,
    att_out,
    qg_out,
    kg_out,
    vg_out,
    qbuf,
    order_v,
    counts_v,
    listing_v,
    pick,
    serial,
    og,
    kv,
    use,
    q_m,
    og_m,
    k_m,
    v_m,
    probs,
    dps,
    m_keep,
    stat_own,
    stat_got,
    fin_got,
    aq,
    x1_got,
    x2_got,
    y_keep,
    y_send,
    y_got,
    c_keep,
    c_send,
    c_got,
    z_send,
    z_got,
    load_sem,
    kv_sem,
    stat_sem,
    fin_sem,
    x1_sem,
    x2_sem,
    y_sem,
    c_sem,
    z_sem,
):
    pb = lax.axis_index("pb")
    ka = lax.axis_index("ka")
    core = lax.rem(ka, 2)
    chip = ka // 2
    xi = lax.rem(chip, NX)
    yi = chip // NX
    xr = lax.rem(xi + 1, NX)
    xl = lax.rem(xi + NX - 1, NX)
    xo = lax.rem(xi + 2, NX)
    yo = 1 - yi

    def at_ka(y, x, c):
        return {"ka": (y * NX + x) * 2 + c}

    right, left = at_ka(yi, xr, core), at_ka(yi, xl, core)
    across = at_ka(yo, xi, core)
    mate = {"ka": chip * 2 + (1 - core)}

    def peer(d):
        return {"ka": lax.rem(chip + d, NM) * 2 + core}

    def slab(d):
        return {"pb": lax.rem(pb + d, NP)}

    def send(src, dst, send_sem, recv_sem, device):
        return pltpu.make_async_remote_copy(
            src_ref=src, dst_ref=dst, send_sem=send_sem, recv_sem=recv_sem,
            device_id=device, device_id_type=MESH,
        )

    own2 = pl.ds(2 * core, 2)
    load_q = pltpu.make_async_copy(queries, qbuf, load_sem.at[0])
    load_small = [
        pltpu.make_async_copy(order, order_v, load_sem.at[3]),
        pltpu.make_async_copy(counts, counts_v, load_sem.at[4]),
        pltpu.make_async_copy(listing, listing_v, load_sem.at[5]),
    ]
    load_kv = [
        pltpu.make_async_copy(keys, kv.at[0, own2], load_sem.at[1]),
        pltpu.make_async_copy(values, kv.at[1, own2], load_sem.at[2]),
    ]
    load_og = [
        pltpu.make_async_copy(out_grad.at[2 * b + core], og.at[b], load_sem.at[6 + b])
        for b in range(NM)
    ]
    for cp in load_small + [load_q] + load_kv + load_og:
        cp.start()

    barrier = pltpu.get_barrier_semaphore()
    pl.semaphore_signal(barrier, inc=1, device_id=mate, device_id_type=MESH)

    def hello_ka(d, _):
        pl.semaphore_signal(barrier, inc=1, device_id=peer(d), device_id_type=MESH)
        return 0

    def hello_pb(d, _):
        pl.semaphore_signal(barrier, inc=1, device_id=slab(d), device_id_type=MESH)
        return 0

    lax.fori_loop(1, NM, hello_ka, 0)
    lax.fori_loop(1, NP, hello_pb, 0)

    for cp in load_small:
        cp.wait()

    cb = jnp.broadcast_to(counts_v[...].astype(F32), (16, 16))
    i0 = lax.broadcasted_iota(jnp.int32, (16, 16), 0)
    i1 = lax.broadcasted_iota(jnp.int32, (16, 16), 1)
    starts = jnp.sum(jnp.where(i1 < i0, cb, 0.0), axis=1, keepdims=True)
    sizes = jnp.sum(jnp.where(i1 == i0, cb, 0.0), axis=1, keepdims=True)
    slot = lax.broadcasted_iota(jnp.int32, (16, 256), 1).astype(F32)
    inside = jnp.where((slot >= starts) & (slot < starts + sizes), 1.0, 0.0)
    row = lax.broadcasted_iota(jnp.int32, (8, 256), 0) + 4 * chip
    named = jnp.where(jnp.broadcast_to(listing_v[...], (8, 256)) == row, 1.0, 0.0)
    joined = dot(named.astype(BF), inside.astype(BF), NT)
    e0 = lax.broadcasted_iota(jnp.int32, (16, QS), 0)
    e1 = lax.broadcasted_iota(jnp.int32, (16, QS), 1)
    spread = jnp.where(e0 == 2 * (e1 // BS) + core, 1.0, 0.0)
    use[...] = dot(joined.astype(BF), spread.astype(BF))

    half = D // 2

    def mark(b, _):
        at = pl.multiple_of((2 * b + core) * BS, BS)
        column = jnp.broadcast_to(order_v[:, pl.ds(at, BS)], (BS, BS)).T
        lanes = lax.broadcasted_iota(jnp.int32, (BS, BS), 1)
        rows = pl.ds(pl.multiple_of(b * BS, BS), BS)
        for n in range(16):
            pick[rows, n * BS:(n + 1) * BS] = jnp.where(column == lanes + n * BS, 1.0, 0.0).astype(BF)
        return 0

    lax.fori_loop(0, NM, mark, 0)
    load_q.wait()

    def gather(c):
        def part(t, _):
            rows = pl.ds(pl.multiple_of(t * 4 * BS, 4 * BS), 4 * BS)
            lanes = pl.ds(pl.multiple_of(c * half, half), half)
            serial[rows, lanes] = dot(pick[rows, :], qbuf[:, lanes]).astype(BF)
            return 0

        lax.fori_loop(0, 2, part, 0)

    send_k = send(keys, kv.at[0, own2], kv_sem.at[0, 0], kv_sem.at[1, 0], mate)
    send_v = send(values, kv.at[1, own2], kv_sem.at[0, 1], kv_sem.at[1, 1], mate)
    pl.semaphore_wait(barrier, 1 + (NM - 1) + (NP - 1))
    send_k.start()
    send_v.start()
    gather(0)
    for cp in load_kv + load_og:
        cp.wait()
    send_k.wait()
    send_v.wait()

    def lanes_of(hp):
        return pl.ds(pl.multiple_of(hp * 2 * HD, 2 * HD), 2 * HD)

    def split_heads(src, dst, n):
        low = lax.broadcasted_iota(jnp.int32, (n, 2 * HD), 1) < HD
        none = jnp.zeros((n, 2 * HD), BF)
        dst[:n] = jnp.where(low, src, none)
        dst[n:] = jnp.where(low, none, src)

    def columns(u):
        p, h = u // 2, u % 2
        return slice(h * QS + p * PQ, h * QS + (p + 1) * PQ)

    def first(hp):
        par = lax.rem(hp, 2)
        cols = lanes_of(hp)
        k2 = kv[0, :, :, cols].reshape(KS, 2 * HD)
        v2 = kv[1, :, :, cols].reshape(KS, 2 * HD)
        split_heads(serial[:, cols], q_m.at[par], QS)
        split_heads(og[:, :, cols].reshape(QS, 2 * HD), og_m.at[par], QS)

        def products(u):
            cc = columns(u)
            return dot(k2, q_m[par, cc, :], NT), dot(v2, og_m[par, cc, :], NT)

        def softmax(u, st, dp):
            p, h = u // 2, u % 2
            cc = columns(u)
            usable = use[0:4, p * PQ:(p + 1) * PQ] > 0.5
            m_raw = jnp.full((1, PQ), -FAR, F32)
            for kb in range(4):
                top = jnp.max(st[kb * BS:(kb + 1) * BS], axis=0, keepdims=True)
                m_raw = jnp.maximum(m_raw, jnp.where(usable[kb:kb + 1], top, -FAR))
            m = m_raw * C2
            total = jnp.zeros((BS, PQ), F32)
            weighted = jnp.zeros((BS, PQ), F32)
            for kb in range(4):
                ks = slice(kb * BS, (kb + 1) * BS)
                off = jnp.where(usable[kb:kb + 1], m, FAR)
                pr = jnp.exp2(st[ks] * C2 - off)
                total = total + pr
                weighted = weighted + pr * dp[ks]
                probs[par, ks, cc] = pr.astype(BF)
            dps[par, :, cc] = dp.astype(BF)
            total = jnp.maximum(jnp.sum(total, axis=0, keepdims=True), 0.5)
            weighted = jnp.sum(weighted, axis=0, keepdims=True)
            r = slice(u, u + 1)
            m_keep[par, r, :] = m
            lse = m + jnp.log2(total)
            delta = weighted / total
            for e in range(2):
                stat_own[hp, 2 * p + e, h:h + 1, :] = lse[:, e * BS:(e + 1) * BS]
                stat_own[hp, 2 * p + e, 2 + h:3 + h, :] = delta[:, e * BS:(e + 1) * BS]

        ahead = products(0)
        for u in range(NM):
            now = ahead
            if u + 1 < NM:
                ahead = products(u + 1)
            softmax(u, *now)

        def share(d, _):
            send(
                stat_own.at[hp, lax.rem(chip + d, NM)], stat_got.at[hp, d - 1],
                stat_sem.at[0, hp], stat_sem.at[1, hp], peer(d),
            ).start()
            return 0

        lax.fori_loop(1, NM, share, 0)

    def stat_all(hp):
        return send(stat_got.at[hp], stat_got.at[hp], stat_sem.at[0, hp], stat_sem.at[1, hp], right)

    def fin_all(hp):
        got = fin_got.at[hp, pl.ds(0, NM - 1)]
        return send(got, got, fin_sem.at[0, hp], fin_sem.at[1, hp], right)

    def combine(hp):
        stat_all(hp).wait_recv()
        own = stat_own[hp, chip]
        parts = [own] + [stat_got[hp, d] for d in range(NM - 1)]
        lse = [v[0:2] for v in parts]
        top = functools.reduce(jnp.maximum, lse)
        ws = [jnp.exp2(v - top) for v in lse]
        total = functools.reduce(jnp.add, ws)
        delta = functools.reduce(jnp.add, [w * v[2:4] for w, v in zip(ws, parts)]) / total
        fin_got[hp, NM - 1, 0:2] = top + jnp.log2(total)
        fin_got[hp, NM - 1, 2:4] = delta

        def share(d, _):
            send(
                fin_got.at[hp, NM - 1], fin_got.at[hp, d - 1],
                fin_sem.at[0, hp], fin_sem.at[1, hp], peer(d),
            ).start()
            return 0

        lax.fori_loop(1, NM, share, 0)

    def fin_row(hp, p, row):
        return jnp.concatenate(
            [fin_got[hp, lax.rem(chip - (2 * p + e) + 2 * NM - 1, NM), row:row + 1, :] for e in range(2)], axis=1
        )

    def second(hp):
        par = lax.rem(hp, 2)
        cols = lanes_of(hp)
        fin_all(hp).wait_recv()
        split_heads(kv[0, :, :, cols].reshape(KS, 2 * HD), k_m, KS)
        split_heads(kv[1, :, :, cols].reshape(KS, 2 * HD), v_m, KS)

        for u in range(NM):
            w = jnp.exp2(m_keep[par, u:u + 1, :] - fin_row(hp, u // 2, u % 2))
            probs[par, :, columns(u)] = (probs[par, :, columns(u)].astype(F32) * w).astype(BF)
        hand_over(hp, 1, dot(probs[par], og_m[par]))

        @pl.when(hp >= 1)
        def _():
            relay_x(hp - 1)

        def query_side(p, x0, y):
            att = jnp.zeros((PQ, 2 * HD), F32)
            dq = jnp.zeros((PQ, 2 * HD), F32)
            for h in range(2):
                cc = pl.ds(pl.multiple_of(h * QS + p * PQ, PQ), PQ)
                hk = slice(h * KS, (h + 1) * KS)
                qb = probs[par, :, cc]
                ds = (qb.astype(F32) * (dps[par, :, cc].astype(F32) - fin_row(hp, p, 2 + h))).astype(BF)
                dps[par, :, cc] = ds
                att = att + dot(qb, v_m[hk, :], TN)
                dq = dq + dot(ds, k_m[hk, :], TN)
            att = att.astype(BF)
            dq = (dq * SCALE).astype(BF)
            for e in range(2):
                aq[hp, x0 + e, y, 0] = att[e * BS:(e + 1) * BS]
                aq[hp, x0 + e, y, 1] = dq[e * BS:(e + 1) * BS]

        far = 1 - xi // 2
        for y in range(NY):
            query_side(2 * y + far, 2 * far, y)
        for cp in x1_copies(hp):
            cp.start()
        for y in range(NY):
            query_side(2 * y + 1 - far, 2 * (1 - far), y)
        hand_over(hp, 0, dot(dps[par], q_m[par]) * SCALE)

    def hand_over(hp, kind, grad):
        grad = grad.reshape(2, 2 * BS, 2 * HD)
        mine = core == 0
        c_keep[hp, kind] = jnp.where(mine, grad[0], grad[1])
        c_send[hp, kind] = jnp.where(mine, grad[1], grad[0]).astype(BF)
        c_copy(hp, kind).start()

    def x1_copies(hp):
        return (
            send(aq.at[hp, xo, 0], x1_got.at[hp, 0], x1_sem.at[0, hp, 0], x1_sem.at[1, hp, 0], right),
            send(aq.at[hp, xo, 1], x1_got.at[hp, 1], x1_sem.at[0, hp, 1], x1_sem.at[1, hp, 1], left),
        )

    def x2_copies(hp):
        return (
            send(aq.at[hp, xr], x2_got.at[hp, 0], x2_sem.at[0, hp, 0], x2_sem.at[1, hp, 0], right),
            send(aq.at[hp, xl], x2_got.at[hp, 1], x2_sem.at[0, hp, 1], x2_sem.at[1, hp, 1], left),
        )

    def y_copy(hp):
        return send(y_send.at[hp], y_got.at[hp], y_sem.at[0, hp], y_sem.at[1, hp], across)

    def c_copy(hp, kind):
        return send(c_send.at[hp, kind], c_got.at[hp, kind], c_sem.at[0, hp, kind], c_sem.at[1, hp, kind], mate)

    def z_all(hp):
        return send(z_got.at[hp], z_got.at[hp], z_sem.at[0, hp], z_sem.at[1, hp], slab(1))

    def relay_x(hp):
        for cp in x1_copies(hp):
            cp.wait_recv()
        aq[hp, xr, 0] = (aq[hp, xr, 0].astype(F32) + x1_got[hp, 0].astype(F32)).astype(BF)
        aq[hp, xl, 1] = (aq[hp, xl, 1].astype(F32) + x1_got[hp, 1].astype(F32)).astype(BF)
        for cp in x2_copies(hp):
            cp.start()

    def relay_c(hp):
        for a in range(2):
            c_copy(hp, a).wait_recv()
            total = c_keep[hp, a] + c_got[hp, a].astype(F32)
            total = total.reshape(2, NP, 8, 2 * HD).transpose(1, 0, 2, 3)
            z_send[hp, :, a] = total.reshape(NP, 16, 2 * HD).astype(BF)

        def share(d, _):
            send(
                z_send.at[hp, lax.rem(pb + d, NP)], z_got.at[hp, d - 1],
                z_sem.at[0, hp], z_sem.at[1, hp], slab(d),
            ).start()
            return 0

        lax.fori_loop(1, NP, share, 0)

    def relay_y(hp):
        for cp in x2_copies(hp):
            cp.wait_recv()

        def total(y):
            return (
                aq[hp, xi, y].astype(F32)
                + x2_got[hp, 0, y].astype(F32)
                + x2_got[hp, 1, y].astype(F32)
            )

        y_send[hp] = total(yo).astype(BF)
        y_copy(hp).start()
        y_keep[hp] = total(yi)

    def finish(hp):
        cols = lanes_of(hp)
        y_copy(hp).wait_recv()
        both = y_keep[hp] + y_got[hp].astype(F32)
        att_out[0, :, cols] = both[0].astype(BF)
        qg_out[0, :, cols] = both[1]
        z_all(hp).wait_recv()
        for a, out in ((0, kg_out), (1, vg_out)):
            total = z_send[hp, pb, a].astype(F32)
            for d in range(NP - 1):
                total = total + z_got[hp, d, a].astype(F32)
            out[:, :, cols] = total.reshape(2, 8, 2 * HD)
        stat_all(hp).wait_send()
        fin_all(hp).wait_send()
        for cp in x1_copies(hp) + x2_copies(hp):
            cp.wait_send()
        y_copy(hp).wait_send()
        for kind in range(2):
            c_copy(hp, kind).wait_send()
        z_all(hp).wait_send()

    def turn(s, _):
        @pl.when(s < NC)
        def _():
            first(s)

        @pl.when(s == 0)
        def _():
            gather(1)

        @pl.when((s >= 3) & (s < NC + 3))
        def _():
            relay_y(s - 3)

        @pl.when((s >= 1) & (s <= NC))
        def _():
            second(s - 1)

        @pl.when(s == NC + 1)
        def _():
            relay_x(NC - 1)

        @pl.when((s >= 2) & (s < NC + 2))
        def _():
            relay_c(s - 2)

        @pl.when(s < NC)
        def _():
            combine(s)

        @pl.when(s >= 4)
        def _():
            finish(s - 4)

        return 0

    lax.fori_loop(0, NC + 4, turn, 0)


def write_out(*refs):
    sems = refs[8]
    copies = [pltpu.make_async_copy(refs[i], refs[4 + i], sems.at[i]) for i in range(4)]
    for cp in copies:
        cp.start()
    for cp in copies:
        cp.wait()


def local(queries, point_order, keys, values, pair_counts, pair_keys, out_grad):
    hbm = pl.BlockSpec(memory_space=pl.ANY)
    vmem = pl.BlockSpec(memory_space=pltpu.VMEM)
    dma = pltpu.SemaphoreType.DMA
    w2 = 2 * HD
    out_shape = (
        jax.ShapeDtypeStruct((1, BS, D), BF),
        jax.ShapeDtypeStruct((1, BS, D), F32),
        jax.ShapeDtypeStruct((2, 8, D), F32),
        jax.ShapeDtypeStruct((2, 8, D), F32),
    )
    results = pl.pallas_call(
        kernel,
        out_shape=out_shape,
        in_specs=[hbm] * 7,
        out_specs=(vmem, vmem, vmem, vmem),
        scratch_shapes=[
            pltpu.VMEM((NP * BS, D), BF),
            pltpu.VMEM((1, NP * BS), jnp.int32),
            pltpu.VMEM((1, NP), jnp.int32),
            pltpu.VMEM((1, 256), jnp.int32),
            pltpu.VMEM((QS, NP * BS), BF),
            pltpu.VMEM((QS, D), BF),
            pltpu.VMEM((NM, BS, D), BF),
            pltpu.VMEM((2, 4, BS, D), BF),
            pltpu.VMEM((8, QS), F32),
            pltpu.VMEM((2, 2 * QS, w2), BF),
            pltpu.VMEM((2, 2 * QS, w2), BF),
            pltpu.VMEM((2 * KS, w2), BF),
            pltpu.VMEM((2 * KS, w2), BF),
            pltpu.VMEM((2, KS, 2 * QS), BF),
            pltpu.VMEM((2, KS, 2 * QS), BF),
            pltpu.VMEM((2, 8, PQ), F32),
            pltpu.VMEM((NC, NM, 4, BS), F32),
            pltpu.VMEM((NC, NM - 1, 4, BS), F32),
            pltpu.VMEM((NC, NM, 4, BS), F32),
            pltpu.VMEM((NC, NX, NY, 2, BS, w2), BF),
            pltpu.VMEM((NC, 2, 2, BS, w2), BF),
            pltpu.VMEM((NC, 2, NY, 2, BS, w2), BF),
            pltpu.VMEM((NC, 2, BS, w2), F32),
            pltpu.VMEM((NC, 2, BS, w2), BF),
            pltpu.VMEM((NC, 2, BS, w2), BF),
            pltpu.VMEM((NC, 2, 2 * BS, w2), F32),
            pltpu.VMEM((NC, 2, 2 * BS, w2), BF),
            pltpu.VMEM((NC, 2, 2 * BS, w2), BF),
            pltpu.VMEM((NC, NP, 2, 16, w2), BF),
            pltpu.VMEM((NC, NP - 1, 2, 16, w2), BF),
            dma((6 + NM,)),
            dma((2, 2)),
            dma((2, NC)),
            dma((2, NC)),
            dma((2, NC, 2)),
            dma((2, NC, 2)),
            dma((2, NC)),
            dma((2, NC, 2)),
            dma((2, NC)),
        ],
        compiler_params=pltpu.CompilerParams(
            collective_id=0, has_side_effects=True, vmem_limit_bytes=60 * 1024 * 1024
        ),
        name="sparse_attention",
    )(queries, point_order, keys, values, pair_counts, pair_keys, out_grad)
    return pl.pallas_call(
        write_out,
        out_shape=out_shape,
        in_specs=[vmem] * 4,
        out_specs=(hbm,) * 4,
        scratch_shapes=[dma((4,))],
        name="write_out",
    )(*results)


def solution(mesh):
    return jax.shard_map(
        local,
        mesh=mesh,
        in_specs=(
            P("pb", None),
            P("pb", None),
            P("ka", None, None),
            P("ka", None, None),
            P("pb", None),
            P("pb", None),
            P("pb", None, None),
        ),
        out_specs=(
            P(("pb", "ka"), None, None),
            P(("pb", "ka"), None, None),
            P("ka", "pb", None),
            P("ka", "pb", None),
        ),
        check_vma=False,
    )
```

```python
import functools
import math

import jax
import jax.numpy as jnp
from jax import lax
from jax.experimental import pallas as pl
from jax.experimental.pallas import tpu as pltpu
from jax.sharding import PartitionSpec as P

H = 8
HD = 64
D = 512
BS = 128
NP = 16
NX = 4
NY = 2
NM = NX * NY
NC = 4
QS = NM * BS
KS = 4 * BS
PQ = 2 * BS
SCALE = HD ** -0.5
C2 = SCALE * math.log2(math.e)
FAR = 1e30
MESH = pl.DeviceIdType.MESH
BF = jnp.bfloat16
F32 = jnp.float32

NN = (((1,), (0,)), ((), ()))
NT = (((1,), (1,)), ((), ()))
TN = (((0,), (0,)), ((), ()))


def dot(a, b, dims=NN):
    return lax.dot_general(a, b, dims, preferred_element_type=F32)


def kernel(
    queries,
    order,
    keys,
    values,
    counts,
    listing,
    out_grad,
    att_out,
    qg_out,
    kg_out,
    vg_out,
    qbuf,
    order_v,
    counts_v,
    listing_v,
    serial,
    og,
    kv,
    use,
    q_m,
    og_m,
    k_m,
    v_m,
    probs,
    dps,
    m_keep,
    d_keep,
    stat_own,
    stat_got,
    aq,
    x1_got,
    x2_got,
    y_keep,
    y_send,
    y_got,
    c_keep,
    c_send,
    c_got,
    z_send,
    z_got,
    load_sem,
    kv_sem,
    stat_sem,
    x1_sem,
    x2_sem,
    y_sem,
    c_sem,
    z_sem,
):
    pb = lax.axis_index("pb")
    ka = lax.axis_index("ka")
    core = lax.rem(ka, 2)
    chip = ka // 2
    xi = lax.rem(chip, NX)
    yi = chip // NX
    xr = lax.rem(xi + 1, NX)
    xl = lax.rem(xi + NX - 1, NX)
    xo = lax.rem(xi + 2, NX)
    yo = 1 - yi

    def at_ka(y, x, c):
        return {"ka": (y * NX + x) * 2 + c}

    right, left = at_ka(yi, xr, core), at_ka(yi, xl, core)
    across = at_ka(yo, xi, core)
    mate = {"ka": chip * 2 + (1 - core)}

    def peer(d):
        return {"ka": lax.rem(chip + d, NM) * 2 + core}

    def slab(d):
        return {"pb": lax.rem(pb + d, NP)}

    def send(src, dst, send_sem, recv_sem, device):
        return pltpu.make_async_remote_copy(
            src_ref=src, dst_ref=dst, send_sem=send_sem, recv_sem=recv_sem,
            device_id=device, device_id_type=MESH,
        )

    own2 = pl.ds(2 * core, 2)
    load_q = pltpu.make_async_copy(queries, qbuf, load_sem.at[0])
    load_small = [
        pltpu.make_async_copy(order, order_v, load_sem.at[3]),
        pltpu.make_async_copy(counts, counts_v, load_sem.at[4]),
        pltpu.make_async_copy(listing, listing_v, load_sem.at[5]),
    ]
    load_kv = [
        pltpu.make_async_copy(keys, kv.at[0, own2], load_sem.at[1]),
        pltpu.make_async_copy(values, kv.at[1, own2], load_sem.at[2]),
    ]
    load_og = [
        pltpu.make_async_copy(out_grad.at[2 * b + core], og.at[b], load_sem.at[6 + b])
        for b in range(NM)
    ]
    for cp in load_small + [load_q] + load_kv + load_og:
        cp.start()

    barrier = pltpu.get_barrier_semaphore()
    pl.semaphore_signal(barrier, inc=1, device_id=mate, device_id_type=MESH)

    def hello_ka(d, _):
        pl.semaphore_signal(barrier, inc=1, device_id=peer(d), device_id_type=MESH)
        return 0

    def hello_pb(d, _):
        pl.semaphore_signal(barrier, inc=1, device_id=slab(d), device_id_type=MESH)
        return 0

    lax.fori_loop(1, NM, hello_ka, 0)
    lax.fori_loop(1, NP, hello_pb, 0)

    for cp in load_small:
        cp.wait()

    cb = jnp.broadcast_to(counts_v[...].astype(F32), (16, 16))
    i0 = lax.broadcasted_iota(jnp.int32, (16, 16), 0)
    i1 = lax.broadcasted_iota(jnp.int32, (16, 16), 1)
    starts = jnp.sum(jnp.where(i1 < i0, cb, 0.0), axis=1, keepdims=True)
    sizes = jnp.sum(jnp.where(i1 == i0, cb, 0.0), axis=1, keepdims=True)
    slot = lax.broadcasted_iota(jnp.int32, (16, 256), 1).astype(F32)
    inside = jnp.where((slot >= starts) & (slot < starts + sizes), 1.0, 0.0)
    row = lax.broadcasted_iota(jnp.int32, (8, 256), 0) + 4 * chip
    named = jnp.where(jnp.broadcast_to(listing_v[...], (8, 256)) == row, 1.0, 0.0)
    joined = dot(named.astype(BF), inside.astype(BF), NT)
    e0 = lax.broadcasted_iota(jnp.int32, (16, QS), 0)
    e1 = lax.broadcasted_iota(jnp.int32, (16, QS), 1)
    spread = jnp.where(e0 == 2 * (e1 // BS) + core, 1.0, 0.0)
    use[...] = dot(joined.astype(BF), spread.astype(BF))

    load_q.wait()

    send_k = send(keys, kv.at[0, own2], kv_sem.at[0, 0], kv_sem.at[1, 0], mate)
    send_v = send(values, kv.at[1, own2], kv_sem.at[0, 1], kv_sem.at[1, 1], mate)

    def gather(t, _):
        @pl.when(t == 1)
        def _():
            pl.semaphore_wait(barrier, 1 + (NM - 1) + (NP - 1))
            send_k.start()
            send_v.start()

        picks = []
        for e in range(4):
            at = pl.multiple_of((8 * t + 2 * e + core) * BS, BS)
            column = jnp.broadcast_to(order_v[:, pl.ds(at, BS)], (BS, BS)).T
            lanes = lax.broadcasted_iota(jnp.int32, (BS, BS), 1)
            picks.append(jnp.concatenate(
                [jnp.where(column == lanes + n * BS, 1.0, 0.0).astype(BF) for n in range(16)], axis=1
            ))
        pick = jnp.concatenate(picks, axis=0)
        serial[pl.ds(pl.multiple_of(t * 4 * BS, 4 * BS), 4 * BS), :] = dot(pick, qbuf[...]).astype(BF)
        return 0

    lax.fori_loop(0, 2, gather, 0)
    for cp in load_kv + load_og:
        cp.wait()
    send_k.wait()
    send_v.wait()

    def lanes_of(hp):
        return pl.ds(pl.multiple_of(hp * 2 * HD, 2 * HD), 2 * HD)

    def split_heads(src, dst, n):
        low = lax.broadcasted_iota(jnp.int32, (n, 2 * HD), 1) < HD
        none = jnp.zeros((n, 2 * HD), BF)
        dst[:n] = jnp.where(low, src, none)
        dst[n:] = jnp.where(low, none, src)

    def columns(u):
        p, h = u // 2, u % 2
        return slice(h * QS + p * PQ, h * QS + (p + 1) * PQ)

    def first(hp):
        par = lax.rem(hp, 2)
        cols = lanes_of(hp)
        k2 = kv[0, :, :, cols].reshape(KS, 2 * HD)
        v2 = kv[1, :, :, cols].reshape(KS, 2 * HD)
        split_heads(serial[:, cols], q_m.at[par], QS)
        split_heads(og[:, :, cols].reshape(QS, 2 * HD), og_m.at[par], QS)

        def products(u):
            cc = columns(u)
            return dot(k2, q_m[par, cc, :], NT), dot(v2, og_m[par, cc, :], NT)

        def softmax(u, st, dp):
            p, h = u // 2, u % 2
            cc = columns(u)
            usable = use[0:4, p * PQ:(p + 1) * PQ] > 0.5
            m_raw = jnp.full((1, PQ), -FAR, F32)
            for kb in range(4):
                top = jnp.max(st[kb * BS:(kb + 1) * BS], axis=0, keepdims=True)
                m_raw = jnp.maximum(m_raw, jnp.where(usable[kb:kb + 1], top, -FAR))
            m = m_raw * C2
            total = jnp.zeros((BS, PQ), F32)
            weighted = jnp.zeros((BS, PQ), F32)
            for kb in range(4):
                ks = slice(kb * BS, (kb + 1) * BS)
                off = jnp.where(usable[kb:kb + 1], m, FAR)
                pr = jnp.exp2(st[ks] * C2 - off)
                total = total + pr
                weighted = weighted + pr * dp[ks]
                probs[par, ks, cc] = pr.astype(BF)
            dps[par, :, cc] = dp.astype(BF)
            total = jnp.maximum(jnp.sum(total, axis=0, keepdims=True), 0.5)
            weighted = jnp.sum(weighted, axis=0, keepdims=True)
            r = slice(u, u + 1)
            m_keep[par, r, :] = m
            stat_own[hp, 0, r, :] = m + jnp.log2(total)
            stat_own[hp, 1, r, :] = weighted / total

        ahead = products(0)
        for u in range(NM):
            now = ahead
            if u + 1 < NM:
                ahead = products(u + 1)
            softmax(u, *now)

        def share(d, _):
            send(stat_own.at[hp], stat_got.at[hp, d - 1], stat_sem.at[0, hp], stat_sem.at[1, hp], peer(d)).start()
            return 0

        lax.fori_loop(1, NM, share, 0)

    def stat_all(hp):
        return send(stat_got.at[hp], stat_got.at[hp], stat_sem.at[0, hp], stat_sem.at[1, hp], right)

    def second(hp):
        par = lax.rem(hp, 2)
        cols = lanes_of(hp)
        stat_all(hp).wait_recv()
        lse = [stat_own[hp, 0]] + [stat_got[hp, d, 0] for d in range(NM - 1)]
        dlt = [stat_own[hp, 1]] + [stat_got[hp, d, 1] for d in range(NM - 1)]
        top = functools.reduce(jnp.maximum, lse)
        ws = [jnp.exp2(v - top) for v in lse]
        total = functools.reduce(jnp.add, ws)
        delta_all = functools.reduce(jnp.add, [w * v for w, v in zip(ws, dlt)]) / total
        m_keep[par] = jnp.exp2(m_keep[par] - (top + jnp.log2(total)))
        d_keep[...] = delta_all
        split_heads(kv[0, :, :, cols].reshape(KS, 2 * HD), k_m, KS)
        split_heads(kv[1, :, :, cols].reshape(KS, 2 * HD), v_m, KS)

        for u in range(NM):
            probs[par, :, columns(u)] = (
                probs[par, :, columns(u)].astype(F32) * m_keep[par, u:u + 1, :]
            ).astype(BF)

        @pl.when(hp >= 1)
        def _():
            relay_x(hp - 1)

        def query_side(p, x0, y):
            att = jnp.zeros((PQ, 2 * HD), F32)
            dq = jnp.zeros((PQ, 2 * HD), F32)
            for h in range(2):
                cc = pl.ds(pl.multiple_of(h * QS + p * PQ, PQ), PQ)
                hk = slice(h * KS, (h + 1) * KS)
                qb = probs[par, :, cc]
                ds = (
                    qb.astype(F32) * (dps[par, :, cc].astype(F32) - d_keep[pl.ds(2 * p + h, 1), :])
                ).astype(BF)
                dps[par, :, cc] = ds
                att = att + dot(qb, v_m[hk, :], TN)
                dq = dq + dot(ds, k_m[hk, :], TN)
            att = att.astype(BF)
            dq = (dq * SCALE).astype(BF)
            for e in range(2):
                aq[hp, x0 + e, y, 0] = att[e * BS:(e + 1) * BS]
                aq[hp, x0 + e, y, 1] = dq[e * BS:(e + 1) * BS]

        far = 1 - xi // 2
        for y in range(NY):
            query_side(2 * y + far, 2 * far, y)
        for cp in x1_copies(hp):
            cp.start()
        for y in range(NY):
            query_side(2 * y + 1 - far, 2 * (1 - far), y)
        dk = (dot(dps[par], q_m[par]) * SCALE).reshape(2, 2 * BS, 2 * HD)
        dv = dot(probs[par], og_m[par]).reshape(2, 2 * BS, 2 * HD)
        mine = core == 0
        c_keep[hp, 0] = jnp.where(mine, dk[0], dk[1])
        c_keep[hp, 1] = jnp.where(mine, dv[0], dv[1])
        c_send[hp, 0] = jnp.where(mine, dk[1], dk[0]).astype(BF)
        c_send[hp, 1] = jnp.where(mine, dv[1], dv[0]).astype(BF)
        c_copy(hp).start()

    def x1_copies(hp):
        return (
            send(aq.at[hp, xo, 0], x1_got.at[hp, 0], x1_sem.at[0, hp, 0], x1_sem.at[1, hp, 0], right),
            send(aq.at[hp, xo, 1], x1_got.at[hp, 1], x1_sem.at[0, hp, 1], x1_sem.at[1, hp, 1], left),
        )

    def x2_copies(hp):
        return (
            send(aq.at[hp, xr], x2_got.at[hp, 0], x2_sem.at[0, hp, 0], x2_sem.at[1, hp, 0], right),
            send(aq.at[hp, xl], x2_got.at[hp, 1], x2_sem.at[0, hp, 1], x2_sem.at[1, hp, 1], left),
        )

    def y_copy(hp):
        return send(y_send.at[hp], y_got.at[hp], y_sem.at[0, hp], y_sem.at[1, hp], across)

    def c_copy(hp):
        return send(c_send.at[hp], c_got.at[hp], c_sem.at[0, hp], c_sem.at[1, hp], mate)

    def z_all(pair):
        return send(z_got.at[pair], z_got.at[pair], z_sem.at[0, pair], z_sem.at[1, pair], slab(1))

    def relay_x(hp):
        for cp in x1_copies(hp):
            cp.wait_recv()
        aq[hp, xr, 0] = (aq[hp, xr, 0].astype(F32) + x1_got[hp, 0].astype(F32)).astype(BF)
        aq[hp, xl, 1] = (aq[hp, xl, 1].astype(F32) + x1_got[hp, 1].astype(F32)).astype(BF)
        for cp in x2_copies(hp):
            cp.start()

    def relay_c(hp):
        c_copy(hp).wait_recv()
        pair = hp // 2
        for a in range(2):
            total = c_keep[hp, a] + c_got[hp, a].astype(F32)
            total = total.reshape(2, NP, 8, 2 * HD).transpose(1, 0, 2, 3)
            z_send[pair, :, 2 * lax.rem(hp, 2) + a] = total.reshape(NP, 16, 2 * HD).astype(BF)

        def share(d, _):
            send(
                z_send.at[pair, lax.rem(pb + d, NP)], z_got.at[pair, d - 1],
                z_sem.at[0, pair], z_sem.at[1, pair], slab(d),
            ).start()
            return 0

        @pl.when(lax.rem(hp, 2) == 1)
        def _():
            lax.fori_loop(1, NP, share, 0)

    def relay_y(hp):
        for cp in x2_copies(hp):
            cp.wait_recv()

        def total(y):
            return (
                aq[hp, xi, y].astype(F32)
                + x2_got[hp, 0, y].astype(F32)
                + x2_got[hp, 1, y].astype(F32)
            )

        y_send[hp] = total(yo).astype(BF)
        y_copy(hp).start()
        y_keep[hp] = total(yi)

    def finish(hp):
        cols = lanes_of(hp)
        y_copy(hp).wait_recv()
        both = y_keep[hp] + y_got[hp].astype(F32)
        att_out[0, :, cols] = both[0].astype(BF)
        qg_out[0, :, cols] = both[1]
        stat_all(hp).wait_send()
        for cp in x1_copies(hp) + x2_copies(hp):
            cp.wait_send()
        y_copy(hp).wait_send()
        c_copy(hp).wait_send()

        @pl.when(lax.rem(hp, 2) == 1)
        def _():
            pair = hp // 2
            z_all(pair).wait_recv()
            for q in range(2):
                cols = lanes_of(2 * pair + q)
                for a, out in ((0, kg_out), (1, vg_out)):
                    total = z_send[pair, pb, 2 * q + a].astype(F32)
                    for d in range(NP - 1):
                        total = total + z_got[pair, d, 2 * q + a].astype(F32)
                    out[:, :, cols] = total.reshape(2, 8, 2 * HD)
            z_all(pair).wait_send()

    def turn(s, _):
        @pl.when(s < NC)
        def _():
            first(s)

        @pl.when((s >= 3) & (s < NC + 3))
        def _():
            relay_y(s - 3)

        @pl.when((s >= 1) & (s <= NC))
        def _():
            second(s - 1)

        @pl.when(s == NC + 1)
        def _():
            relay_x(NC - 1)

        @pl.when((s >= 2) & (s < NC + 2))
        def _():
            relay_c(s - 2)

        @pl.when(s >= 4)
        def _():
            finish(s - 4)

        return 0

    lax.fori_loop(0, NC + 4, turn, 0)


def write_out(*refs):
    sems = refs[8]
    copies = [pltpu.make_async_copy(refs[i], refs[4 + i], sems.at[i]) for i in range(4)]
    for cp in copies:
        cp.start()
    for cp in copies:
        cp.wait()


def local(queries, point_order, keys, values, pair_counts, pair_keys, out_grad):
    hbm = pl.BlockSpec(memory_space=pl.ANY)
    vmem = pl.BlockSpec(memory_space=pltpu.VMEM)
    dma = pltpu.SemaphoreType.DMA
    w2 = 2 * HD
    out_shape = (
        jax.ShapeDtypeStruct((1, BS, D), BF),
        jax.ShapeDtypeStruct((1, BS, D), F32),
        jax.ShapeDtypeStruct((2, 8, D), F32),
        jax.ShapeDtypeStruct((2, 8, D), F32),
    )
    results = pl.pallas_call(
        kernel,
        out_shape=out_shape,
        in_specs=[hbm] * 7,
        out_specs=(vmem, vmem, vmem, vmem),
        scratch_shapes=[
            pltpu.VMEM((NP * BS, D), BF),
            pltpu.VMEM((1, NP * BS), jnp.int32),
            pltpu.VMEM((1, NP), jnp.int32),
            pltpu.VMEM((1, 256), jnp.int32),
            pltpu.VMEM((QS, D), BF),
            pltpu.VMEM((NM, BS, D), BF),
            pltpu.VMEM((2, 4, BS, D), BF),
            pltpu.VMEM((8, QS), F32),
            pltpu.VMEM((2, 2 * QS, w2), BF),
            pltpu.VMEM((2, 2 * QS, w2), BF),
            pltpu.VMEM((2 * KS, w2), BF),
            pltpu.VMEM((2 * KS, w2), BF),
            pltpu.VMEM((2, KS, 2 * QS), BF),
            pltpu.VMEM((2, KS, 2 * QS), BF),
            pltpu.VMEM((2, 8, PQ), F32),
            pltpu.VMEM((8, PQ), F32),
            pltpu.VMEM((NC, 2, 8, PQ), F32),
            pltpu.VMEM((NC, NM - 1, 2, 8, PQ), F32),
            pltpu.VMEM((NC, NX, NY, 2, BS, w2), BF),
            pltpu.VMEM((NC, 2, 2, BS, w2), BF),
            pltpu.VMEM((NC, 2, NY, 2, BS, w2), BF),
            pltpu.VMEM((NC, 2, BS, w2), F32),
            pltpu.VMEM((NC, 2, BS, w2), BF),
            pltpu.VMEM((NC, 2, BS, w2), BF),
            pltpu.VMEM((NC, 2, 2 * BS, w2), F32),
            pltpu.VMEM((NC, 2, 2 * BS, w2), BF),
            pltpu.VMEM((NC, 2, 2 * BS, w2), BF),
            pltpu.VMEM((NC // 2, NP, 4, 16, w2), BF),
            pltpu.VMEM((NC // 2, NP - 1, 4, 16, w2), BF),
            dma((6 + NM,)),
            dma((2, 2)),
            dma((2, NC)),
            dma((2, NC, 2)),
            dma((2, NC, 2)),
            dma((2, NC)),
            dma((2, NC)),
            dma((2, NC // 2)),
        ],
        compiler_params=pltpu.CompilerParams(
            collective_id=0, has_side_effects=True, vmem_limit_bytes=60 * 1024 * 1024
        ),
        name="sparse_attention",
    )(queries, point_order, keys, values, pair_counts, pair_keys, out_grad)
    return pl.pallas_call(
        write_out,
        out_shape=out_shape,
        in_specs=[vmem] * 4,
        out_specs=(hbm,) * 4,
        scratch_shapes=[dma((4,))],
        name="write_out",
    )(*results)


def solution(mesh):
    return jax.shard_map(
        local,
        mesh=mesh,
        in_specs=(
            P("pb", None),
            P("pb", None),
            P("ka", None, None),
            P("ka", None, None),
            P("pb", None),
            P("pb", None),
            P("pb", None, None),
        ),
        out_specs=(
            P(("pb", "ka"), None, None),
            P(("pb", "ka"), None, None),
            P("ka", "pb", None),
            P("ka", "pb", None),
        ),
        check_vma=False,
    )
```

```python
import functools
import math

import jax
import jax.numpy as jnp
from jax import lax
from jax.experimental import pallas as pl
from jax.experimental.pallas import tpu as pltpu
from jax.sharding import PartitionSpec as P

H = 8
HD = 64
D = 512
BS = 128
NP = 16
NX = 4
NY = 2
NM = NX * NY
NC = 4
QS = NM * BS
KS = 4 * BS
PQ = 2 * BS
SCALE = HD ** -0.5
C2 = SCALE * math.log2(math.e)
FAR = 1e30
MESH = pl.DeviceIdType.MESH
BF = jnp.bfloat16
F32 = jnp.float32

NN = (((1,), (0,)), ((), ()))
NT = (((1,), (1,)), ((), ()))
TN = (((0,), (0,)), ((), ()))


def dot(a, b, dims=NN):
    return lax.dot_general(a, b, dims, preferred_element_type=F32)


def kernel(
    queries,
    order,
    keys,
    values,
    counts,
    listing,
    out_grad,
    att_out,
    qg_out,
    kg_out,
    vg_out,
    qbuf,
    order_v,
    counts_v,
    listing_v,
    serial,
    og,
    kv,
    use,
    q_m,
    og_m,
    k_m,
    v_m,
    probs,
    dps,
    m_keep,
    d_keep,
    stat_own,
    stat_got,
    aq,
    x1_got,
    x2_got,
    y_keep,
    y_send,
    y_got,
    c_keep,
    c_send,
    c_got,
    z_send,
    z_got,
    load_sem,
    kv_sem,
    stat_sem,
    x1_sem,
    x2_sem,
    y_sem,
    c_sem,
    z_sem,
):
    pb = lax.axis_index("pb")
    ka = lax.axis_index("ka")
    core = lax.rem(ka, 2)
    chip = ka // 2
    xi = lax.rem(chip, NX)
    yi = chip // NX
    xr = lax.rem(xi + 1, NX)
    xl = lax.rem(xi + NX - 1, NX)
    xo = lax.rem(xi + 2, NX)
    yo = 1 - yi

    def at_ka(y, x, c):
        return {"ka": (y * NX + x) * 2 + c}

    right, left = at_ka(yi, xr, core), at_ka(yi, xl, core)
    across = at_ka(yo, xi, core)
    mate = {"ka": chip * 2 + (1 - core)}

    def peer(d):
        return {"ka": lax.rem(chip + d, NM) * 2 + core}

    def slab(d):
        return {"pb": lax.rem(pb + d, NP)}

    def send(src, dst, send_sem, recv_sem, device):
        return pltpu.make_async_remote_copy(
            src_ref=src, dst_ref=dst, send_sem=send_sem, recv_sem=recv_sem,
            device_id=device, device_id_type=MESH,
        )

    own2 = pl.ds(2 * core, 2)
    load_q = pltpu.make_async_copy(queries, qbuf, load_sem.at[0])
    load_small = [
        pltpu.make_async_copy(order, order_v, load_sem.at[3]),
        pltpu.make_async_copy(counts, counts_v, load_sem.at[4]),
        pltpu.make_async_copy(listing, listing_v, load_sem.at[5]),
    ]
    load_kv = [
        pltpu.make_async_copy(keys, kv.at[0, own2], load_sem.at[1]),
        pltpu.make_async_copy(values, kv.at[1, own2], load_sem.at[2]),
    ]
    load_og = [
        pltpu.make_async_copy(out_grad.at[2 * b + core], og.at[b], load_sem.at[6 + b])
        for b in range(NM)
    ]
    for cp in load_small + [load_q] + load_kv + load_og:
        cp.start()

    barrier = pltpu.get_barrier_semaphore()
    pl.semaphore_signal(barrier, inc=1, device_id=mate, device_id_type=MESH)

    def hello_ka(d, _):
        pl.semaphore_signal(barrier, inc=1, device_id=peer(d), device_id_type=MESH)
        return 0

    def hello_pb(d, _):
        pl.semaphore_signal(barrier, inc=1, device_id=slab(d), device_id_type=MESH)
        return 0

    lax.fori_loop(1, NM, hello_ka, 0)
    lax.fori_loop(1, NP, hello_pb, 0)

    for cp in load_small:
        cp.wait()

    cb = jnp.broadcast_to(counts_v[...].astype(F32), (16, 16))
    i0 = lax.broadcasted_iota(jnp.int32, (16, 16), 0)
    i1 = lax.broadcasted_iota(jnp.int32, (16, 16), 1)
    starts = jnp.sum(jnp.where(i1 < i0, cb, 0.0), axis=1, keepdims=True)
    sizes = jnp.sum(jnp.where(i1 == i0, cb, 0.0), axis=1, keepdims=True)
    slot = lax.broadcasted_iota(jnp.int32, (16, 256), 1).astype(F32)
    inside = jnp.where((slot >= starts) & (slot < starts + sizes), 1.0, 0.0)
    row = lax.broadcasted_iota(jnp.int32, (8, 256), 0) + 4 * chip
    named = jnp.where(jnp.broadcast_to(listing_v[...], (8, 256)) == row, 1.0, 0.0)
    joined = dot(named.astype(BF), inside.astype(BF), NT)
    e0 = lax.broadcasted_iota(jnp.int32, (16, QS), 0)
    e1 = lax.broadcasted_iota(jnp.int32, (16, QS), 1)
    spread = jnp.where(e0 == 2 * (e1 // BS) + core, 1.0, 0.0)
    use[...] = dot(joined.astype(BF), spread.astype(BF))

    load_q.wait()

    send_k = send(keys, kv.at[0, own2], kv_sem.at[0, 0], kv_sem.at[1, 0], mate)
    send_v = send(values, kv.at[1, own2], kv_sem.at[0, 1], kv_sem.at[1, 1], mate)

    def gather(t, _):
        @pl.when(t == 1)
        def _():
            pl.semaphore_wait(barrier, 1 + (NM - 1) + (NP - 1))
            send_k.start()
            send_v.start()

        picks = []
        for e in range(4):
            at = pl.multiple_of((8 * t + 2 * e + core) * BS, BS)
            column = jnp.broadcast_to(order_v[:, pl.ds(at, BS)], (BS, BS)).T
            lanes = lax.broadcasted_iota(jnp.int32, (BS, BS), 1)
            picks.append(jnp.concatenate(
                [jnp.where(column == lanes + n * BS, 1.0, 0.0).astype(BF) for n in range(16)], axis=1
            ))
        pick = jnp.concatenate(picks, axis=0)
        serial[pl.ds(pl.multiple_of(t * 4 * BS, 4 * BS), 4 * BS), :] = dot(pick, qbuf[...]).astype(BF)
        return 0

    lax.fori_loop(0, 2, gather, 0)
    for cp in load_kv + load_og:
        cp.wait()
    send_k.wait()
    send_v.wait()

    def lanes_of(hp):
        return pl.ds(pl.multiple_of(hp * 2 * HD, 2 * HD), 2 * HD)

    def split_heads(src, dst, n):
        low = lax.broadcasted_iota(jnp.int32, (n, 2 * HD), 1) < HD
        none = jnp.zeros((n, 2 * HD), BF)
        dst[:n] = jnp.where(low, src, none)
        dst[n:] = jnp.where(low, none, src)

    def columns(p, h):
        return pl.ds(pl.multiple_of(h * QS + p * PQ, PQ), PQ)

    def first(hp):
        par = lax.rem(hp, 2)
        cols = lanes_of(hp)
        k2 = kv[0, :, :, cols].reshape(KS, 2 * HD)
        v2 = kv[1, :, :, cols].reshape(KS, 2 * HD)
        split_heads(serial[:, cols], q_m.at[par], QS)
        split_heads(og[:, :, cols].reshape(QS, 2 * HD), og_m.at[par], QS)

        def softmax(p, h):
            cc = columns(p, h)
            st = dot(k2, q_m[par, cc, :], NT)
            dp = dot(v2, og_m[par, cc, :], NT)
            usable = use[0:4, columns(p, 0)] > 0.5
            m_raw = jnp.full((1, PQ), -FAR, F32)
            for kb in range(4):
                top = jnp.max(st[kb * BS:(kb + 1) * BS], axis=0, keepdims=True)
                m_raw = jnp.maximum(m_raw, jnp.where(usable[kb:kb + 1], top, -FAR))
            m = m_raw * C2
            total = jnp.zeros((BS, PQ), F32)
            weighted = jnp.zeros((BS, PQ), F32)
            for kb in range(4):
                ks = slice(kb * BS, (kb + 1) * BS)
                off = jnp.where(usable[kb:kb + 1], m, FAR)
                pr = jnp.exp2(st[ks] * C2 - off)
                total = total + pr
                weighted = weighted + pr * dp[ks]
                probs[par, ks, cc] = pr.astype(BF)
            dps[par, :, cc] = dp.astype(BF)
            total = jnp.maximum(jnp.sum(total, axis=0, keepdims=True), 0.5)
            weighted = jnp.sum(weighted, axis=0, keepdims=True)
            r = pl.ds(2 * p + h, 1)
            m_keep[par, r, :] = m
            stat_own[hp, 0, r, :] = m + jnp.log2(total)
            stat_own[hp, 1, r, :] = weighted / total

        def steps(y, _):
            for i in range(2):
                for h in range(2):
                    softmax(2 * y + i, h)
            return 0

        lax.fori_loop(0, NY, steps, 0)

        def share(d, _):
            send(stat_own.at[hp], stat_got.at[hp, d - 1], stat_sem.at[0, hp], stat_sem.at[1, hp], peer(d)).start()
            return 0

        lax.fori_loop(1, NM, share, 0)

    def stat_all(hp):
        return send(stat_got.at[hp], stat_got.at[hp], stat_sem.at[0, hp], stat_sem.at[1, hp], right)

    def second(hp):
        par = lax.rem(hp, 2)
        cols = lanes_of(hp)
        stat_all(hp).wait_recv()
        lse = [stat_own[hp, 0]] + [stat_got[hp, d, 0] for d in range(NM - 1)]
        dlt = [stat_own[hp, 1]] + [stat_got[hp, d, 1] for d in range(NM - 1)]
        top = functools.reduce(jnp.maximum, lse)
        ws = [jnp.exp2(v - top) for v in lse]
        total = functools.reduce(jnp.add, ws)
        delta_all = functools.reduce(jnp.add, [w * v for w, v in zip(ws, dlt)]) / total
        m_keep[par] = jnp.exp2(m_keep[par] - (top + jnp.log2(total)))
        d_keep[...] = delta_all
        split_heads(kv[0, :, :, cols].reshape(KS, 2 * HD), k_m, KS)
        split_heads(kv[1, :, :, cols].reshape(KS, 2 * HD), v_m, KS)

        def steps(y, _):
            for i in range(2):
                p = 2 * y + i
                att = jnp.zeros((PQ, 2 * HD), F32)
                dq = jnp.zeros((PQ, 2 * HD), F32)
                for h in range(2):
                    cc = columns(p, h)
                    hk = slice(h * KS, (h + 1) * KS)
                    r = pl.ds(2 * p + h, 1)
                    qf = probs[par, :, cc].astype(F32) * m_keep[par, r, :]
                    qb = qf.astype(BF)
                    ds = (qf * (dps[par, :, cc].astype(F32) - d_keep[r, :])).astype(BF)
                    probs[par, :, cc] = qb
                    dps[par, :, cc] = ds
                    att = att + dot(qb, v_m[hk, :], TN)
                    dq = dq + dot(ds, k_m[hk, :], TN)
                att = att.astype(BF)
                dq = (dq * SCALE).astype(BF)
                for e in range(2):
                    aq[hp, 2 * i + e, y, 0] = att[e * BS:(e + 1) * BS]
                    aq[hp, 2 * i + e, y, 1] = dq[e * BS:(e + 1) * BS]
            return 0

        lax.fori_loop(0, NY, steps, 0)
        for cp in x1_copies(hp):
            cp.start()
        dk = (dot(dps[par], q_m[par]) * SCALE).reshape(2, 2 * BS, 2 * HD)
        dv = dot(probs[par], og_m[par]).reshape(2, 2 * BS, 2 * HD)
        mine = core == 0
        c_keep[hp, 0] = jnp.where(mine, dk[0], dk[1])
        c_keep[hp, 1] = jnp.where(mine, dv[0], dv[1])
        c_send[hp, 0] = jnp.where(mine, dk[1], dk[0]).astype(BF)
        c_send[hp, 1] = jnp.where(mine, dv[1], dv[0]).astype(BF)
        c_copy(hp).start()

    def x1_copies(hp):
        return (
            send(aq.at[hp, xo, 0], x1_got.at[hp, 0], x1_sem.at[0, hp, 0], x1_sem.at[1, hp, 0], right),
            send(aq.at[hp, xo, 1], x1_got.at[hp, 1], x1_sem.at[0, hp, 1], x1_sem.at[1, hp, 1], left),
        )

    def x2_copies(hp):
        return (
            send(aq.at[hp, xr], x2_got.at[hp, 0], x2_sem.at[0, hp, 0], x2_sem.at[1, hp, 0], right),
            send(aq.at[hp, xl], x2_got.at[hp, 1], x2_sem.at[0, hp, 1], x2_sem.at[1, hp, 1], left),
        )

    def y_copy(hp):
        return send(y_send.at[hp], y_got.at[hp], y_sem.at[0, hp], y_sem.at[1, hp], across)

    def c_copy(hp):
        return send(c_send.at[hp], c_got.at[hp], c_sem.at[0, hp], c_sem.at[1, hp], mate)

    def z_all(pair):
        return send(z_got.at[pair], z_got.at[pair], z_sem.at[0, pair], z_sem.at[1, pair], slab(1))

    def relay_x(hp):
        for cp in x1_copies(hp):
            cp.wait_recv()
        aq[hp, xr, 0] = (aq[hp, xr, 0].astype(F32) + x1_got[hp, 0].astype(F32)).astype(BF)
        aq[hp, xl, 1] = (aq[hp, xl, 1].astype(F32) + x1_got[hp, 1].astype(F32)).astype(BF)
        for cp in x2_copies(hp):
            cp.start()

    def relay_c(hp):
        c_copy(hp).wait_recv()
        pair = hp // 2
        for a in range(2):
            total = c_keep[hp, a] + c_got[hp, a].astype(F32)
            total = total.reshape(2, NP, 8, 2 * HD).transpose(1, 0, 2, 3)
            z_send[pair, :, 2 * lax.rem(hp, 2) + a] = total.reshape(NP, 16, 2 * HD).astype(BF)

        def share(d, _):
            send(
                z_send.at[pair, lax.rem(pb + d, NP)], z_got.at[pair, d - 1],
                z_sem.at[0, pair], z_sem.at[1, pair], slab(d),
            ).start()
            return 0

        @pl.when(lax.rem(hp, 2) == 1)
        def _():
            lax.fori_loop(1, NP, share, 0)

    def relay_y(hp):
        for cp in x2_copies(hp):
            cp.wait_recv()

        def total(y):
            return (
                aq[hp, xi, y].astype(F32)
                + x2_got[hp, 0, y].astype(F32)
                + x2_got[hp, 1, y].astype(F32)
            )

        y_send[hp] = total(yo).astype(BF)
        y_copy(hp).start()
        y_keep[hp] = total(yi)

    def finish(hp):
        cols = lanes_of(hp)
        y_copy(hp).wait_recv()
        both = y_keep[hp] + y_got[hp].astype(F32)
        att_out[0, :, cols] = both[0].astype(BF)
        qg_out[0, :, cols] = both[1]
        stat_all(hp).wait_send()
        for cp in x1_copies(hp) + x2_copies(hp):
            cp.wait_send()
        y_copy(hp).wait_send()
        c_copy(hp).wait_send()

        @pl.when(lax.rem(hp, 2) == 1)
        def _():
            pair = hp // 2
            z_all(pair).wait_recv()
            for q in range(2):
                cols = lanes_of(2 * pair + q)
                for a, out in ((0, kg_out), (1, vg_out)):
                    total = z_send[pair, pb, 2 * q + a].astype(F32)
                    for d in range(NP - 1):
                        total = total + z_got[pair, d, 2 * q + a].astype(F32)
                    out[:, :, cols] = total.reshape(2, 8, 2 * HD)
            z_all(pair).wait_send()

    def turn(s, _):
        @pl.when(s < NC)
        def _():
            first(s)

        @pl.when((s >= 1) & (s < NC + 1))
        def _():
            second(s - 1)

        @pl.when((s >= 2) & (s < NC + 2))
        def _():
            relay_x(s - 2)
            relay_c(s - 2)

        @pl.when((s >= 3) & (s < NC + 3))
        def _():
            relay_y(s - 3)

        @pl.when(s >= 4)
        def _():
            finish(s - 4)

        return 0

    lax.fori_loop(0, NC + 4, turn, 0)


def write_out(*refs):
    sems = refs[8]
    copies = [pltpu.make_async_copy(refs[i], refs[4 + i], sems.at[i]) for i in range(4)]
    for cp in copies:
        cp.start()
    for cp in copies:
        cp.wait()


def local(queries, point_order, keys, values, pair_counts, pair_keys, out_grad):
    hbm = pl.BlockSpec(memory_space=pl.ANY)
    vmem = pl.BlockSpec(memory_space=pltpu.VMEM)
    dma = pltpu.SemaphoreType.DMA
    w2 = 2 * HD
    out_shape = (
        jax.ShapeDtypeStruct((1, BS, D), BF),
        jax.ShapeDtypeStruct((1, BS, D), F32),
        jax.ShapeDtypeStruct((2, 8, D), F32),
        jax.ShapeDtypeStruct((2, 8, D), F32),
    )
    results = pl.pallas_call(
        kernel,
        out_shape=out_shape,
        in_specs=[hbm] * 7,
        out_specs=(vmem, vmem, vmem, vmem),
        scratch_shapes=[
            pltpu.VMEM((NP * BS, D), BF),
            pltpu.VMEM((1, NP * BS), jnp.int32),
            pltpu.VMEM((1, NP), jnp.int32),
            pltpu.VMEM((1, 256), jnp.int32),
            pltpu.VMEM((QS, D), BF),
            pltpu.VMEM((NM, BS, D), BF),
            pltpu.VMEM((2, 4, BS, D), BF),
            pltpu.VMEM((8, QS), F32),
            pltpu.VMEM((2, 2 * QS, w2), BF),
            pltpu.VMEM((2, 2 * QS, w2), BF),
            pltpu.VMEM((2 * KS, w2), BF),
            pltpu.VMEM((2 * KS, w2), BF),
            pltpu.VMEM((2, KS, 2 * QS), BF),
            pltpu.VMEM((2, KS, 2 * QS), BF),
            pltpu.VMEM((2, 8, PQ), F32),
            pltpu.VMEM((8, PQ), F32),
            pltpu.VMEM((NC, 2, 8, PQ), F32),
            pltpu.VMEM((NC, NM - 1, 2, 8, PQ), F32),
            pltpu.VMEM((NC, NX, NY, 2, BS, w2), BF),
            pltpu.VMEM((NC, 2, 2, BS, w2), BF),
            pltpu.VMEM((NC, 2, NY, 2, BS, w2), BF),
            pltpu.VMEM((NC, 2, BS, w2), F32),
            pltpu.VMEM((NC, 2, BS, w2), BF),
            pltpu.VMEM((NC, 2, BS, w2), BF),
            pltpu.VMEM((NC, 2, 2 * BS, w2), F32),
            pltpu.VMEM((NC, 2, 2 * BS, w2), BF),
            pltpu.VMEM((NC, 2, 2 * BS, w2), BF),
            pltpu.VMEM((NC // 2, NP, 4, 16, w2), BF),
            pltpu.VMEM((NC // 2, NP - 1, 4, 16, w2), BF),
            dma((6 + NM,)),
            dma((2, 2)),
            dma((2, NC)),
            dma((2, NC, 2)),
            dma((2, NC, 2)),
            dma((2, NC)),
            dma((2, NC)),
            dma((2, NC // 2)),
        ],
        compiler_params=pltpu.CompilerParams(
            collective_id=0, has_side_effects=True, vmem_limit_bytes=60 * 1024 * 1024
        ),
        name="sparse_attention",
    )(queries, point_order, keys, values, pair_counts, pair_keys, out_grad)
    return pl.pallas_call(
        write_out,
        out_shape=out_shape,
        in_specs=[vmem] * 4,
        out_specs=(hbm,) * 4,
        scratch_shapes=[dma((4,))],
        name="write_out",
    )(*results)


def solution(mesh):
    return jax.shard_map(
        local,
        mesh=mesh,
        in_specs=(
            P("pb", None),
            P("pb", None),
            P("ka", None, None),
            P("ka", None, None),
            P("pb", None),
            P("pb", None),
            P("pb", None, None),
        ),
        out_specs=(
            P(("pb", "ka"), None, None),
            P(("pb", "ka"), None, None),
            P("ka", "pb", None),
            P("ka", "pb", None),
        ),
        check_vma=False,
    )
```

```python
import functools
import math

import jax
import jax.numpy as jnp
from jax import lax
from jax.experimental import pallas as pl
from jax.experimental.pallas import tpu as pltpu
from jax.sharding import PartitionSpec as P

H = 8
HD = 64
D = 512
BS = 128
NP = 16
NX = 4
NY = 2
NM = NX * NY
NC = 4
QS = NM * BS
KS = 4 * BS
PQ = 2 * BS
SCALE = HD ** -0.5
C2 = SCALE * math.log2(math.e)
FAR = 1e30
MESH = pl.DeviceIdType.MESH
BF = jnp.bfloat16
F32 = jnp.float32

NN = (((1,), (0,)), ((), ()))
NT = (((1,), (1,)), ((), ()))
TN = (((0,), (0,)), ((), ()))


def dot(a, b, dims=NN):
    return lax.dot_general(a, b, dims, preferred_element_type=F32)


def kernel(
    queries,
    order,
    keys,
    values,
    counts,
    listing,
    out_grad,
    att_out,
    qg_out,
    kg_out,
    vg_out,
    qbuf,
    order_v,
    counts_v,
    listing_v,
    serial,
    og,
    kv,
    use,
    q_m,
    og_m,
    k_m,
    v_m,
    probs,
    dps,
    qs,
    dss,
    m_keep,
    w_all,
    d_keep,
    stat_own,
    stat_got,
    aq,
    x1_got,
    x2_got,
    y_keep,
    y_send,
    y_got,
    c_keep,
    c_send,
    c_got,
    z_send,
    z_got,
    load_sem,
    kv_sem,
    stat_sem,
    x1_sem,
    x2_sem,
    y_sem,
    c_sem,
    z_sem,
):
    pb = lax.axis_index("pb")
    ka = lax.axis_index("ka")
    core = lax.rem(ka, 2)
    chip = ka // 2
    xi = lax.rem(chip, NX)
    yi = chip // NX
    xr = lax.rem(xi + 1, NX)
    xl = lax.rem(xi + NX - 1, NX)
    xo = lax.rem(xi + 2, NX)
    yo = 1 - yi

    def at_ka(y, x, c):
        return {"ka": (y * NX + x) * 2 + c}

    right, left = at_ka(yi, xr, core), at_ka(yi, xl, core)
    across = at_ka(yo, xi, core)
    mate = {"ka": chip * 2 + (1 - core)}

    def peer(d):
        return {"ka": lax.rem(chip + d, NM) * 2 + core}

    def slab(d):
        return {"pb": lax.rem(pb + d, NP)}

    def send(src, dst, send_sem, recv_sem, device):
        return pltpu.make_async_remote_copy(
            src_ref=src, dst_ref=dst, send_sem=send_sem, recv_sem=recv_sem,
            device_id=device, device_id_type=MESH,
        )

    own2 = pl.ds(2 * core, 2)
    load_q = pltpu.make_async_copy(queries, qbuf, load_sem.at[0])
    load_small = [
        pltpu.make_async_copy(order, order_v, load_sem.at[3]),
        pltpu.make_async_copy(counts, counts_v, load_sem.at[4]),
        pltpu.make_async_copy(listing, listing_v, load_sem.at[5]),
    ]
    load_kv = [
        pltpu.make_async_copy(keys, kv.at[0, own2], load_sem.at[1]),
        pltpu.make_async_copy(values, kv.at[1, own2], load_sem.at[2]),
    ]
    load_og = [
        pltpu.make_async_copy(out_grad.at[2 * b + core], og.at[b], load_sem.at[6 + b])
        for b in range(NM)
    ]
    for cp in load_small + [load_q] + load_kv + load_og:
        cp.start()

    barrier = pltpu.get_barrier_semaphore()
    pl.semaphore_signal(barrier, inc=1, device_id=mate, device_id_type=MESH)

    def hello_ka(d, _):
        pl.semaphore_signal(barrier, inc=1, device_id=peer(d), device_id_type=MESH)
        return 0

    def hello_pb(d, _):
        pl.semaphore_signal(barrier, inc=1, device_id=slab(d), device_id_type=MESH)
        return 0

    lax.fori_loop(1, NM, hello_ka, 0)
    lax.fori_loop(1, NP, hello_pb, 0)

    for cp in load_small:
        cp.wait()

    cb = jnp.broadcast_to(counts_v[...].astype(F32), (16, 16))
    i0 = lax.broadcasted_iota(jnp.int32, (16, 16), 0)
    i1 = lax.broadcasted_iota(jnp.int32, (16, 16), 1)
    starts = jnp.sum(jnp.where(i1 < i0, cb, 0.0), axis=1, keepdims=True)
    sizes = jnp.sum(jnp.where(i1 == i0, cb, 0.0), axis=1, keepdims=True)
    slot = lax.broadcasted_iota(jnp.int32, (16, 256), 1).astype(F32)
    inside = jnp.where((slot >= starts) & (slot < starts + sizes), 1.0, 0.0)
    row = lax.broadcasted_iota(jnp.int32, (8, 256), 0) + 4 * chip
    named = jnp.where(jnp.broadcast_to(listing_v[...], (8, 256)) == row, 1.0, 0.0)
    joined = dot(named.astype(BF), inside.astype(BF), NT)
    e0 = lax.broadcasted_iota(jnp.int32, (16, QS), 0)
    e1 = lax.broadcasted_iota(jnp.int32, (16, QS), 1)
    spread = jnp.where(e0 == 2 * (e1 // BS) + core, 1.0, 0.0)
    use[...] = dot(joined.astype(BF), spread.astype(BF))

    load_q.wait()

    send_k = send(keys, kv.at[0, own2], kv_sem.at[0, 0], kv_sem.at[1, 0], mate)
    send_v = send(values, kv.at[1, own2], kv_sem.at[0, 1], kv_sem.at[1, 1], mate)

    def gather(t, _):
        @pl.when(t == 1)
        def _():
            pl.semaphore_wait(barrier, 1 + (NM - 1) + (NP - 1))
            send_k.start()
            send_v.start()

        picks = []
        for e in range(4):
            at = pl.multiple_of((8 * t + 2 * e + core) * BS, BS)
            column = jnp.broadcast_to(order_v[:, pl.ds(at, BS)], (BS, BS)).T
            lanes = lax.broadcasted_iota(jnp.int32, (BS, BS), 1)
            picks.append(jnp.concatenate(
                [jnp.where(column == lanes + n * BS, 1.0, 0.0).astype(BF) for n in range(16)], axis=1
            ))
        pick = jnp.concatenate(picks, axis=0)
        serial[pl.ds(pl.multiple_of(t * 4 * BS, 4 * BS), 4 * BS), :] = dot(pick, qbuf[...]).astype(BF)
        return 0

    lax.fori_loop(0, 2, gather, 0)
    for cp in load_kv + load_og:
        cp.wait()
    send_k.wait()
    send_v.wait()

    def lanes_of(hp):
        return pl.ds(pl.multiple_of(hp * 2 * HD, 2 * HD), 2 * HD)

    def split_heads(src, dst, n):
        low = lax.broadcasted_iota(jnp.int32, (n, 2 * HD), 1) < HD
        none = jnp.zeros((n, 2 * HD), BF)
        dst[:n] = jnp.where(low, src, none)
        dst[n:] = jnp.where(low, none, src)

    def columns(u):
        p, h = u // 2, u % 2
        return slice(h * QS + p * PQ, h * QS + (p + 1) * PQ)

    def first(hp):
        par = lax.rem(hp, 2)
        cols = lanes_of(hp)
        k2 = kv[0, :, :, cols].reshape(KS, 2 * HD)
        v2 = kv[1, :, :, cols].reshape(KS, 2 * HD)
        split_heads(serial[:, cols], q_m.at[par], QS)
        split_heads(og[:, :, cols].reshape(QS, 2 * HD), og_m.at[par], QS)

        def products(u):
            cc = columns(u)
            return dot(k2, q_m[par, cc, :], NT), dot(v2, og_m[par, cc, :], NT)

        def softmax(u, st, dp):
            p, h = u // 2, u % 2
            cc = columns(u)
            usable = use[0:4, p * PQ:(p + 1) * PQ] > 0.5
            m_raw = jnp.full((1, PQ), -FAR, F32)
            for kb in range(4):
                top = jnp.max(st[kb * BS:(kb + 1) * BS], axis=0, keepdims=True)
                m_raw = jnp.maximum(m_raw, jnp.where(usable[kb:kb + 1], top, -FAR))
            m = m_raw * C2
            total = jnp.zeros((BS, PQ), F32)
            weighted = jnp.zeros((BS, PQ), F32)
            for kb in range(4):
                ks = slice(kb * BS, (kb + 1) * BS)
                off = jnp.where(usable[kb:kb + 1], m, FAR)
                pr = jnp.exp2(st[ks] * C2 - off)
                total = total + pr
                weighted = weighted + pr * dp[ks]
                probs[par, ks, cc] = pr.astype(BF)
            dps[par, :, cc] = dp.astype(BF)
            total = jnp.maximum(jnp.sum(total, axis=0, keepdims=True), 0.5)
            weighted = jnp.sum(weighted, axis=0, keepdims=True)
            r = slice(u, u + 1)
            m_keep[par, r, :] = m
            stat_own[hp, 0, r, :] = m + jnp.log2(total)
            stat_own[hp, 1, r, :] = weighted / total

        ahead = products(0)
        for u in range(NM):
            now = ahead
            if u + 1 < NM:
                ahead = products(u + 1)
            softmax(u, *now)

        def share(d, _):
            send(stat_own.at[hp], stat_got.at[hp, d - 1], stat_sem.at[0, hp], stat_sem.at[1, hp], peer(d)).start()
            return 0

        lax.fori_loop(1, NM, share, 0)

    def stat_all(hp):
        return send(stat_got.at[hp], stat_got.at[hp], stat_sem.at[0, hp], stat_sem.at[1, hp], right)

    def second(hp):
        par = lax.rem(hp, 2)
        cols = lanes_of(hp)
        stat_all(hp).wait_recv()
        lse = [stat_own[hp, 0]] + [stat_got[hp, d, 0] for d in range(NM - 1)]
        dlt = [stat_own[hp, 1]] + [stat_got[hp, d, 1] for d in range(NM - 1)]
        top = functools.reduce(jnp.maximum, lse)
        ws = [jnp.exp2(v - top) for v in lse]
        total = functools.reduce(jnp.add, ws)
        delta_all = functools.reduce(jnp.add, [w * v for w, v in zip(ws, dlt)]) / total
        w_all[...] = jnp.exp2(m_keep[par] - (top + jnp.log2(total)))
        d_keep[...] = delta_all
        split_heads(kv[0, :, :, cols].reshape(KS, 2 * HD), k_m, KS)
        split_heads(kv[1, :, :, cols].reshape(KS, 2 * HD), v_m, KS)

        for p in range(NM // 2):
            att = jnp.zeros((PQ, 2 * HD), F32)
            dq = jnp.zeros((PQ, 2 * HD), F32)
            for h in range(2):
                u = 2 * p + h
                cc = columns(u)
                hk = slice(h * KS, (h + 1) * KS)
                qf = probs[par, :, cc].astype(F32) * w_all[u:u + 1, :]
                qb = qf.astype(BF)
                ds = (qf * (dps[par, :, cc].astype(F32) - d_keep[u:u + 1, :])).astype(BF)
                qs[:, cc] = qb
                dss[:, cc] = ds
                att = att + dot(qb, v_m[hk, :], TN)
                dq = dq + dot(ds, k_m[hk, :], TN)
            att = att.astype(BF)
            dq = (dq * SCALE).astype(BF)
            for e in range(2):
                b = 2 * p + e
                x, y = b % NX, b // NX
                aq[hp, x, y, 0] = att[e * BS:(e + 1) * BS]
                aq[hp, x, y, 1] = dq[e * BS:(e + 1) * BS]
        for cp in x1_copies(hp):
            cp.start()
        dk = (dot(dss[...], q_m[par]) * SCALE).reshape(2, 2 * BS, 2 * HD)
        dv = dot(qs[...], og_m[par]).reshape(2, 2 * BS, 2 * HD)
        mine = core == 0
        c_keep[hp, 0] = jnp.where(mine, dk[0], dk[1])
        c_keep[hp, 1] = jnp.where(mine, dv[0], dv[1])
        c_send[hp, 0] = jnp.where(mine, dk[1], dk[0]).astype(BF)
        c_send[hp, 1] = jnp.where(mine, dv[1], dv[0]).astype(BF)
        c_copy(hp).start()

    def x1_copies(hp):
        return (
            send(aq.at[hp, xo, 0], x1_got.at[hp, 0], x1_sem.at[0, hp, 0], x1_sem.at[1, hp, 0], right),
            send(aq.at[hp, xo, 1], x1_got.at[hp, 1], x1_sem.at[0, hp, 1], x1_sem.at[1, hp, 1], left),
        )

    def x2_copies(hp):
        return (
            send(aq.at[hp, xr], x2_got.at[hp, 0], x2_sem.at[0, hp, 0], x2_sem.at[1, hp, 0], right),
            send(aq.at[hp, xl], x2_got.at[hp, 1], x2_sem.at[0, hp, 1], x2_sem.at[1, hp, 1], left),
        )

    def y_copy(hp):
        return send(y_send.at[hp], y_got.at[hp], y_sem.at[0, hp], y_sem.at[1, hp], across)

    def c_copy(hp):
        return send(c_send.at[hp], c_got.at[hp], c_sem.at[0, hp], c_sem.at[1, hp], mate)

    def z_all(hp):
        return send(z_got.at[hp], z_got.at[hp], z_sem.at[0, hp], z_sem.at[1, hp], slab(1))

    def relay_x(hp):
        for cp in x1_copies(hp):
            cp.wait_recv()
        aq[hp, xr, 0] = (aq[hp, xr, 0].astype(F32) + x1_got[hp, 0].astype(F32)).astype(BF)
        aq[hp, xl, 1] = (aq[hp, xl, 1].astype(F32) + x1_got[hp, 1].astype(F32)).astype(BF)
        for cp in x2_copies(hp):
            cp.start()

    def relay_c(hp):
        c_copy(hp).wait_recv()
        for a in range(2):
            total = c_keep[hp, a] + c_got[hp, a].astype(F32)
            total = total.reshape(2, NP, 8, 2 * HD).transpose(1, 0, 2, 3)
            z_send[hp, :, a] = total.reshape(NP, 16, 2 * HD).astype(BF)

        def share(d, _):
            send(
                z_send.at[hp, lax.rem(pb + d, NP)], z_got.at[hp, d - 1],
                z_sem.at[0, hp], z_sem.at[1, hp], slab(d),
            ).start()
            return 0

        lax.fori_loop(1, NP, share, 0)

    def relay_y(hp):
        for cp in x2_copies(hp):
            cp.wait_recv()

        def total(y):
            return (
                aq[hp, xi, y].astype(F32)
                + x2_got[hp, 0, y].astype(F32)
                + x2_got[hp, 1, y].astype(F32)
            )

        y_send[hp] = total(yo).astype(BF)
        y_copy(hp).start()
        y_keep[hp] = total(yi)

    def finish(hp):
        cols = lanes_of(hp)
        z_all(hp).wait_recv()
        for a, out in ((0, kg_out), (1, vg_out)):
            total = z_send[hp, pb, a].astype(F32)
            for d in range(NP - 1):
                total = total + z_got[hp, d, a].astype(F32)
            out[:, :, cols] = total.reshape(2, 8, 2 * HD)
        y_copy(hp).wait_recv()
        both = y_keep[hp] + y_got[hp].astype(F32)
        att_out[0, :, cols] = both[0].astype(BF)
        qg_out[0, :, cols] = both[1]
        stat_all(hp).wait_send()
        for cp in x1_copies(hp) + x2_copies(hp):
            cp.wait_send()
        y_copy(hp).wait_send()
        c_copy(hp).wait_send()
        z_all(hp).wait_send()

    def turn(s, _):
        @pl.when(s < NC)
        def _():
            first(s)

        @pl.when((s >= 1) & (s < NC + 1))
        def _():
            second(s - 1)

        @pl.when((s >= 2) & (s < NC + 2))
        def _():
            relay_x(s - 2)
            relay_c(s - 2)

        @pl.when((s >= 3) & (s < NC + 3))
        def _():
            relay_y(s - 3)

        @pl.when(s >= 4)
        def _():
            finish(s - 4)

        return 0

    lax.fori_loop(0, NC + 4, turn, 0)


def write_out(*refs):
    sems = refs[8]
    copies = [pltpu.make_async_copy(refs[i], refs[4 + i], sems.at[i]) for i in range(4)]
    for cp in copies:
        cp.start()
    for cp in copies:
        cp.wait()


def local(queries, point_order, keys, values, pair_counts, pair_keys, out_grad):
    hbm = pl.BlockSpec(memory_space=pl.ANY)
    vmem = pl.BlockSpec(memory_space=pltpu.VMEM)
    dma = pltpu.SemaphoreType.DMA
    w2 = 2 * HD
    out_shape = (
        jax.ShapeDtypeStruct((1, BS, D), BF),
        jax.ShapeDtypeStruct((1, BS, D), F32),
        jax.ShapeDtypeStruct((2, 8, D), F32),
        jax.ShapeDtypeStruct((2, 8, D), F32),
    )
    results = pl.pallas_call(
        kernel,
        out_shape=out_shape,
        in_specs=[hbm] * 7,
        out_specs=(vmem, vmem, vmem, vmem),
        scratch_shapes=[
            pltpu.VMEM((NP * BS, D), BF),
            pltpu.VMEM((1, NP * BS), jnp.int32),
            pltpu.VMEM((1, NP), jnp.int32),
            pltpu.VMEM((1, 256), jnp.int32),
            pltpu.VMEM((QS, D), BF),
            pltpu.VMEM((NM, BS, D), BF),
            pltpu.VMEM((2, 4, BS, D), BF),
            pltpu.VMEM((8, QS), F32),
            pltpu.VMEM((2, 2 * QS, w2), BF),
            pltpu.VMEM((2, 2 * QS, w2), BF),
            pltpu.VMEM((2 * KS, w2), BF),
            pltpu.VMEM((2 * KS, w2), BF),
            pltpu.VMEM((2, KS, 2 * QS), BF),
            pltpu.VMEM((2, KS, 2 * QS), BF),
            pltpu.VMEM((KS, 2 * QS), BF),
            pltpu.VMEM((KS, 2 * QS), BF),
            pltpu.VMEM((2, 8, PQ), F32),
            pltpu.VMEM((8, PQ), F32),
            pltpu.VMEM((8, PQ), F32),
            pltpu.VMEM((NC, 2, 8, PQ), F32),
            pltpu.VMEM((NC, NM - 1, 2, 8, PQ), F32),
            pltpu.VMEM((NC, NX, NY, 2, BS, w2), BF),
            pltpu.VMEM((NC, 2, 2, BS, w2), BF),
            pltpu.VMEM((NC, 2, NY, 2, BS, w2), BF),
            pltpu.VMEM((NC, 2, BS, w2), F32),
            pltpu.VMEM((NC, 2, BS, w2), BF),
            pltpu.VMEM((NC, 2, BS, w2), BF),
            pltpu.VMEM((NC, 2, 2 * BS, w2), F32),
            pltpu.VMEM((NC, 2, 2 * BS, w2), BF),
            pltpu.VMEM((NC, 2, 2 * BS, w2), BF),
            pltpu.VMEM((NC, NP, 2, 16, w2), BF),
            pltpu.VMEM((NC, NP - 1, 2, 16, w2), BF),
            dma((6 + NM,)),
            dma((2, 2)),
            dma((2, NC)),
            dma((2, NC, 2)),
            dma((2, NC, 2)),
            dma((2, NC)),
            dma((2, NC)),
            dma((2, NC)),
        ],
        compiler_params=pltpu.CompilerParams(
            collective_id=0, has_side_effects=True, vmem_limit_bytes=60 * 1024 * 1024
        ),
        name="sparse_attention",
    )(queries, point_order, keys, values, pair_counts, pair_keys, out_grad)
    return pl.pallas_call(
        write_out,
        out_shape=out_shape,
        in_specs=[vmem] * 4,
        out_specs=(hbm,) * 4,
        scratch_shapes=[dma((4,))],
        name="write_out",
    )(*results)


def solution(mesh):
    return jax.shard_map(
        local,
        mesh=mesh,
        in_specs=(
            P("pb", None),
            P("pb", None),
            P("ka", None, None),
            P("ka", None, None),
            P("pb", None),
            P("pb", None),
            P("pb", None, None),
        ),
        out_specs=(
            P(("pb", "ka"), None, None),
            P(("pb", "ka"), None, None),
            P("ka", "pb", None),
            P("ka", "pb", None),
        ),
        check_vma=False,
    )
```

```python
import functools
import math

import jax
import jax.numpy as jnp
from jax import lax
from jax.experimental import pallas as pl
from jax.experimental.pallas import tpu as pltpu
from jax.sharding import PartitionSpec as P

H = 8
HD = 64
D = 512
BS = 128
NP = 16
NX = 4
NY = 2
NM = NX * NY
NC = 4
QS = NM * BS
KS = 4 * BS
PQ = 2 * BS
SCALE = HD ** -0.5
C2 = SCALE * math.log2(math.e)
FAR = 1e30
MESH = pl.DeviceIdType.MESH
BF = jnp.bfloat16
F32 = jnp.float32

NN = (((1,), (0,)), ((), ()))
NT = (((1,), (1,)), ((), ()))
TN = (((0,), (0,)), ((), ()))


def dot(a, b, dims=NN):
    return lax.dot_general(a, b, dims, preferred_element_type=F32)


def kernel(
    queries,
    order,
    keys,
    values,
    counts,
    listing,
    out_grad,
    att_out,
    qg_out,
    kg_out,
    vg_out,
    qbuf,
    order_v,
    counts_v,
    listing_v,
    serial,
    og,
    kv,
    use,
    q_m,
    og_m,
    k_m,
    v_m,
    probs,
    dps,
    qs,
    dss,
    m_keep,
    w_all,
    d_keep,
    stat_own,
    stat_got,
    aq,
    x1_got,
    near_got,
    x2_got,
    y_keep,
    y_send,
    y_got,
    c_keep,
    c_send,
    c_got,
    z_send,
    z_got,
    load_sem,
    kv_sem,
    stat_sem,
    x1_sem,
    near_sem,
    x2_sem,
    y_sem,
    c_sem,
    z_sem,
):
    pb = lax.axis_index("pb")
    ka = lax.axis_index("ka")
    core = lax.rem(ka, 2)
    chip = ka // 2
    xi = lax.rem(chip, NX)
    yi = chip // NX
    xr = lax.rem(xi + 1, NX)
    xl = lax.rem(xi + NX - 1, NX)
    xo = lax.rem(xi + 2, NX)
    yo = 1 - yi

    def at_ka(y, x, c):
        return {"ka": (y * NX + x) * 2 + c}

    right, left = at_ka(yi, xr, core), at_ka(yi, xl, core)
    across = at_ka(yo, xi, core)
    mate = {"ka": chip * 2 + (1 - core)}

    def peer(d):
        return {"ka": lax.rem(chip + d, NM) * 2 + core}

    def slab(d):
        return {"pb": lax.rem(pb + d, NP)}

    def send(src, dst, send_sem, recv_sem, device):
        return pltpu.make_async_remote_copy(
            src_ref=src, dst_ref=dst, send_sem=send_sem, recv_sem=recv_sem,
            device_id=device, device_id_type=MESH,
        )

    own2 = pl.ds(2 * core, 2)
    load_q = pltpu.make_async_copy(queries, qbuf, load_sem.at[0])
    load_small = [
        pltpu.make_async_copy(order, order_v, load_sem.at[3]),
        pltpu.make_async_copy(counts, counts_v, load_sem.at[4]),
        pltpu.make_async_copy(listing, listing_v, load_sem.at[5]),
    ]
    load_kv = [
        pltpu.make_async_copy(keys, kv.at[0, own2], load_sem.at[1]),
        pltpu.make_async_copy(values, kv.at[1, own2], load_sem.at[2]),
    ]
    load_og = [
        pltpu.make_async_copy(out_grad.at[2 * b + core], og.at[b], load_sem.at[6 + b])
        for b in range(NM)
    ]
    for cp in load_small + [load_q] + load_kv + load_og:
        cp.start()

    barrier = pltpu.get_barrier_semaphore()
    pl.semaphore_signal(barrier, inc=1, device_id=mate, device_id_type=MESH)

    def hello_ka(d, _):
        pl.semaphore_signal(barrier, inc=1, device_id=peer(d), device_id_type=MESH)
        return 0

    def hello_pb(d, _):
        pl.semaphore_signal(barrier, inc=1, device_id=slab(d), device_id_type=MESH)
        return 0

    lax.fori_loop(1, NM, hello_ka, 0)
    lax.fori_loop(1, NP, hello_pb, 0)

    for cp in load_small:
        cp.wait()

    cb = jnp.broadcast_to(counts_v[...].astype(F32), (16, 16))
    i0 = lax.broadcasted_iota(jnp.int32, (16, 16), 0)
    i1 = lax.broadcasted_iota(jnp.int32, (16, 16), 1)
    starts = jnp.sum(jnp.where(i1 < i0, cb, 0.0), axis=1, keepdims=True)
    sizes = jnp.sum(jnp.where(i1 == i0, cb, 0.0), axis=1, keepdims=True)
    slot = lax.broadcasted_iota(jnp.int32, (16, 256), 1).astype(F32)
    inside = jnp.where((slot >= starts) & (slot < starts + sizes), 1.0, 0.0)
    row = lax.broadcasted_iota(jnp.int32, (8, 256), 0) + 4 * chip
    named = jnp.where(jnp.broadcast_to(listing_v[...], (8, 256)) == row, 1.0, 0.0)
    joined = dot(named.astype(BF), inside.astype(BF), NT)
    e0 = lax.broadcasted_iota(jnp.int32, (16, QS), 0)
    e1 = lax.broadcasted_iota(jnp.int32, (16, QS), 1)
    spread = jnp.where(e0 == 2 * (e1 // BS) + core, 1.0, 0.0)
    use[...] = dot(joined.astype(BF), spread.astype(BF))

    load_q.wait()

    send_k = send(keys, kv.at[0, own2], kv_sem.at[0, 0], kv_sem.at[1, 0], mate)
    send_v = send(values, kv.at[1, own2], kv_sem.at[0, 1], kv_sem.at[1, 1], mate)

    def gather(t, _):
        @pl.when(t == 1)
        def _():
            pl.semaphore_wait(barrier, 1 + (NM - 1) + (NP - 1))
            send_k.start()
            send_v.start()

        picks = []
        for e in range(4):
            at = pl.multiple_of((8 * t + 2 * e + core) * BS, BS)
            column = jnp.broadcast_to(order_v[:, pl.ds(at, BS)], (BS, BS)).T
            lanes = lax.broadcasted_iota(jnp.int32, (BS, BS), 1)
            picks.append(jnp.concatenate(
                [jnp.where(column == lanes + n * BS, 1.0, 0.0).astype(BF) for n in range(16)], axis=1
            ))
        pick = jnp.concatenate(picks, axis=0)
        serial[pl.ds(pl.multiple_of(t * 4 * BS, 4 * BS), 4 * BS), :] = dot(pick, qbuf[...]).astype(BF)
        return 0

    lax.fori_loop(0, 2, gather, 0)
    for cp in load_kv + load_og:
        cp.wait()
    send_k.wait()
    send_v.wait()

    def lanes_of(hp):
        return pl.ds(pl.multiple_of(hp * 2 * HD, 2 * HD), 2 * HD)

    def split_heads(src, dst, n):
        low = lax.broadcasted_iota(jnp.int32, (n, 2 * HD), 1) < HD
        none = jnp.zeros((n, 2 * HD), BF)
        dst[:n] = jnp.where(low, src, none)
        dst[n:] = jnp.where(low, none, src)

    def columns(u):
        p, h = u // 2, u % 2
        return slice(h * QS + p * PQ, h * QS + (p + 1) * PQ)

    def first(hp):
        par = lax.rem(hp, 2)
        cols = lanes_of(hp)
        k2 = kv[0, :, :, cols].reshape(KS, 2 * HD)
        v2 = kv[1, :, :, cols].reshape(KS, 2 * HD)
        split_heads(serial[:, cols], q_m.at[par], QS)
        split_heads(og[:, :, cols].reshape(QS, 2 * HD), og_m.at[par], QS)

        def products(u):
            cc = columns(u)
            return dot(k2, q_m[par, cc, :], NT), dot(v2, og_m[par, cc, :], NT)

        def softmax(u, st, dp):
            p, h = u // 2, u % 2
            cc = columns(u)
            usable = use[0:4, p * PQ:(p + 1) * PQ] > 0.5
            m_raw = jnp.full((1, PQ), -FAR, F32)
            for kb in range(4):
                top = jnp.max(st[kb * BS:(kb + 1) * BS], axis=0, keepdims=True)
                m_raw = jnp.maximum(m_raw, jnp.where(usable[kb:kb + 1], top, -FAR))
            m = m_raw * C2
            total = jnp.zeros((BS, PQ), F32)
            weighted = jnp.zeros((BS, PQ), F32)
            for kb in range(4):
                ks = slice(kb * BS, (kb + 1) * BS)
                off = jnp.where(usable[kb:kb + 1], m, FAR)
                pr = jnp.exp2(st[ks] * C2 - off)
                total = total + pr
                weighted = weighted + pr * dp[ks]
                probs[par, ks, cc] = pr.astype(BF)
            dps[par, :, cc] = dp.astype(BF)
            total = jnp.maximum(jnp.sum(total, axis=0, keepdims=True), 0.5)
            weighted = jnp.sum(weighted, axis=0, keepdims=True)
            r = slice(u, u + 1)
            m_keep[par, r, :] = m
            stat_own[hp, 0, r, :] = m + jnp.log2(total)
            stat_own[hp, 1, r, :] = weighted / total

        ahead = products(0)
        for u in range(NM):
            now = ahead
            if u + 1 < NM:
                ahead = products(u + 1)
            softmax(u, *now)

        def share(d, _):
            send(stat_own.at[hp], stat_got.at[hp, d - 1], stat_sem.at[0, hp], stat_sem.at[1, hp], peer(d)).start()
            return 0

        lax.fori_loop(1, NM, share, 0)

    def stat_all(hp):
        return send(stat_got.at[hp], stat_got.at[hp], stat_sem.at[0, hp], stat_sem.at[1, hp], right)

    def second(hp):
        par = lax.rem(hp, 2)
        cols = lanes_of(hp)
        stat_all(hp).wait_recv()
        lse = [stat_own[hp, 0]] + [stat_got[hp, d, 0] for d in range(NM - 1)]
        dlt = [stat_own[hp, 1]] + [stat_got[hp, d, 1] for d in range(NM - 1)]
        top = functools.reduce(jnp.maximum, lse)
        ws = [jnp.exp2(v - top) for v in lse]
        total = functools.reduce(jnp.add, ws)
        delta_all = functools.reduce(jnp.add, [w * v for w, v in zip(ws, dlt)]) / total
        w_all[...] = jnp.exp2(m_keep[par] - (top + jnp.log2(total)))
        d_keep[...] = delta_all
        split_heads(kv[0, :, :, cols].reshape(KS, 2 * HD), k_m, KS)
        split_heads(kv[1, :, :, cols].reshape(KS, 2 * HD), v_m, KS)

        for p in range(NM // 2):
            att = jnp.zeros((PQ, 2 * HD), F32)
            dq = jnp.zeros((PQ, 2 * HD), F32)
            for h in range(2):
                u = 2 * p + h
                cc = columns(u)
                hk = slice(h * KS, (h + 1) * KS)
                qf = probs[par, :, cc].astype(F32) * w_all[u:u + 1, :]
                qb = qf.astype(BF)
                ds = (qf * (dps[par, :, cc].astype(F32) - d_keep[u:u + 1, :])).astype(BF)
                qs[:, cc] = qb
                dss[:, cc] = ds
                att = att + dot(qb, v_m[hk, :], TN)
                dq = dq + dot(ds, k_m[hk, :], TN)
            att = att.astype(BF)
            dq = (dq * SCALE).astype(BF)
            for e in range(2):
                b = 2 * p + e
                x, y = b % NX, b // NX
                aq[hp, x, y, 0] = att[e * BS:(e + 1) * BS]
                aq[hp, x, y, 1] = dq[e * BS:(e + 1) * BS]
        for cp in x1_copies(hp, 0) + x1_copies(hp, 1) + near_copies(hp):
            cp.start()
        dk = (dot(dss[...], q_m[par]) * SCALE).reshape(2, 2 * BS, 2 * HD)
        dv = dot(qs[...], og_m[par]).reshape(2, 2 * BS, 2 * HD)
        mine = core == 0
        c_keep[hp, 0] = jnp.where(mine, dk[0], dk[1])
        c_keep[hp, 1] = jnp.where(mine, dv[0], dv[1])
        c_send[hp, 0] = jnp.where(mine, dk[1], dk[0]).astype(BF)
        c_send[hp, 1] = jnp.where(mine, dv[1], dv[0]).astype(BF)
        c_copy(hp).start()

    def x1_copies(hp, kind):
        return tuple(
            send(
                aq.at[hp, xo, way, kind], x1_got.at[hp, way, kind],
                x1_sem.at[0, hp, way, kind], x1_sem.at[1, hp, way, kind], (right, left)[way],
            ) for way in range(2)
        )

    def near_copies(hp):
        return tuple(
            send(
                aq.at[hp, (xr, xl)[way], 1 - way], near_got.at[hp, way],
                near_sem.at[0, hp, way], near_sem.at[1, hp, way], (right, left)[way],
            ) for way in range(2)
        )

    def x2_copies(hp, kind):
        return tuple(
            send(
                aq.at[hp, (xr, xl)[way], way, kind], x2_got.at[hp, way, kind],
                x2_sem.at[0, hp, way, kind], x2_sem.at[1, hp, way, kind], (right, left)[way],
            ) for way in range(2)
        )

    def y_copy(hp, kind):
        return send(y_send.at[hp, kind], y_got.at[hp, kind], y_sem.at[0, hp, kind], y_sem.at[1, hp, kind], across)

    def c_copy(hp):
        return send(c_send.at[hp], c_got.at[hp], c_sem.at[0, hp], c_sem.at[1, hp], mate)

    def z_all(hp):
        return send(z_got.at[hp], z_got.at[hp], z_sem.at[0, hp], z_sem.at[1, hp], slab(1))

    def relay_x(hp):
        for kind in range(2):
            for cp in x1_copies(hp, kind):
                cp.wait_recv()
            for way, x in ((0, xr), (1, xl)):
                aq[hp, x, way, kind] = (
                    aq[hp, x, way, kind].astype(F32) + x1_got[hp, way, kind].astype(F32)
                ).astype(BF)
            for cp in x2_copies(hp, kind):
                cp.start()

    def relay_c(hp):
        c_copy(hp).wait_recv()
        for a in range(2):
            total = c_keep[hp, a] + c_got[hp, a].astype(F32)
            total = total.reshape(2, NP, 8, 2 * HD).transpose(1, 0, 2, 3)
            z_send[hp, :, a] = total.reshape(NP, 16, 2 * HD).astype(BF)

        def share(d, _):
            send(
                z_send.at[hp, lax.rem(pb + d, NP)], z_got.at[hp, d - 1],
                z_sem.at[0, hp], z_sem.at[1, hp], slab(d),
            ).start()
            return 0

        lax.fori_loop(1, NP, share, 0)

    def relay_y(hp):
        for cp in near_copies(hp):
            cp.wait_recv()
        low = yi == 0
        for kind in range(2):
            for cp in x2_copies(hp, kind):
                cp.wait_recv()
            t0, t1 = (
                aq[hp, xi, y, kind].astype(F32)
                + x2_got[hp, y, kind].astype(F32)
                + near_got[hp, 1 - y, kind].astype(F32)
                for y in range(NY)
            )
            y_send[hp, kind] = jnp.where(low, t1, t0).astype(BF)
            y_copy(hp, kind).start()
            y_keep[hp, kind] = jnp.where(low, t0, t1)

    def finish(hp):
        cols = lanes_of(hp)
        z_all(hp).wait_recv()
        for a, out in ((0, kg_out), (1, vg_out)):
            total = z_send[hp, pb, a].astype(F32)
            for d in range(NP - 1):
                total = total + z_got[hp, d, a].astype(F32)
            out[:, :, cols] = total.reshape(2, 8, 2 * HD)
        for kind, out in ((0, att_out), (1, qg_out)):
            y_copy(hp, kind).wait_recv()
            out[0, :, cols] = (y_keep[hp, kind] + y_got[hp, kind].astype(F32)).astype(out.dtype)
        stat_all(hp).wait_send()
        for kind in range(2):
            for cp in x1_copies(hp, kind) + x2_copies(hp, kind):
                cp.wait_send()
            y_copy(hp, kind).wait_send()
        for cp in near_copies(hp):
            cp.wait_send()
        c_copy(hp).wait_send()
        z_all(hp).wait_send()

    def turn(s, _):
        @pl.when(s < NC)
        def _():
            first(s)

        @pl.when((s >= 1) & (s < NC + 1))
        def _():
            second(s - 1)

        @pl.when((s >= 2) & (s < NC + 2))
        def _():
            relay_x(s - 2)

        @pl.when((s >= 3) & (s < NC + 3))
        def _():
            relay_y(s - 3)

        @pl.when((s >= 2) & (s < NC + 2))
        def _():
            relay_c(s - 2)

        @pl.when(s >= 4)
        def _():
            finish(s - 4)

        return 0

    lax.fori_loop(0, NC + 4, turn, 0)


def write_out(*refs):
    sems = refs[8]
    copies = [pltpu.make_async_copy(refs[i], refs[4 + i], sems.at[i]) for i in range(4)]
    for cp in copies:
        cp.start()
    for cp in copies:
        cp.wait()


def local(queries, point_order, keys, values, pair_counts, pair_keys, out_grad):
    hbm = pl.BlockSpec(memory_space=pl.ANY)
    vmem = pl.BlockSpec(memory_space=pltpu.VMEM)
    dma = pltpu.SemaphoreType.DMA
    w2 = 2 * HD
    out_shape = (
        jax.ShapeDtypeStruct((1, BS, D), BF),
        jax.ShapeDtypeStruct((1, BS, D), F32),
        jax.ShapeDtypeStruct((2, 8, D), F32),
        jax.ShapeDtypeStruct((2, 8, D), F32),
    )
    results = pl.pallas_call(
        kernel,
        out_shape=out_shape,
        in_specs=[hbm] * 7,
        out_specs=(vmem, vmem, vmem, vmem),
        scratch_shapes=[
            pltpu.VMEM((NP * BS, D), BF),
            pltpu.VMEM((1, NP * BS), jnp.int32),
            pltpu.VMEM((1, NP), jnp.int32),
            pltpu.VMEM((1, 256), jnp.int32),
            pltpu.VMEM((QS, D), BF),
            pltpu.VMEM((NM, BS, D), BF),
            pltpu.VMEM((2, 4, BS, D), BF),
            pltpu.VMEM((8, QS), F32),
            pltpu.VMEM((2, 2 * QS, w2), BF),
            pltpu.VMEM((2, 2 * QS, w2), BF),
            pltpu.VMEM((2 * KS, w2), BF),
            pltpu.VMEM((2 * KS, w2), BF),
            pltpu.VMEM((2, KS, 2 * QS), BF),
            pltpu.VMEM((2, KS, 2 * QS), BF),
            pltpu.VMEM((KS, 2 * QS), BF),
            pltpu.VMEM((KS, 2 * QS), BF),
            pltpu.VMEM((2, 8, PQ), F32),
            pltpu.VMEM((8, PQ), F32),
            pltpu.VMEM((8, PQ), F32),
            pltpu.VMEM((NC, 2, 8, PQ), F32),
            pltpu.VMEM((NC, NM - 1, 2, 8, PQ), F32),
            pltpu.VMEM((NC, NX, NY, 2, BS, w2), BF),
            pltpu.VMEM((NC, 2, 2, BS, w2), BF),
            pltpu.VMEM((NC, 2, 2, BS, w2), BF),
            pltpu.VMEM((NC, 2, 2, BS, w2), BF),
            pltpu.VMEM((NC, 2, BS, w2), F32),
            pltpu.VMEM((NC, 2, BS, w2), BF),
            pltpu.VMEM((NC, 2, BS, w2), BF),
            pltpu.VMEM((NC, 2, 2 * BS, w2), F32),
            pltpu.VMEM((NC, 2, 2 * BS, w2), BF),
            pltpu.VMEM((NC, 2, 2 * BS, w2), BF),
            pltpu.VMEM((NC, NP, 2, 16, w2), BF),
            pltpu.VMEM((NC, NP - 1, 2, 16, w2), BF),
            dma((6 + NM,)),
            dma((2, 2)),
            dma((2, NC)),
            dma((2, NC, 2, 2)),
            dma((2, NC, 2)),
            dma((2, NC, 2, 2)),
            dma((2, NC, 2)),
            dma((2, NC)),
            dma((2, NC)),
        ],
        compiler_params=pltpu.CompilerParams(
            collective_id=0, has_side_effects=True, vmem_limit_bytes=60 * 1024 * 1024
        ),
        name="sparse_attention",
    )(queries, point_order, keys, values, pair_counts, pair_keys, out_grad)
    return pl.pallas_call(
        write_out,
        out_shape=out_shape,
        in_specs=[vmem] * 4,
        out_specs=(hbm,) * 4,
        scratch_shapes=[dma((4,))],
        name="write_out",
    )(*results)


def solution(mesh):
    return jax.shard_map(
        local,
        mesh=mesh,
        in_specs=(
            P("pb", None),
            P("pb", None),
            P("ka", None, None),
            P("ka", None, None),
            P("pb", None),
            P("pb", None),
            P("pb", None, None),
        ),
        out_specs=(
            P(("pb", "ka"), None, None),
            P(("pb", "ka"), None, None),
            P("ka", "pb", None),
            P("ka", "pb", None),
        ),
        check_vma=False,
    )
```

```python
import functools
import math

import jax
import jax.numpy as jnp
from jax import lax
from jax.experimental import pallas as pl
from jax.experimental.pallas import tpu as pltpu
from jax.sharding import PartitionSpec as P

H = 8
HD = 64
D = 512
BS = 128
NP = 16
NX = 4
NY = 2
NM = NX * NY
NC = 4
QS = NM * BS
KS = 4 * BS
PQ = 2 * BS
SCALE = HD ** -0.5
C2 = SCALE * math.log2(math.e)
FAR = 1e30
MESH = pl.DeviceIdType.MESH
BF = jnp.bfloat16
F32 = jnp.float32

NN = (((1,), (0,)), ((), ()))
NT = (((1,), (1,)), ((), ()))
TN = (((0,), (0,)), ((), ()))


def dot(a, b, dims=NN):
    return lax.dot_general(a, b, dims, preferred_element_type=F32)


def kernel(
    queries,
    order,
    keys,
    values,
    counts,
    listing,
    out_grad,
    att_out,
    qg_out,
    kg_out,
    vg_out,
    qbuf,
    order_v,
    counts_v,
    listing_v,
    serial,
    og,
    kv,
    use,
    q_m,
    og_m,
    k_m,
    v_m,
    probs,
    dps,
    qs,
    dss,
    m_keep,
    w_all,
    d_keep,
    stat_own,
    stat_got,
    aq,
    x1_got,
    near_got,
    x2_got,
    y_keep,
    y_send,
    y_got,
    c_keep,
    c_send,
    c_got,
    z_send,
    z_got,
    load_sem,
    kv_sem,
    stat_sem,
    x1_sem,
    near_sem,
    x2_sem,
    y_sem,
    c_sem,
    z_sem,
):
    pb = lax.axis_index("pb")
    ka = lax.axis_index("ka")
    core = lax.rem(ka, 2)
    chip = ka // 2
    xi = lax.rem(chip, NX)
    yi = chip // NX
    xr = lax.rem(xi + 1, NX)
    xl = lax.rem(xi + NX - 1, NX)
    xo = lax.rem(xi + 2, NX)
    yo = 1 - yi

    def at_ka(y, x, c):
        return {"ka": (y * NX + x) * 2 + c}

    right, left = at_ka(yi, xr, core), at_ka(yi, xl, core)
    across = at_ka(yo, xi, core)
    mate = {"ka": chip * 2 + (1 - core)}

    def peer(d):
        return {"ka": lax.rem(chip + d, NM) * 2 + core}

    def slab(d):
        return {"pb": lax.rem(pb + d, NP)}

    def send(src, dst, send_sem, recv_sem, device):
        return pltpu.make_async_remote_copy(
            src_ref=src, dst_ref=dst, send_sem=send_sem, recv_sem=recv_sem,
            device_id=device, device_id_type=MESH,
        )

    own2 = pl.ds(2 * core, 2)
    load_q = pltpu.make_async_copy(queries, qbuf, load_sem.at[0])
    load_small = [
        pltpu.make_async_copy(order, order_v, load_sem.at[3]),
        pltpu.make_async_copy(counts, counts_v, load_sem.at[4]),
        pltpu.make_async_copy(listing, listing_v, load_sem.at[5]),
    ]
    load_kv = [
        pltpu.make_async_copy(keys, kv.at[0, own2], load_sem.at[1]),
        pltpu.make_async_copy(values, kv.at[1, own2], load_sem.at[2]),
    ]
    load_og = [
        pltpu.make_async_copy(out_grad.at[2 * b + core], og.at[b], load_sem.at[6 + b])
        for b in range(NM)
    ]
    for cp in load_small + [load_q] + load_kv + load_og:
        cp.start()

    barrier = pltpu.get_barrier_semaphore()
    pl.semaphore_signal(barrier, inc=1, device_id=mate, device_id_type=MESH)

    def hello_ka(d, _):
        pl.semaphore_signal(barrier, inc=1, device_id=peer(d), device_id_type=MESH)
        return 0

    def hello_pb(d, _):
        pl.semaphore_signal(barrier, inc=1, device_id=slab(d), device_id_type=MESH)
        return 0

    lax.fori_loop(1, NM, hello_ka, 0)
    lax.fori_loop(1, NP, hello_pb, 0)

    for cp in load_small:
        cp.wait()

    cb = jnp.broadcast_to(counts_v[...].astype(F32), (16, 16))
    i0 = lax.broadcasted_iota(jnp.int32, (16, 16), 0)
    i1 = lax.broadcasted_iota(jnp.int32, (16, 16), 1)
    starts = jnp.sum(jnp.where(i1 < i0, cb, 0.0), axis=1, keepdims=True)
    sizes = jnp.sum(jnp.where(i1 == i0, cb, 0.0), axis=1, keepdims=True)
    slot = lax.broadcasted_iota(jnp.int32, (16, 256), 1).astype(F32)
    inside = jnp.where((slot >= starts) & (slot < starts + sizes), 1.0, 0.0)
    row = lax.broadcasted_iota(jnp.int32, (8, 256), 0) + 4 * chip
    named = jnp.where(jnp.broadcast_to(listing_v[...], (8, 256)) == row, 1.0, 0.0)
    joined = dot(named.astype(BF), inside.astype(BF), NT)
    e0 = lax.broadcasted_iota(jnp.int32, (16, QS), 0)
    e1 = lax.broadcasted_iota(jnp.int32, (16, QS), 1)
    spread = jnp.where(e0 == 2 * (e1 // BS) + core, 1.0, 0.0)
    use[...] = dot(joined.astype(BF), spread.astype(BF))

    load_q.wait()

    send_k = send(keys, kv.at[0, own2], kv_sem.at[0, 0], kv_sem.at[1, 0], mate)
    send_v = send(values, kv.at[1, own2], kv_sem.at[0, 1], kv_sem.at[1, 1], mate)

    def gather(t, _):
        @pl.when(t == 1)
        def _():
            pl.semaphore_wait(barrier, 1 + (NM - 1) + (NP - 1))
            send_k.start()
            send_v.start()

        picks = []
        for e in range(4):
            at = pl.multiple_of((8 * t + 2 * e + core) * BS, BS)
            column = jnp.broadcast_to(order_v[:, pl.ds(at, BS)], (BS, BS)).T
            lanes = lax.broadcasted_iota(jnp.int32, (BS, BS), 1)
            picks.append(jnp.concatenate(
                [jnp.where(column == lanes + n * BS, 1.0, 0.0).astype(BF) for n in range(16)], axis=1
            ))
        pick = jnp.concatenate(picks, axis=0)
        serial[pl.ds(pl.multiple_of(t * 4 * BS, 4 * BS), 4 * BS), :] = dot(pick, qbuf[...]).astype(BF)
        return 0

    lax.fori_loop(0, 2, gather, 0)
    for cp in load_kv + load_og:
        cp.wait()
    send_k.wait()
    send_v.wait()

    def lanes_of(hp):
        return pl.ds(pl.multiple_of(hp * 2 * HD, 2 * HD), 2 * HD)

    def split_heads(src, dst, n):
        low = lax.broadcasted_iota(jnp.int32, (n, 2 * HD), 1) < HD
        none = jnp.zeros((n, 2 * HD), BF)
        dst[:n] = jnp.where(low, src, none)
        dst[n:] = jnp.where(low, none, src)

    def columns(u):
        p, h = u // 2, u % 2
        return slice(h * QS + p * PQ, h * QS + (p + 1) * PQ)

    def first(hp):
        par = lax.rem(hp, 2)
        cols = lanes_of(hp)
        k2 = kv[0, :, :, cols].reshape(KS, 2 * HD)
        v2 = kv[1, :, :, cols].reshape(KS, 2 * HD)
        split_heads(serial[:, cols], q_m.at[par], QS)
        split_heads(og[:, :, cols].reshape(QS, 2 * HD), og_m.at[par], QS)

        def products(u):
            cc = columns(u)
            return dot(k2, q_m[par, cc, :], NT), dot(v2, og_m[par, cc, :], NT)

        def softmax(u, st, dp):
            p, h = u // 2, u % 2
            cc = columns(u)
            usable = use[0:4, p * PQ:(p + 1) * PQ] > 0.5
            m_raw = jnp.full((1, PQ), -FAR, F32)
            for kb in range(4):
                top = jnp.max(st[kb * BS:(kb + 1) * BS], axis=0, keepdims=True)
                m_raw = jnp.maximum(m_raw, jnp.where(usable[kb:kb + 1], top, -FAR))
            m = m_raw * C2
            total = jnp.zeros((BS, PQ), F32)
            weighted = jnp.zeros((BS, PQ), F32)
            for kb in range(4):
                ks = slice(kb * BS, (kb + 1) * BS)
                off = jnp.where(usable[kb:kb + 1], m, FAR)
                pr = jnp.exp2(st[ks] * C2 - off)
                total = total + pr
                weighted = weighted + pr * dp[ks]
                probs[par, ks, cc] = pr.astype(BF)
            dps[par, :, cc] = dp.astype(BF)
            total = jnp.maximum(jnp.sum(total, axis=0, keepdims=True), 0.5)
            weighted = jnp.sum(weighted, axis=0, keepdims=True)
            r = slice(u, u + 1)
            m_keep[par, r, :] = m
            stat_own[hp, 0, r, :] = m + jnp.log2(total)
            stat_own[hp, 1, r, :] = weighted / total

        ahead = products(0)
        for u in range(NM):
            now = ahead
            if u + 1 < NM:
                ahead = products(u + 1)
            softmax(u, *now)

        def share(d, _):
            send(stat_own.at[hp], stat_got.at[hp, d - 1], stat_sem.at[0, hp], stat_sem.at[1, hp], peer(d)).start()
            return 0

        lax.fori_loop(1, NM, share, 0)

    def stat_all(hp):
        return send(stat_got.at[hp], stat_got.at[hp], stat_sem.at[0, hp], stat_sem.at[1, hp], right)

    def second(hp):
        par = lax.rem(hp, 2)
        cols = lanes_of(hp)
        split_heads(kv[0, :, :, cols].reshape(KS, 2 * HD), k_m, KS)
        split_heads(kv[1, :, :, cols].reshape(KS, 2 * HD), v_m, KS)
        stat_all(hp).wait_recv()
        lse = [stat_own[hp, 0]] + [stat_got[hp, d, 0] for d in range(NM - 1)]
        dlt = [stat_own[hp, 1]] + [stat_got[hp, d, 1] for d in range(NM - 1)]
        top = functools.reduce(jnp.maximum, lse)
        ws = [jnp.exp2(v - top) for v in lse]
        total = functools.reduce(jnp.add, ws)
        delta_all = functools.reduce(jnp.add, [w * v for w, v in zip(ws, dlt)]) / total
        w_all[...] = jnp.exp2(m_keep[par] - (top + jnp.log2(total)))
        d_keep[...] = delta_all

        for p in range(NM // 2):
            att = jnp.zeros((PQ, 2 * HD), F32)
            dq = jnp.zeros((PQ, 2 * HD), F32)
            for h in range(2):
                u = 2 * p + h
                cc = columns(u)
                hk = slice(h * KS, (h + 1) * KS)
                qf = probs[par, :, cc].astype(F32) * w_all[u:u + 1, :]
                qb = qf.astype(BF)
                ds = (qf * (dps[par, :, cc].astype(F32) - d_keep[u:u + 1, :])).astype(BF)
                qs[:, cc] = qb
                dss[:, cc] = ds
                att = att + dot(qb, v_m[hk, :], TN)
                dq = dq + dot(ds, k_m[hk, :], TN)
            att = att.astype(BF)
            dq = (dq * SCALE).astype(BF)
            for e in range(2):
                b = 2 * p + e
                x, y = b % NX, b // NX
                aq[hp, x, y, 0] = att[e * BS:(e + 1) * BS]
                aq[hp, x, y, 1] = dq[e * BS:(e + 1) * BS]
        for cp in x1_copies(hp, 0) + x1_copies(hp, 1) + near_copies(hp):
            cp.start()
        dk = (dot(dss[...], q_m[par]) * SCALE).reshape(2, 2 * BS, 2 * HD)
        dv = dot(qs[...], og_m[par]).reshape(2, 2 * BS, 2 * HD)
        mine = core == 0
        c_keep[hp, 0] = jnp.where(mine, dk[0], dk[1])
        c_keep[hp, 1] = jnp.where(mine, dv[0], dv[1])
        c_send[hp, 0] = jnp.where(mine, dk[1], dk[0]).astype(BF)
        c_send[hp, 1] = jnp.where(mine, dv[1], dv[0]).astype(BF)
        c_copy(hp).start()

    def x1_copies(hp, kind):
        return tuple(
            send(
                aq.at[hp, xo, way, kind], x1_got.at[hp, way, kind],
                x1_sem.at[0, hp, way, kind], x1_sem.at[1, hp, way, kind], (right, left)[way],
            ) for way in range(2)
        )

    def near_copies(hp):
        return tuple(
            send(
                aq.at[hp, (xr, xl)[way], 1 - way], near_got.at[hp, way],
                near_sem.at[0, hp, way], near_sem.at[1, hp, way], (right, left)[way],
            ) for way in range(2)
        )

    def x2_copies(hp, kind):
        return tuple(
            send(
                aq.at[hp, (xr, xl)[way], way, kind], x2_got.at[hp, way, kind],
                x2_sem.at[0, hp, way, kind], x2_sem.at[1, hp, way, kind], (right, left)[way],
            ) for way in range(2)
        )

    def y_copy(hp, kind):
        return send(y_send.at[hp, kind], y_got.at[hp, kind], y_sem.at[0, hp, kind], y_sem.at[1, hp, kind], across)

    def c_copy(hp):
        return send(c_send.at[hp], c_got.at[hp], c_sem.at[0, hp], c_sem.at[1, hp], mate)

    def z_all(hp):
        return send(z_got.at[hp], z_got.at[hp], z_sem.at[0, hp], z_sem.at[1, hp], slab(1))

    def relay_x(hp):
        for kind in range(2):
            for cp in x1_copies(hp, kind):
                cp.wait_recv()
            for way, x in ((0, xr), (1, xl)):
                aq[hp, x, way, kind] = (
                    aq[hp, x, way, kind].astype(F32) + x1_got[hp, way, kind].astype(F32)
                ).astype(BF)
            for cp in x2_copies(hp, kind):
                cp.start()

    def relay_c(hp):
        c_copy(hp).wait_recv()
        for a in range(2):
            total = c_keep[hp, a] + c_got[hp, a].astype(F32)
            total = total.reshape(2, NP, 8, 2 * HD).transpose(1, 0, 2, 3)
            z_send[hp, :, a] = total.reshape(NP, 16, 2 * HD).astype(BF)

        def share(d, _):
            send(
                z_send.at[hp, lax.rem(pb + d, NP)], z_got.at[hp, d - 1],
                z_sem.at[0, hp], z_sem.at[1, hp], slab(d),
            ).start()
            return 0

        lax.fori_loop(1, NP, share, 0)

    def relay_y(hp):
        for cp in near_copies(hp):
            cp.wait_recv()
        low = yi == 0
        for kind in range(2):
            for cp in x2_copies(hp, kind):
                cp.wait_recv()
            t0, t1 = (
                aq[hp, xi, y, kind].astype(F32)
                + x2_got[hp, y, kind].astype(F32)
                + near_got[hp, 1 - y, kind].astype(F32)
                for y in range(NY)
            )
            y_send[hp, kind] = jnp.where(low, t1, t0).astype(BF)
            y_copy(hp, kind).start()
            y_keep[hp, kind] = jnp.where(low, t0, t1)

    def finish(hp):
        cols = lanes_of(hp)
        z_all(hp).wait_recv()
        for a, out in ((0, kg_out), (1, vg_out)):
            total = z_send[hp, pb, a].astype(F32)
            for d in range(NP - 1):
                total = total + z_got[hp, d, a].astype(F32)
            out[:, :, cols] = total.reshape(2, 8, 2 * HD)
        for kind, out in ((0, att_out), (1, qg_out)):
            y_copy(hp, kind).wait_recv()
            out[0, :, cols] = (y_keep[hp, kind] + y_got[hp, kind].astype(F32)).astype(out.dtype)
        stat_all(hp).wait_send()
        for kind in range(2):
            for cp in x1_copies(hp, kind) + x2_copies(hp, kind):
                cp.wait_send()
            y_copy(hp, kind).wait_send()
        for cp in near_copies(hp):
            cp.wait_send()
        c_copy(hp).wait_send()
        z_all(hp).wait_send()

    def turn(s, _):
        @pl.when(s < NC)
        def _():
            first(s)

        @pl.when((s >= 1) & (s < NC + 1))
        def _():
            second(s - 1)

        @pl.when((s >= 2) & (s < NC + 2))
        def _():
            relay_c(s - 2)

        @pl.when((s >= 2) & (s < NC + 2))
        def _():
            relay_x(s - 2)

        @pl.when((s >= 3) & (s < NC + 3))
        def _():
            relay_y(s - 3)

        @pl.when(s >= 4)
        def _():
            finish(s - 4)

        return 0

    lax.fori_loop(0, NC + 4, turn, 0)


def write_out(*refs):
    sems = refs[8]
    copies = [pltpu.make_async_copy(refs[i], refs[4 + i], sems.at[i]) for i in range(4)]
    for cp in copies:
        cp.start()
    for cp in copies:
        cp.wait()


def local(queries, point_order, keys, values, pair_counts, pair_keys, out_grad):
    hbm = pl.BlockSpec(memory_space=pl.ANY)
    vmem = pl.BlockSpec(memory_space=pltpu.VMEM)
    dma = pltpu.SemaphoreType.DMA
    w2 = 2 * HD
    out_shape = (
        jax.ShapeDtypeStruct((1, BS, D), BF),
        jax.ShapeDtypeStruct((1, BS, D), F32),
        jax.ShapeDtypeStruct((2, 8, D), F32),
        jax.ShapeDtypeStruct((2, 8, D), F32),
    )
    results = pl.pallas_call(
        kernel,
        out_shape=out_shape,
        in_specs=[hbm] * 7,
        out_specs=(vmem, vmem, vmem, vmem),
        scratch_shapes=[
            pltpu.VMEM((NP * BS, D), BF),
            pltpu.VMEM((1, NP * BS), jnp.int32),
            pltpu.VMEM((1, NP), jnp.int32),
            pltpu.VMEM((1, 256), jnp.int32),
            pltpu.VMEM((QS, D), BF),
            pltpu.VMEM((NM, BS, D), BF),
            pltpu.VMEM((2, 4, BS, D), BF),
            pltpu.VMEM((8, QS), F32),
            pltpu.VMEM((2, 2 * QS, w2), BF),
            pltpu.VMEM((2, 2 * QS, w2), BF),
            pltpu.VMEM((2 * KS, w2), BF),
            pltpu.VMEM((2 * KS, w2), BF),
            pltpu.VMEM((2, KS, 2 * QS), BF),
            pltpu.VMEM((2, KS, 2 * QS), BF),
            pltpu.VMEM((KS, 2 * QS), BF),
            pltpu.VMEM((KS, 2 * QS), BF),
            pltpu.VMEM((2, 8, PQ), F32),
            pltpu.VMEM((8, PQ), F32),
            pltpu.VMEM((8, PQ), F32),
            pltpu.VMEM((NC, 2, 8, PQ), F32),
            pltpu.VMEM((NC, NM - 1, 2, 8, PQ), F32),
            pltpu.VMEM((NC, NX, NY, 2, BS, w2), BF),
            pltpu.VMEM((NC, 2, 2, BS, w2), BF),
            pltpu.VMEM((NC, 2, 2, BS, w2), BF),
            pltpu.VMEM((NC, 2, 2, BS, w2), BF),
            pltpu.VMEM((NC, 2, BS, w2), F32),
            pltpu.VMEM((NC, 2, BS, w2), BF),
            pltpu.VMEM((NC, 2, BS, w2), BF),
            pltpu.VMEM((NC, 2, 2 * BS, w2), F32),
            pltpu.VMEM((NC, 2, 2 * BS, w2), BF),
            pltpu.VMEM((NC, 2, 2 * BS, w2), BF),
            pltpu.VMEM((NC, NP, 2, 16, w2), BF),
            pltpu.VMEM((NC, NP - 1, 2, 16, w2), BF),
            dma((6 + NM,)),
            dma((2, 2)),
            dma((2, NC)),
            dma((2, NC, 2, 2)),
            dma((2, NC, 2)),
            dma((2, NC, 2, 2)),
            dma((2, NC, 2)),
            dma((2, NC)),
            dma((2, NC)),
        ],
        compiler_params=pltpu.CompilerParams(
            collective_id=0, has_side_effects=True, vmem_limit_bytes=60 * 1024 * 1024
        ),
        name="sparse_attention",
    )(queries, point_order, keys, values, pair_counts, pair_keys, out_grad)
    return pl.pallas_call(
        write_out,
        out_shape=out_shape,
        in_specs=[vmem] * 4,
        out_specs=(hbm,) * 4,
        scratch_shapes=[dma((4,))],
        name="write_out",
    )(*results)


def solution(mesh):
    return jax.shard_map(
        local,
        mesh=mesh,
        in_specs=(
            P("pb", None),
            P("pb", None),
            P("ka", None, None),
            P("ka", None, None),
            P("pb", None),
            P("pb", None),
            P("pb", None, None),
        ),
        out_specs=(
            P(("pb", "ka"), None, None),
            P(("pb", "ka"), None, None),
            P("ka", "pb", None),
            P("ka", "pb", None),
        ),
        check_vma=False,
    )
```

```python
import functools
import math

import jax
import jax.numpy as jnp
from jax import lax
from jax.experimental import pallas as pl
from jax.experimental.pallas import tpu as pltpu
from jax.sharding import PartitionSpec as P

H = 8
HD = 64
D = 512
BS = 128
NP = 16
NX = 4
NY = 2
NM = NX * NY
NC = 4
QS = NM * BS
KS = 4 * BS
PQ = 2 * BS
SCALE = HD ** -0.5
C2 = SCALE * math.log2(math.e)
FAR = 1e30
MESH = pl.DeviceIdType.MESH
BF = jnp.bfloat16
F32 = jnp.float32

NN = (((1,), (0,)), ((), ()))
NT = (((1,), (1,)), ((), ()))
TN = (((0,), (0,)), ((), ()))


def dot(a, b, dims=NN):
    return lax.dot_general(a, b, dims, preferred_element_type=F32)


def kernel(
    queries,
    order,
    keys,
    values,
    counts,
    listing,
    out_grad,
    att_out,
    qg_out,
    kg_out,
    vg_out,
    qbuf,
    order_v,
    counts_v,
    listing_v,
    serial,
    og,
    kv,
    use,
    q_m,
    og_m,
    k_m,
    v_m,
    probs,
    dps,
    qs,
    dss,
    m_keep,
    w_all,
    d_keep,
    stat_own,
    stat_got,
    aq,
    x1_got,
    near_got,
    x2_got,
    y_keep,
    y_send,
    y_got,
    c_keep,
    c_send,
    c_got,
    z_send,
    z_got,
    load_sem,
    kv_sem,
    stat_sem,
    x1_sem,
    near_sem,
    x2_sem,
    y_sem,
    c_sem,
    z_sem,
):
    pb = lax.axis_index("pb")
    ka = lax.axis_index("ka")
    core = lax.rem(ka, 2)
    chip = ka // 2
    xi = lax.rem(chip, NX)
    yi = chip // NX
    xr = lax.rem(xi + 1, NX)
    xl = lax.rem(xi + NX - 1, NX)
    xo = lax.rem(xi + 2, NX)
    yo = 1 - yi

    def at_ka(y, x, c):
        return {"ka": (y * NX + x) * 2 + c}

    right, left = at_ka(yi, xr, core), at_ka(yi, xl, core)
    across = at_ka(yo, xi, core)
    mate = {"ka": chip * 2 + (1 - core)}

    def peer(d):
        return {"ka": lax.rem(chip + d, NM) * 2 + core}

    def slab(d):
        return {"pb": lax.rem(pb + d, NP)}

    def send(src, dst, send_sem, recv_sem, device):
        return pltpu.make_async_remote_copy(
            src_ref=src, dst_ref=dst, send_sem=send_sem, recv_sem=recv_sem,
            device_id=device, device_id_type=MESH,
        )

    own2 = pl.ds(2 * core, 2)
    load_q = pltpu.make_async_copy(queries, qbuf, load_sem.at[0])
    load_small = [
        pltpu.make_async_copy(order, order_v, load_sem.at[3]),
        pltpu.make_async_copy(counts, counts_v, load_sem.at[4]),
        pltpu.make_async_copy(listing, listing_v, load_sem.at[5]),
    ]
    load_kv = [
        pltpu.make_async_copy(keys, kv.at[0, own2], load_sem.at[1]),
        pltpu.make_async_copy(values, kv.at[1, own2], load_sem.at[2]),
    ]
    load_og = [
        pltpu.make_async_copy(out_grad.at[2 * b + core], og.at[b], load_sem.at[6 + b])
        for b in range(NM)
    ]
    for cp in load_small + [load_q] + load_kv + load_og:
        cp.start()

    barrier = pltpu.get_barrier_semaphore()
    pl.semaphore_signal(barrier, inc=1, device_id=mate, device_id_type=MESH)

    def hello_ka(d, _):
        pl.semaphore_signal(barrier, inc=1, device_id=peer(d), device_id_type=MESH)
        return 0

    def hello_pb(d, _):
        pl.semaphore_signal(barrier, inc=1, device_id=slab(d), device_id_type=MESH)
        return 0

    lax.fori_loop(1, NM, hello_ka, 0)
    lax.fori_loop(1, NP, hello_pb, 0)

    for cp in load_small:
        cp.wait()

    cb = jnp.broadcast_to(counts_v[...].astype(F32), (16, 16))
    i0 = lax.broadcasted_iota(jnp.int32, (16, 16), 0)
    i1 = lax.broadcasted_iota(jnp.int32, (16, 16), 1)
    starts = jnp.sum(jnp.where(i1 < i0, cb, 0.0), axis=1, keepdims=True)
    sizes = jnp.sum(jnp.where(i1 == i0, cb, 0.0), axis=1, keepdims=True)
    slot = lax.broadcasted_iota(jnp.int32, (16, 256), 1).astype(F32)
    inside = jnp.where((slot >= starts) & (slot < starts + sizes), 1.0, 0.0)
    row = lax.broadcasted_iota(jnp.int32, (8, 256), 0) + 4 * chip
    named = jnp.where(jnp.broadcast_to(listing_v[...], (8, 256)) == row, 1.0, 0.0)
    joined = dot(named.astype(BF), inside.astype(BF), NT)
    e0 = lax.broadcasted_iota(jnp.int32, (16, QS), 0)
    e1 = lax.broadcasted_iota(jnp.int32, (16, QS), 1)
    spread = jnp.where(e0 == 2 * (e1 // BS) + core, 1.0, 0.0)
    use[...] = dot(joined.astype(BF), spread.astype(BF))

    load_q.wait()

    send_k = send(keys, kv.at[0, own2], kv_sem.at[0, 0], kv_sem.at[1, 0], mate)
    send_v = send(values, kv.at[1, own2], kv_sem.at[0, 1], kv_sem.at[1, 1], mate)

    def gather(t, _):
        @pl.when(t == 1)
        def _():
            pl.semaphore_wait(barrier, 1 + (NM - 1) + (NP - 1))
            send_k.start()
            send_v.start()

        picks = []
        for e in range(4):
            at = pl.multiple_of((8 * t + 2 * e + core) * BS, BS)
            column = jnp.broadcast_to(order_v[:, pl.ds(at, BS)], (BS, BS)).T
            lanes = lax.broadcasted_iota(jnp.int32, (BS, BS), 1)
            picks.append(jnp.concatenate(
                [jnp.where(column == lanes + n * BS, 1.0, 0.0).astype(BF) for n in range(16)], axis=1
            ))
        pick = jnp.concatenate(picks, axis=0)
        serial[pl.ds(pl.multiple_of(t * 4 * BS, 4 * BS), 4 * BS), :] = dot(pick, qbuf[...]).astype(BF)
        return 0

    lax.fori_loop(0, 2, gather, 0)
    for cp in load_kv + load_og:
        cp.wait()
    send_k.wait()
    send_v.wait()

    def lanes_of(hp):
        return pl.ds(pl.multiple_of(hp * 2 * HD, 2 * HD), 2 * HD)

    def split_heads(src, dst, n):
        low = lax.broadcasted_iota(jnp.int32, (n, 2 * HD), 1) < HD
        none = jnp.zeros((n, 2 * HD), BF)
        dst[:n] = jnp.where(low, src, none)
        dst[n:] = jnp.where(low, none, src)

    def columns(u):
        p, h = u // 2, u % 2
        return slice(h * QS + p * PQ, h * QS + (p + 1) * PQ)

    def first(hp):
        par = lax.rem(hp, 3)
        cols = lanes_of(hp)
        k2 = kv[0, :, :, cols].reshape(KS, 2 * HD)
        v2 = kv[1, :, :, cols].reshape(KS, 2 * HD)
        split_heads(serial[:, cols], q_m.at[par], QS)
        split_heads(og[:, :, cols].reshape(QS, 2 * HD), og_m.at[par], QS)

        def products(u):
            cc = columns(u)
            return dot(k2, q_m[par, cc, :], NT), dot(v2, og_m[par, cc, :], NT)

        def softmax(u, st, dp):
            p, h = u // 2, u % 2
            cc = columns(u)
            usable = use[0:4, p * PQ:(p + 1) * PQ] > 0.5
            m_raw = jnp.full((1, PQ), -FAR, F32)
            for kb in range(4):
                top = jnp.max(st[kb * BS:(kb + 1) * BS], axis=0, keepdims=True)
                m_raw = jnp.maximum(m_raw, jnp.where(usable[kb:kb + 1], top, -FAR))
            m = m_raw * C2
            total = jnp.zeros((BS, PQ), F32)
            weighted = jnp.zeros((BS, PQ), F32)
            for kb in range(4):
                ks = slice(kb * BS, (kb + 1) * BS)
                off = jnp.where(usable[kb:kb + 1], m, FAR)
                pr = jnp.exp2(st[ks] * C2 - off)
                total = total + pr
                weighted = weighted + pr * dp[ks]
                probs[par, ks, cc] = pr.astype(BF)
            dps[par, :, cc] = dp.astype(BF)
            total = jnp.maximum(jnp.sum(total, axis=0, keepdims=True), 0.5)
            weighted = jnp.sum(weighted, axis=0, keepdims=True)
            r = slice(u, u + 1)
            m_keep[par, r, :] = m
            stat_own[hp, 0, r, :] = m + jnp.log2(total)
            stat_own[hp, 1, r, :] = weighted / total

        ahead = products(0)
        for u in range(NM):
            now = ahead
            if u + 1 < NM:
                ahead = products(u + 1)
            softmax(u, *now)

        def share(d, _):
            send(stat_own.at[hp], stat_got.at[hp, d - 1], stat_sem.at[0, hp], stat_sem.at[1, hp], peer(d)).start()
            return 0

        lax.fori_loop(1, NM, share, 0)

    def stat_all(hp):
        return send(stat_got.at[hp], stat_got.at[hp], stat_sem.at[0, hp], stat_sem.at[1, hp], right)

    def second(hp):
        par = lax.rem(hp, 3)
        cols = lanes_of(hp)
        split_heads(kv[0, :, :, cols].reshape(KS, 2 * HD), k_m, KS)
        split_heads(kv[1, :, :, cols].reshape(KS, 2 * HD), v_m, KS)
        stat_all(hp).wait_recv()
        lse = [stat_own[hp, 0]] + [stat_got[hp, d, 0] for d in range(NM - 1)]
        dlt = [stat_own[hp, 1]] + [stat_got[hp, d, 1] for d in range(NM - 1)]
        top = functools.reduce(jnp.maximum, lse)
        ws = [jnp.exp2(v - top) for v in lse]
        total = functools.reduce(jnp.add, ws)
        delta_all = functools.reduce(jnp.add, [w * v for w, v in zip(ws, dlt)]) / total
        w_all[...] = jnp.exp2(m_keep[par] - (top + jnp.log2(total)))
        d_keep[...] = delta_all

        for p in range(NM // 2):
            att = jnp.zeros((PQ, 2 * HD), F32)
            dq = jnp.zeros((PQ, 2 * HD), F32)
            for h in range(2):
                u = 2 * p + h
                cc = columns(u)
                hk = slice(h * KS, (h + 1) * KS)
                qf = probs[par, :, cc].astype(F32) * w_all[u:u + 1, :]
                qb = qf.astype(BF)
                ds = (qf * (dps[par, :, cc].astype(F32) - d_keep[u:u + 1, :])).astype(BF)
                qs[:, cc] = qb
                dss[:, cc] = ds
                att = att + dot(qb, v_m[hk, :], TN)
                dq = dq + dot(ds, k_m[hk, :], TN)
            att = att.astype(BF)
            dq = (dq * SCALE).astype(BF)
            for e in range(2):
                b = 2 * p + e
                x, y = b % NX, b // NX
                aq[hp, x, y, 0] = att[e * BS:(e + 1) * BS]
                aq[hp, x, y, 1] = dq[e * BS:(e + 1) * BS]
        for cp in x1_copies(hp, 0) + x1_copies(hp, 1) + near_copies(hp):
            cp.start()
        dk = (dot(dss[...], q_m[par]) * SCALE).reshape(2, 2 * BS, 2 * HD)
        dv = dot(qs[...], og_m[par]).reshape(2, 2 * BS, 2 * HD)
        mine = core == 0
        c_keep[hp, 0] = jnp.where(mine, dk[0], dk[1])
        c_keep[hp, 1] = jnp.where(mine, dv[0], dv[1])
        c_send[hp, 0] = jnp.where(mine, dk[1], dk[0]).astype(BF)
        c_send[hp, 1] = jnp.where(mine, dv[1], dv[0]).astype(BF)
        c_copy(hp).start()

    def x1_copies(hp, kind):
        return tuple(
            send(
                aq.at[hp, xo, way, kind], x1_got.at[hp, way, kind],
                x1_sem.at[0, hp, way, kind], x1_sem.at[1, hp, way, kind], (right, left)[way],
            ) for way in range(2)
        )

    def near_copies(hp):
        return tuple(
            send(
                aq.at[hp, (xr, xl)[way], 1 - way], near_got.at[hp, way],
                near_sem.at[0, hp, way], near_sem.at[1, hp, way], (right, left)[way],
            ) for way in range(2)
        )

    def x2_copies(hp, kind):
        return tuple(
            send(
                aq.at[hp, (xr, xl)[way], way, kind], x2_got.at[hp, way, kind],
                x2_sem.at[0, hp, way, kind], x2_sem.at[1, hp, way, kind], (right, left)[way],
            ) for way in range(2)
        )

    def y_copy(hp, kind):
        return send(y_send.at[hp, kind], y_got.at[hp, kind], y_sem.at[0, hp, kind], y_sem.at[1, hp, kind], across)

    def c_copy(hp):
        return send(c_send.at[hp], c_got.at[hp], c_sem.at[0, hp], c_sem.at[1, hp], mate)

    def z_all(hp):
        return send(z_got.at[hp], z_got.at[hp], z_sem.at[0, hp], z_sem.at[1, hp], slab(1))

    def relay_x(hp):
        for kind in range(2):
            for cp in x1_copies(hp, kind):
                cp.wait_recv()
            for way, x in ((0, xr), (1, xl)):
                aq[hp, x, way, kind] = (
                    aq[hp, x, way, kind].astype(F32) + x1_got[hp, way, kind].astype(F32)
                ).astype(BF)
            for cp in x2_copies(hp, kind):
                cp.start()

    def relay_c(hp):
        c_copy(hp).wait_recv()
        for a in range(2):
            total = c_keep[hp, a] + c_got[hp, a].astype(F32)
            total = total.reshape(2, NP, 8, 2 * HD).transpose(1, 0, 2, 3)
            z_send[hp, :, a] = total.reshape(NP, 16, 2 * HD).astype(BF)

        def share(d, _):
            send(
                z_send.at[hp, lax.rem(pb + d, NP)], z_got.at[hp, d - 1],
                z_sem.at[0, hp], z_sem.at[1, hp], slab(d),
            ).start()
            return 0

        lax.fori_loop(1, NP, share, 0)

    def relay_y(hp):
        for cp in near_copies(hp):
            cp.wait_recv()
        low = yi == 0
        for kind in range(2):
            for cp in x2_copies(hp, kind):
                cp.wait_recv()
            t0, t1 = (
                aq[hp, xi, y, kind].astype(F32)
                + x2_got[hp, y, kind].astype(F32)
                + near_got[hp, 1 - y, kind].astype(F32)
                for y in range(NY)
            )
            y_send[hp, kind] = jnp.where(low, t1, t0).astype(BF)
            y_copy(hp, kind).start()
            y_keep[hp, kind] = jnp.where(low, t0, t1)

    def finish(hp):
        cols = lanes_of(hp)
        z_all(hp).wait_recv()
        for a, out in ((0, kg_out), (1, vg_out)):
            total = z_send[hp, pb, a].astype(F32)
            for d in range(NP - 1):
                total = total + z_got[hp, d, a].astype(F32)
            out[:, :, cols] = total.reshape(2, 8, 2 * HD)
        for kind, out in ((0, att_out), (1, qg_out)):
            y_copy(hp, kind).wait_recv()
            out[0, :, cols] = (y_keep[hp, kind] + y_got[hp, kind].astype(F32)).astype(out.dtype)
        stat_all(hp).wait_send()
        for kind in range(2):
            for cp in x1_copies(hp, kind) + x2_copies(hp, kind):
                cp.wait_send()
            y_copy(hp, kind).wait_send()
        for cp in near_copies(hp):
            cp.wait_send()
        c_copy(hp).wait_send()
        z_all(hp).wait_send()

    def turn(s, _):
        @pl.when(s < NC)
        def _():
            first(s)

        @pl.when((s >= 2) & (s < NC + 2))
        def _():
            second(s - 2)

        @pl.when((s >= 3) & (s < NC + 3))
        def _():
            relay_c(s - 3)
            relay_x(s - 3)

        @pl.when((s >= 4) & (s < NC + 4))
        def _():
            relay_y(s - 4)

        @pl.when(s >= 5)
        def _():
            finish(s - 5)

        return 0

    lax.fori_loop(0, NC + 5, turn, 0)


def write_out(*refs):
    sems = refs[8]
    copies = [pltpu.make_async_copy(refs[i], refs[4 + i], sems.at[i]) for i in range(4)]
    for cp in copies:
        cp.start()
    for cp in copies:
        cp.wait()


def local(queries, point_order, keys, values, pair_counts, pair_keys, out_grad):
    hbm = pl.BlockSpec(memory_space=pl.ANY)
    vmem = pl.BlockSpec(memory_space=pltpu.VMEM)
    dma = pltpu.SemaphoreType.DMA
    w2 = 2 * HD
    out_shape = (
        jax.ShapeDtypeStruct((1, BS, D), BF),
        jax.ShapeDtypeStruct((1, BS, D), F32),
        jax.ShapeDtypeStruct((2, 8, D), F32),
        jax.ShapeDtypeStruct((2, 8, D), F32),
    )
    results = pl.pallas_call(
        kernel,
        out_shape=out_shape,
        in_specs=[hbm] * 7,
        out_specs=(vmem, vmem, vmem, vmem),
        scratch_shapes=[
            pltpu.VMEM((NP * BS, D), BF),
            pltpu.VMEM((1, NP * BS), jnp.int32),
            pltpu.VMEM((1, NP), jnp.int32),
            pltpu.VMEM((1, 256), jnp.int32),
            pltpu.VMEM((QS, D), BF),
            pltpu.VMEM((NM, BS, D), BF),
            pltpu.VMEM((2, 4, BS, D), BF),
            pltpu.VMEM((8, QS), F32),
            pltpu.VMEM((3, 2 * QS, w2), BF),
            pltpu.VMEM((3, 2 * QS, w2), BF),
            pltpu.VMEM((2 * KS, w2), BF),
            pltpu.VMEM((2 * KS, w2), BF),
            pltpu.VMEM((3, KS, 2 * QS), BF),
            pltpu.VMEM((3, KS, 2 * QS), BF),
            pltpu.VMEM((KS, 2 * QS), BF),
            pltpu.VMEM((KS, 2 * QS), BF),
            pltpu.VMEM((3, 8, PQ), F32),
            pltpu.VMEM((8, PQ), F32),
            pltpu.VMEM((8, PQ), F32),
            pltpu.VMEM((NC, 2, 8, PQ), F32),
            pltpu.VMEM((NC, NM - 1, 2, 8, PQ), F32),
            pltpu.VMEM((NC, NX, NY, 2, BS, w2), BF),
            pltpu.VMEM((NC, 2, 2, BS, w2), BF),
            pltpu.VMEM((NC, 2, 2, BS, w2), BF),
            pltpu.VMEM((NC, 2, 2, BS, w2), BF),
            pltpu.VMEM((NC, 2, BS, w2), F32),
            pltpu.VMEM((NC, 2, BS, w2), BF),
            pltpu.VMEM((NC, 2, BS, w2), BF),
            pltpu.VMEM((NC, 2, 2 * BS, w2), F32),
            pltpu.VMEM((NC, 2, 2 * BS, w2), BF),
            pltpu.VMEM((NC, 2, 2 * BS, w2), BF),
            pltpu.VMEM((NC, NP, 2, 16, w2), BF),
            pltpu.VMEM((NC, NP - 1, 2, 16, w2), BF),
            dma((6 + NM,)),
            dma((2, 2)),
            dma((2, NC)),
            dma((2, NC, 2, 2)),
            dma((2, NC, 2)),
            dma((2, NC, 2, 2)),
            dma((2, NC, 2)),
            dma((2, NC)),
            dma((2, NC)),
        ],
        compiler_params=pltpu.CompilerParams(
            collective_id=0, has_side_effects=True, vmem_limit_bytes=60 * 1024 * 1024
        ),
        name="sparse_attention",
    )(queries, point_order, keys, values, pair_counts, pair_keys, out_grad)
    return pl.pallas_call(
        write_out,
        out_shape=out_shape,
        in_specs=[vmem] * 4,
        out_specs=(hbm,) * 4,
        scratch_shapes=[dma((4,))],
        name="write_out",
    )(*results)


def solution(mesh):
    return jax.shard_map(
        local,
        mesh=mesh,
        in_specs=(
            P("pb", None),
            P("pb", None),
            P("ka", None, None),
            P("ka", None, None),
            P("pb", None),
            P("pb", None),
            P("pb", None, None),
        ),
        out_specs=(
            P(("pb", "ka"), None, None),
            P(("pb", "ka"), None, None),
            P("ka", "pb", None),
            P("ka", "pb", None),
        ),
        check_vma=False,
    )
```

```python
import functools
import math

import jax
import jax.numpy as jnp
from jax import lax
from jax.experimental import pallas as pl
from jax.experimental.pallas import tpu as pltpu
from jax.sharding import PartitionSpec as P

H = 8
HD = 64
D = 512
BS = 128
NP = 16
NX = 4
NY = 2
NM = NX * NY
NC = 4
QS = NM * BS
KS = 4 * BS
PQ = 2 * BS
SCALE = HD ** -0.5
C2 = SCALE * math.log2(math.e)
FAR = 1e30
MESH = pl.DeviceIdType.MESH
BF = jnp.bfloat16
F32 = jnp.float32

NN = (((1,), (0,)), ((), ()))
NT = (((1,), (1,)), ((), ()))
TN = (((0,), (0,)), ((), ()))


def dot(a, b, dims=NN):
    return lax.dot_general(a, b, dims, preferred_element_type=F32)


def kernel(
    queries,
    order,
    keys,
    values,
    counts,
    listing,
    out_grad,
    att_out,
    qg_out,
    kg_out,
    vg_out,
    qbuf,
    order_v,
    counts_v,
    listing_v,
    serial,
    og,
    kv,
    use,
    q_m,
    og_m,
    k_m,
    v_m,
    probs,
    dps,
    qs,
    dss,
    m_keep,
    w_all,
    d_keep,
    stat_own,
    stat_got,
    aq,
    x1_got,
    near_got,
    x2_got,
    y_keep,
    y_send,
    y_got,
    c_keep,
    c_send,
    c_got,
    z_send,
    z_got,
    load_sem,
    kv_sem,
    stat_sem,
    x1_sem,
    near_sem,
    x2_sem,
    y_sem,
    c_sem,
    z_sem,
):
    pb = lax.axis_index("pb")
    ka = lax.axis_index("ka")
    core = lax.rem(ka, 2)
    chip = ka // 2
    xi = lax.rem(chip, NX)
    yi = chip // NX
    xr = lax.rem(xi + 1, NX)
    xl = lax.rem(xi + NX - 1, NX)
    xo = lax.rem(xi + 2, NX)
    yo = 1 - yi

    def at_ka(y, x, c):
        return {"ka": (y * NX + x) * 2 + c}

    right, left = at_ka(yi, xr, core), at_ka(yi, xl, core)
    across = at_ka(yo, xi, core)
    mate = {"ka": chip * 2 + (1 - core)}

    def peer(d):
        return {"ka": lax.rem(chip + d, NM) * 2 + core}

    def slab(d):
        return {"pb": lax.rem(pb + d, NP)}

    def send(src, dst, send_sem, recv_sem, device):
        return pltpu.make_async_remote_copy(
            src_ref=src, dst_ref=dst, send_sem=send_sem, recv_sem=recv_sem,
            device_id=device, device_id_type=MESH,
        )

    own2 = pl.ds(2 * core, 2)
    load_q = pltpu.make_async_copy(queries, qbuf, load_sem.at[0])
    load_small = [
        pltpu.make_async_copy(order, order_v, load_sem.at[3]),
        pltpu.make_async_copy(counts, counts_v, load_sem.at[4]),
        pltpu.make_async_copy(listing, listing_v, load_sem.at[5]),
    ]
    load_kv = [
        pltpu.make_async_copy(keys, kv.at[0, own2], load_sem.at[1]),
        pltpu.make_async_copy(values, kv.at[1, own2], load_sem.at[2]),
    ]
    load_og = [
        pltpu.make_async_copy(out_grad.at[2 * b + core], og.at[b], load_sem.at[6 + b])
        for b in range(NM)
    ]
    for cp in load_small + [load_q] + load_kv + load_og:
        cp.start()

    barrier = pltpu.get_barrier_semaphore()
    pl.semaphore_signal(barrier, inc=1, device_id=mate, device_id_type=MESH)

    def hello_ka(d, _):
        pl.semaphore_signal(barrier, inc=1, device_id=peer(d), device_id_type=MESH)
        return 0

    def hello_pb(d, _):
        pl.semaphore_signal(barrier, inc=1, device_id=slab(d), device_id_type=MESH)
        return 0

    lax.fori_loop(1, NM, hello_ka, 0)
    lax.fori_loop(1, NP, hello_pb, 0)

    for cp in load_small:
        cp.wait()

    cb = jnp.broadcast_to(counts_v[...].astype(F32), (16, 16))
    i0 = lax.broadcasted_iota(jnp.int32, (16, 16), 0)
    i1 = lax.broadcasted_iota(jnp.int32, (16, 16), 1)
    starts = jnp.sum(jnp.where(i1 < i0, cb, 0.0), axis=1, keepdims=True)
    sizes = jnp.sum(jnp.where(i1 == i0, cb, 0.0), axis=1, keepdims=True)
    slot = lax.broadcasted_iota(jnp.int32, (16, 256), 1).astype(F32)
    inside = jnp.where((slot >= starts) & (slot < starts + sizes), 1.0, 0.0)
    row = lax.broadcasted_iota(jnp.int32, (8, 256), 0) + 4 * chip
    named = jnp.where(jnp.broadcast_to(listing_v[...], (8, 256)) == row, 1.0, 0.0)
    joined = dot(named.astype(BF), inside.astype(BF), NT)
    e0 = lax.broadcasted_iota(jnp.int32, (16, QS), 0)
    e1 = lax.broadcasted_iota(jnp.int32, (16, QS), 1)
    spread = jnp.where(e0 == 2 * (e1 // BS) + core, 1.0, 0.0)
    use[...] = dot(joined.astype(BF), spread.astype(BF))

    load_q.wait()

    send_k = send(keys, kv.at[0, own2], kv_sem.at[0, 0], kv_sem.at[1, 0], mate)
    send_v = send(values, kv.at[1, own2], kv_sem.at[0, 1], kv_sem.at[1, 1], mate)

    def gather(t, _):
        @pl.when(t == 1)
        def _():
            pl.semaphore_wait(barrier, 1 + (NM - 1) + (NP - 1))
            send_k.start()
            send_v.start()

        picks = []
        for e in range(4):
            at = pl.multiple_of((8 * t + 2 * e + core) * BS, BS)
            column = jnp.broadcast_to(order_v[:, pl.ds(at, BS)], (BS, BS)).T
            lanes = lax.broadcasted_iota(jnp.int32, (BS, BS), 1)
            picks.append(jnp.concatenate(
                [jnp.where(column == lanes + n * BS, 1.0, 0.0).astype(BF) for n in range(16)], axis=1
            ))
        pick = jnp.concatenate(picks, axis=0)
        serial[pl.ds(pl.multiple_of(t * 4 * BS, 4 * BS), 4 * BS), :] = dot(pick, qbuf[...]).astype(BF)
        return 0

    lax.fori_loop(0, 2, gather, 0)
    for cp in load_kv + load_og:
        cp.wait()
    send_k.wait()
    send_v.wait()

    def lanes_of(hp):
        return pl.ds(pl.multiple_of(hp * 2 * HD, 2 * HD), 2 * HD)

    def split_heads(src, dst, n):
        low = lax.broadcasted_iota(jnp.int32, (n, 2 * HD), 1) < HD
        none = jnp.zeros((n, 2 * HD), BF)
        dst[:n] = jnp.where(low, src, none)
        dst[n:] = jnp.where(low, none, src)

    def columns(u):
        p, h = u // 2, u % 2
        return slice(h * QS + p * PQ, h * QS + (p + 1) * PQ)

    def first(hp):
        par = hp
        cols = lanes_of(hp)
        k2 = kv[0, :, :, cols].reshape(KS, 2 * HD)
        v2 = kv[1, :, :, cols].reshape(KS, 2 * HD)
        split_heads(serial[:, cols], q_m.at[par], QS)
        split_heads(og[:, :, cols].reshape(QS, 2 * HD), og_m.at[par], QS)

        def products(u):
            cc = columns(u)
            return dot(k2, q_m[par, cc, :], NT), dot(v2, og_m[par, cc, :], NT)

        def softmax(u, st, dp):
            p, h = u // 2, u % 2
            cc = columns(u)
            usable = use[0:4, p * PQ:(p + 1) * PQ] > 0.5
            m_raw = jnp.full((1, PQ), -FAR, F32)
            for kb in range(4):
                top = jnp.max(st[kb * BS:(kb + 1) * BS], axis=0, keepdims=True)
                m_raw = jnp.maximum(m_raw, jnp.where(usable[kb:kb + 1], top, -FAR))
            m = m_raw * C2
            total = jnp.zeros((BS, PQ), F32)
            weighted = jnp.zeros((BS, PQ), F32)
            for kb in range(4):
                ks = slice(kb * BS, (kb + 1) * BS)
                off = jnp.where(usable[kb:kb + 1], m, FAR)
                pr = jnp.exp2(st[ks] * C2 - off)
                total = total + pr
                weighted = weighted + pr * dp[ks]
                probs[par, ks, cc] = pr.astype(BF)
            dps[par, :, cc] = dp.astype(BF)
            total = jnp.maximum(jnp.sum(total, axis=0, keepdims=True), 0.5)
            weighted = jnp.sum(weighted, axis=0, keepdims=True)
            r = slice(u, u + 1)
            m_keep[par, r, :] = m
            stat_own[hp, 0, r, :] = m + jnp.log2(total)
            stat_own[hp, 1, r, :] = weighted / total

        ahead = products(0)
        for u in range(NM):
            now = ahead
            if u + 1 < NM:
                ahead = products(u + 1)
            softmax(u, *now)

        def share(d, _):
            send(stat_own.at[hp], stat_got.at[hp, d - 1], stat_sem.at[0, hp], stat_sem.at[1, hp], peer(d)).start()
            return 0

        lax.fori_loop(1, NM, share, 0)

    def stat_all(hp):
        return send(stat_got.at[hp], stat_got.at[hp], stat_sem.at[0, hp], stat_sem.at[1, hp], right)

    def second(hp):
        par = hp
        cols = lanes_of(hp)
        split_heads(kv[0, :, :, cols].reshape(KS, 2 * HD), k_m, KS)
        split_heads(kv[1, :, :, cols].reshape(KS, 2 * HD), v_m, KS)
        stat_all(hp).wait_recv()
        lse = [stat_own[hp, 0]] + [stat_got[hp, d, 0] for d in range(NM - 1)]
        dlt = [stat_own[hp, 1]] + [stat_got[hp, d, 1] for d in range(NM - 1)]
        top = functools.reduce(jnp.maximum, lse)
        ws = [jnp.exp2(v - top) for v in lse]
        total = functools.reduce(jnp.add, ws)
        delta_all = functools.reduce(jnp.add, [w * v for w, v in zip(ws, dlt)]) / total
        w_all[...] = jnp.exp2(m_keep[par] - (top + jnp.log2(total)))
        d_keep[...] = delta_all

        for p in range(NM // 2):
            att = jnp.zeros((PQ, 2 * HD), F32)
            dq = jnp.zeros((PQ, 2 * HD), F32)
            for h in range(2):
                u = 2 * p + h
                cc = columns(u)
                hk = slice(h * KS, (h + 1) * KS)
                qf = probs[par, :, cc].astype(F32) * w_all[u:u + 1, :]
                qb = qf.astype(BF)
                ds = (qf * (dps[par, :, cc].astype(F32) - d_keep[u:u + 1, :])).astype(BF)
                qs[:, cc] = qb
                dss[:, cc] = ds
                att = att + dot(qb, v_m[hk, :], TN)
                dq = dq + dot(ds, k_m[hk, :], TN)
            att = att.astype(BF)
            dq = (dq * SCALE).astype(BF)
            for e in range(2):
                b = 2 * p + e
                x, y = b % NX, b // NX
                aq[hp, x, y, 0] = att[e * BS:(e + 1) * BS]
                aq[hp, x, y, 1] = dq[e * BS:(e + 1) * BS]
        for cp in x1_copies(hp, 0) + x1_copies(hp, 1) + near_copies(hp):
            cp.start()
        dk = (dot(dss[...], q_m[par]) * SCALE).reshape(2, 2 * BS, 2 * HD)
        dv = dot(qs[...], og_m[par]).reshape(2, 2 * BS, 2 * HD)
        mine = core == 0
        c_keep[hp, 0] = jnp.where(mine, dk[0], dk[1])
        c_keep[hp, 1] = jnp.where(mine, dv[0], dv[1])
        c_send[hp, 0] = jnp.where(mine, dk[1], dk[0]).astype(BF)
        c_send[hp, 1] = jnp.where(mine, dv[1], dv[0]).astype(BF)
        c_copy(hp).start()

    def x1_copies(hp, kind):
        return tuple(
            send(
                aq.at[hp, xo, way, kind], x1_got.at[hp, way, kind],
                x1_sem.at[0, hp, way, kind], x1_sem.at[1, hp, way, kind], (right, left)[way],
            ) for way in range(2)
        )

    def near_copies(hp):
        return tuple(
            send(
                aq.at[hp, (xr, xl)[way], 1 - way], near_got.at[hp, way],
                near_sem.at[0, hp, way], near_sem.at[1, hp, way], (right, left)[way],
            ) for way in range(2)
        )

    def x2_copies(hp, kind):
        return tuple(
            send(
                aq.at[hp, (xr, xl)[way], way, kind], x2_got.at[hp, way, kind],
                x2_sem.at[0, hp, way, kind], x2_sem.at[1, hp, way, kind], (right, left)[way],
            ) for way in range(2)
        )

    def y_copy(hp, kind):
        return send(y_send.at[hp, kind], y_got.at[hp, kind], y_sem.at[0, hp, kind], y_sem.at[1, hp, kind], across)

    def c_copy(hp):
        return send(c_send.at[hp], c_got.at[hp], c_sem.at[0, hp], c_sem.at[1, hp], mate)

    def z_all(hp):
        return send(z_got.at[hp], z_got.at[hp], z_sem.at[0, hp], z_sem.at[1, hp], slab(1))

    def relay_x(hp):
        for kind in range(2):
            for cp in x1_copies(hp, kind):
                cp.wait_recv()
            for way, x in ((0, xr), (1, xl)):
                aq[hp, x, way, kind] = (
                    aq[hp, x, way, kind].astype(F32) + x1_got[hp, way, kind].astype(F32)
                ).astype(BF)
            for cp in x2_copies(hp, kind):
                cp.start()

    def relay_c(hp):
        c_copy(hp).wait_recv()
        for a in range(2):
            total = c_keep[hp, a] + c_got[hp, a].astype(F32)
            total = total.reshape(2, NP, 8, 2 * HD).transpose(1, 0, 2, 3)
            z_send[hp, :, a] = total.reshape(NP, 16, 2 * HD).astype(BF)

        def share(d, _):
            send(
                z_send.at[hp, lax.rem(pb + d, NP)], z_got.at[hp, d - 1],
                z_sem.at[0, hp], z_sem.at[1, hp], slab(d),
            ).start()
            return 0

        lax.fori_loop(1, NP, share, 0)

    def relay_y(hp):
        for cp in near_copies(hp):
            cp.wait_recv()
        low = yi == 0
        for kind in range(2):
            for cp in x2_copies(hp, kind):
                cp.wait_recv()
            t0, t1 = (
                aq[hp, xi, y, kind].astype(F32)
                + x2_got[hp, y, kind].astype(F32)
                + near_got[hp, 1 - y, kind].astype(F32)
                for y in range(NY)
            )
            y_send[hp, kind] = jnp.where(low, t1, t0).astype(BF)
            y_copy(hp, kind).start()
            y_keep[hp, kind] = jnp.where(low, t0, t1)

    def finish(hp):
        cols = lanes_of(hp)
        z_all(hp).wait_recv()
        for a, out in ((0, kg_out), (1, vg_out)):
            total = z_send[hp, pb, a].astype(F32)
            for d in range(NP - 1):
                total = total + z_got[hp, d, a].astype(F32)
            out[:, :, cols] = total.reshape(2, 8, 2 * HD)
        for kind, out in ((0, att_out), (1, qg_out)):
            y_copy(hp, kind).wait_recv()
            out[0, :, cols] = (y_keep[hp, kind] + y_got[hp, kind].astype(F32)).astype(out.dtype)
        stat_all(hp).wait_send()
        for kind in range(2):
            for cp in x1_copies(hp, kind) + x2_copies(hp, kind):
                cp.wait_send()
            y_copy(hp, kind).wait_send()
        for cp in near_copies(hp):
            cp.wait_send()
        c_copy(hp).wait_send()
        z_all(hp).wait_send()

    def turn(s, _):
        @pl.when(s < NC)
        def _():
            first(s)

        @pl.when((s >= 3) & (s < NC + 3))
        def _():
            second(s - 3)

        @pl.when((s >= 4) & (s < NC + 4))
        def _():
            relay_c(s - 4)
            relay_x(s - 4)

        @pl.when((s >= 5) & (s < NC + 5))
        def _():
            relay_y(s - 5)

        @pl.when(s >= 6)
        def _():
            finish(s - 6)

        return 0

    lax.fori_loop(0, NC + 6, turn, 0)


def write_out(*refs):
    sems = refs[8]
    copies = [pltpu.make_async_copy(refs[i], refs[4 + i], sems.at[i]) for i in range(4)]
    for cp in copies:
        cp.start()
    for cp in copies:
        cp.wait()


def local(queries, point_order, keys, values, pair_counts, pair_keys, out_grad):
    hbm = pl.BlockSpec(memory_space=pl.ANY)
    vmem = pl.BlockSpec(memory_space=pltpu.VMEM)
    dma = pltpu.SemaphoreType.DMA
    w2 = 2 * HD
    out_shape = (
        jax.ShapeDtypeStruct((1, BS, D), BF),
        jax.ShapeDtypeStruct((1, BS, D), F32),
        jax.ShapeDtypeStruct((2, 8, D), F32),
        jax.ShapeDtypeStruct((2, 8, D), F32),
    )
    results = pl.pallas_call(
        kernel,
        out_shape=out_shape,
        in_specs=[hbm] * 7,
        out_specs=(vmem, vmem, vmem, vmem),
        scratch_shapes=[
            pltpu.VMEM((NP * BS, D), BF),
            pltpu.VMEM((1, NP * BS), jnp.int32),
            pltpu.VMEM((1, NP), jnp.int32),
            pltpu.VMEM((1, 256), jnp.int32),
            pltpu.VMEM((QS, D), BF),
            pltpu.VMEM((NM, BS, D), BF),
            pltpu.VMEM((2, 4, BS, D), BF),
            pltpu.VMEM((8, QS), F32),
            pltpu.VMEM((NC, 2 * QS, w2), BF),
            pltpu.VMEM((NC, 2 * QS, w2), BF),
            pltpu.VMEM((2 * KS, w2), BF),
            pltpu.VMEM((2 * KS, w2), BF),
            pltpu.VMEM((NC, KS, 2 * QS), BF),
            pltpu.VMEM((NC, KS, 2 * QS), BF),
            pltpu.VMEM((KS, 2 * QS), BF),
            pltpu.VMEM((KS, 2 * QS), BF),
            pltpu.VMEM((NC, 8, PQ), F32),
            pltpu.VMEM((8, PQ), F32),
            pltpu.VMEM((8, PQ), F32),
            pltpu.VMEM((NC, 2, 8, PQ), F32),
            pltpu.VMEM((NC, NM - 1, 2, 8, PQ), F32),
            pltpu.VMEM((NC, NX, NY, 2, BS, w2), BF),
            pltpu.VMEM((NC, 2, 2, BS, w2), BF),
            pltpu.VMEM((NC, 2, 2, BS, w2), BF),
            pltpu.VMEM((NC, 2, 2, BS, w2), BF),
            pltpu.VMEM((NC, 2, BS, w2), F32),
            pltpu.VMEM((NC, 2, BS, w2), BF),
            pltpu.VMEM((NC, 2, BS, w2), BF),
            pltpu.VMEM((NC, 2, 2 * BS, w2), F32),
            pltpu.VMEM((NC, 2, 2 * BS, w2), BF),
            pltpu.VMEM((NC, 2, 2 * BS, w2), BF),
            pltpu.VMEM((NC, NP, 2, 16, w2), BF),
            pltpu.VMEM((NC, NP - 1, 2, 16, w2), BF),
            dma((6 + NM,)),
            dma((2, 2)),
            dma((2, NC)),
            dma((2, NC, 2, 2)),
            dma((2, NC, 2)),
            dma((2, NC, 2, 2)),
            dma((2, NC, 2)),
            dma((2, NC)),
            dma((2, NC)),
        ],
        compiler_params=pltpu.CompilerParams(
            collective_id=0, has_side_effects=True, vmem_limit_bytes=60 * 1024 * 1024
        ),
        name="sparse_attention",
    )(queries, point_order, keys, values, pair_counts, pair_keys, out_grad)
    return pl.pallas_call(
        write_out,
        out_shape=out_shape,
        in_specs=[vmem] * 4,
        out_specs=(hbm,) * 4,
        scratch_shapes=[dma((4,))],
        name="write_out",
    )(*results)


def solution(mesh):
    return jax.shard_map(
        local,
        mesh=mesh,
        in_specs=(
            P("pb", None),
            P("pb", None),
            P("ka", None, None),
            P("ka", None, None),
            P("pb", None),
            P("pb", None),
            P("pb", None, None),
        ),
        out_specs=(
            P(("pb", "ka"), None, None),
            P(("pb", "ka"), None, None),
            P("ka", "pb", None),
            P("ka", "pb", None),
        ),
        check_vma=False,
    )
```
